32 devices in a mesh: dp: 16 (over z, x, core), tensor: 2 (over y).
Axes of the slice: x: 2, y: 2, z: 4, core: 2. Of those that a mesh axis runs over, the one named last changes fastest.
Arguments:
- inputs: bfloat16 [16384, 768], P(('dp', 'tensor')), may hold values from -6 to 6
- out_grad: bfloat16 [16384, 768], P(('dp', 'tensor')), may hold values from -6 to 6
- span_starts: int32 [32], P('dp'), may hold values from 0 to 1535
- span_lengths: int32 [32], P('dp'), may hold values from 102 to 512
- norm1_gain: bfloat16 [768], replicated, may hold values from 0.5 to 1.5
- norm1_bias: bfloat16 [768], replicated, may hold values from -1.75 to 1.75
- projections: bfloat16 [3, 768, 768], P(None, None, 'tensor'), may hold values from -0.3125 to 0.3125
- query_value_bias: bfloat16 [2, 768], P(None, 'tensor'), may hold values from -1.75 to 1.75
- mix_weight: bfloat16 [768, 768], P('tensor'), may hold values from -1.25 to 1.25
- mix_bias: bfloat16 [768], replicated, may hold values from -1.75 to 1.75
- norm2_gain: bfloat16 [768], replicated, may hold values from 0.5 to 1.5
- norm2_bias: bfloat16 [768], replicated, may hold values from -1.75 to 1.75
- expand_weight: bfloat16 [768, 3072], P(None, 'tensor'), may hold values from -0.21875 to 0.21875
- expand_bias: bfloat16 [3072], P('tensor'), may hold values from -1.75 to 1.75
- contract_weight: bfloat16 [3072, 768], P('tensor'), may hold values from -0.109375 to 0.109375
- contract_bias: bfloat16 [768], replicated, may hold values from -1.75 to 1.75
Outputs:
- layer_out: bfloat16 [16384, 768], P(('dp', 'tensor'))
- input_grad: float32 [16384, 768], P(('dp', 'tensor'))
- grad_norm1_gain: float32 [768], replicated
- grad_norm1_bias: float32 [768], replicated
- grad_projections: float32 [3, 768, 768], P(None, None, 'tensor')
- grad_query_value_bias: float32 [2, 768], P(None, 'tensor')
- grad_mix_weight: float32 [768, 768], P('tensor')
- grad_mix_bias: float32 [768], replicated
- grad_norm2_gain: float32 [768], replicated
- grad_norm2_bias: float32 [768], replicated
- grad_expand_weight: float32 [768, 3072], P(None, 'tensor')
- grad_expand_bias: float32 [3072], P('tensor')
- grad_contract_weight: float32 [3072, 768], P('tensor')
- grad_contract_bias: float32 [768], replicated
The draws below stay inside these ranges and needn't reach their ends.
All inputs are finite; a program needn't handle non-finite values.
Results may differ from the reference program's by a relative error of at most 0.012.
The reference program's roundings to bfloat16 on the way count: a program that leaves them out, or rounds other values in their place, can miss the bound.
Values may be sent and summed in bfloat16 or wider, within the bound.
No kernel may reach another device: no remote copies, remote signals or barrier semaphores. Data moves between devices by JAX's collectives and lax.ppermute only.
A program may use at most 128 MiB of HBM per device.

```python
import jax
import jax.numpy as jnp
from jax import lax

D = 768
HEADS = 12
FF = 3072
LEN = 512
RATE = 4
SEQ_DEV = 2
HEAD = 64
TOK_DEV = 1024
SEQS = 32
TOKENS = 16384
N_DP = 16


def set_ends(drawn, stream_key, low, high):
    longest = drawn.shape.index(max(drawn.shape))
    spots = []
    for shift in (0, 1):
        where = [jax.random.randint(jax.random.fold_in(stream_key, axis), (), 0, length) for axis, length in enumerate(drawn.shape)]
        where[longest] = (where[longest] + shift) % drawn.shape[longest]
        spots.append(tuple(where))
    return drawn.at[spots[0]].set(low).at[spots[1]].set(high)


def block_scale(own_key, extent, shards, smallest, largest):
    def one(position, blocks):
        draws = jax.random.uniform(jax.random.fold_in(jax.random.fold_in(own_key, 6), position), (blocks,), jnp.float32, smallest / len(shards), largest / len(shards))
        return jnp.repeat(jnp.exp(draws), extent[position] // blocks).reshape((-1,) + (1,) * (len(extent) - position - 1))

    factor_of = one(*shards[0])
    for cut in shards[1:]:
        factor_of = factor_of * one(*cut)
    return factor_of


def scatter_about(stream_key, shape, scale, bound, shards=(), kind=jnp.bfloat16):
    entries = scale * jax.random.normal(stream_key, shape, jnp.float32)
    if shards:
        entries = entries * block_scale(stream_key, shape, shards, -0.22, 0.18)
    return jnp.clip(entries, -bound, bound).astype(kind)


def setup_inputs(seed: int = 0) -> dict:
    arg_keys = jax.random.split(jax.random.key(seed), 17)
    inputs = scatter_about(arg_keys[0], (TOKENS, D), 1.0, 6.0, ((0, 32),))
    out_grad = scatter_about(arg_keys[1], (TOKENS, D), 1.0, 6.0, ((0, 32),))
    span_starts = set_ends(jax.random.randint(arg_keys[2], (SEQS,), 0, RATE * LEN * 3 // 4), jax.random.fold_in(arg_keys[2], 1), 0, (RATE * LEN * 3 // 4) - 1).astype(jnp.int32)
    span_lengths = set_ends(jax.random.randint(arg_keys[3], (SEQS,), RATE * LEN // 20, RATE * LEN // 4 + 1), jax.random.fold_in(arg_keys[3], 1), RATE * LEN // 20, (RATE * LEN // 4 + 1) - 1).astype(jnp.int32)
    norm1_gain = jnp.clip(1.0 + 0.1 * jax.random.normal(arg_keys[4], (D,), jnp.float32), 0.5, 1.5).astype(jnp.bfloat16)
    norm1_bias = scatter_about(arg_keys[5], (D,), 0.3, 1.75)
    projections = scatter_about(arg_keys[6], (3, D, D), (D // 2) ** -0.5, 0.3125, ((2, 2),))
    query_value_bias = scatter_about(arg_keys[7], (2, D), 0.3, 1.75, ((1, 2),))
    mix_weight = scatter_about(arg_keys[8], (D, D), (D // 32) ** -0.5, 1.25, ((0, 2),))
    mix_bias = scatter_about(arg_keys[9], (D,), 0.3, 1.75)
    norm2_gain = jnp.clip(1.0 + 0.1 * jax.random.normal(arg_keys[10], (D,), jnp.float32), 0.5, 1.5).astype(jnp.bfloat16)
    norm2_bias = scatter_about(arg_keys[11], (D,), 0.3, 1.75)
    expand_weight = scatter_about(arg_keys[12], (D, FF), D ** -0.5, 0.21875, ((1, 2),))
    expand_bias = scatter_about(arg_keys[13], (FF,), 0.3, 1.75, ((0, 2),))
    contract_weight = scatter_about(arg_keys[14], (FF, D), FF ** -0.5, 0.109375, ((0, 2),))
    contract_bias = scatter_about(arg_keys[15], (D,), 0.3, 1.75)
    return dict(inputs=inputs, out_grad=out_grad, span_starts=span_starts, span_lengths=span_lengths, norm1_gain=norm1_gain, norm1_bias=norm1_bias, projections=projections, query_value_bias=query_value_bias, mix_weight=mix_weight, mix_bias=mix_bias, norm2_gain=norm2_gain, norm2_bias=norm2_bias, expand_weight=expand_weight, expand_bias=expand_bias, contract_weight=contract_weight, contract_bias=contract_bias)


@jax.custom_vjp
def low(v):
    return lax.optimization_barrier(v.astype(jnp.bfloat16)).astype(jnp.float32)

@jax.custom_vjp
def low_back(v):
    return v

def low_keep(v):
    return (low(v), None)

def low_pass(kept, grad):
    return (grad,)

def back_keep(v):
    return (v, None)

def back_low(kept, grad):
    return (low(grad),)
low.defvjp(low_keep, low_pass)
low_back.defvjp(back_keep, back_low)
EPS = 1e-12
HIGH = lax.Precision.HIGHEST

def layer_norm(values, gain, bias):
    mean = lax.optimization_barrier(jnp.mean(values, axis=-1, keepdims=True))
    centred = values - mean
    var = lax.optimization_barrier(jnp.mean(centred * centred, axis=-1, keepdims=True))
    return centred * lax.rsqrt(var + EPS) * gain + bias

def layer_rows(params, rows):
    gain_one, bias_one, projections, qv_bias, mix_weight, mix_bias, gain_two, bias_two, expand_weight, expand_bias, contract_weight, contract_bias = params
    scale = HEAD ** (-0.5)
    h_one = low(layer_norm(rows, gain_one, bias_one))
    query_rows = low(low_back(jnp.dot(h_one, projections[0], precision=HIGH) + qv_bias[0]))
    key_rows = low(low_back(jnp.dot(h_one, projections[1], precision=HIGH)))
    value_rows = low(low_back(jnp.dot(h_one, projections[2], precision=HIGH) + qv_bias[1]))
    shape = (SEQ_DEV, LEN, HEADS, HEAD)
    query_rows = query_rows.reshape(shape)
    key_rows = key_rows.reshape(shape)
    value_rows = value_rows.reshape(shape)
    scores = low_back(jnp.einsum('sqhd,skhd->shqk', query_rows, key_rows, precision=HIGH) * scale)
    probs = low(jax.nn.softmax(scores, axis=-1))
    context = jnp.einsum('shqk,skhd->sqhd', probs, value_rows, precision=HIGH).reshape(TOK_DEV, D)
    context = low(low_back(context))
    branch = low_back(jnp.dot(context, mix_weight, precision=HIGH))
    resid_one = rows + branch + mix_bias
    h_two = low(layer_norm(resid_one, gain_two, bias_two))
    pre = low_back(jnp.dot(h_two, expand_weight, precision=HIGH) + expand_bias)
    act = low(jax.nn.gelu(pre, approximate=False))
    return resid_one + low_back(jnp.dot(act, contract_weight, precision=HIGH)) + contract_bias

def reference(inputs, out_grad, span_starts, span_lengths, norm1_gain, norm1_bias, projections, query_value_bias, mix_weight, mix_bias, norm2_gain, norm2_bias, expand_weight, expand_bias, contract_weight, contract_bias):
    positions = jnp.arange(LEN, dtype=jnp.int32) * RATE
    ends = span_starts + span_lengths
    masked = (positions[None, :] < ends[:, None]) & (positions[None, :] + RATE > span_starts[:, None])
    cotangent = out_grad.astype(jnp.float32) * masked.astype(jnp.float32).reshape(TOKENS, 1)
    params = tuple((p.astype(jnp.float32) for p in (norm1_gain, norm1_bias, projections, query_value_bias, mix_weight, mix_bias, norm2_gain, norm2_bias, expand_weight, expand_bias, contract_weight, contract_bias)))
    inputs_f = inputs.astype(jnp.float32)

    def whole(params_in, rows_in):
        blocks = rows_in.reshape(N_DP, TOK_DEV, D)
        block_fn = jax.checkpoint(lambda rows: layer_rows(params_in, rows))
        return lax.map(block_fn, blocks).reshape(TOKENS, D)
    output, pull = jax.vjp(whole, params, inputs_f)
    grads, input_grad = pull(cotangent)
    return (output.astype(jnp.bfloat16), input_grad, grads[0], grads[1], grads[2], grads[3], grads[4], grads[5], grads[6], grads[7], grads[8], grads[9], grads[10], grads[11])
```

```python
from functools import partial

import jax
import jax.numpy as jnp
from jax import lax
from jax.experimental import pallas as pl
from jax.experimental.pallas import tpu as pltpu
from jax.sharding import PartitionSpec as P

RATE = 4
HEAD = 64
PAIR = 2 * HEAD
EPS = 1e-12
WIN = 144
ALIGN = 16
PARTS = 16
F32 = jnp.float32
BF16 = jnp.bfloat16
MIB = 1 << 20
ROOT_HALF = 0.7071067811865476
GAUSS = 0.3989422804014327

GAIN1, BIAS1, MIXB, GAIN2, BIAS2, OUTB, QB, VB, EXPB = 0, 1, 2, 3, 4, 5, 6, 7, 8


def mm(a, b):
    return lax.dot_general(a, b, (((1,), (0,)), ((), ())), preferred_element_type=F32)


def mm_right(a, b):
    return lax.dot_general(a, b, (((1,), (1,)), ((), ())), preferred_element_type=F32)


def mm_left(a, b):
    return lax.dot_general(a, b, (((0,), (0,)), ((), ())), preferred_element_type=F32)


def norm(values):
    mean = jnp.mean(values, axis=-1, keepdims=True)
    centred = values - mean
    var = jnp.mean(centred * centred, axis=-1, keepdims=True)
    inverse = lax.rsqrt(var + EPS)
    return centred * inverse, inverse


def norm_back(scaled, normed, inverse):
    inner = jnp.mean(scaled, axis=-1, keepdims=True)
    cross = jnp.mean(scaled * normed, axis=-1, keepdims=True)
    return inverse * (scaled - inner - normed * cross)


def call(kernel, outs, name, flops, args, scratch=(), smem=0, limit=32):
    moved = sum(a.size * a.dtype.itemsize for a in args)
    moved += sum(o.size * o.dtype.itemsize for o in outs)
    specs = [pl.BlockSpec(memory_space=pltpu.SMEM)] * smem
    specs += [pl.BlockSpec(memory_space=pltpu.VMEM)] * (len(args) - smem)
    return pl.pallas_call(
        kernel,
        out_shape=tuple(outs),
        in_specs=specs,
        out_specs=tuple(pl.BlockSpec(memory_space=pltpu.VMEM) for _ in outs),
        scratch_shapes=list(scratch),
        compiler_params=pltpu.CompilerParams(vmem_limit_bytes=limit * MIB),
        cost_estimate=pl.CostEstimate(flops=flops, bytes_accessed=moved, transcendentals=0),
        name=name,
    )(*args)


def struct(shape, kind):
    return jax.ShapeDtypeStruct(shape, kind)


def project_kernel(x_ref, p_ref, w_ref, h_ref, q_ref, k_ref, v_ref):
    rows = x_ref.shape[0]
    width = q_ref.shape[1]
    gain, bias = p_ref[GAIN1 : GAIN1 + 1], p_ref[BIAS1 : BIAS1 + 1]
    q_bias, v_bias = p_ref[QB : QB + 1, :width], p_ref[VB : VB + 1, :width]
    for at in range(0, rows, 256):
        part = slice(at, at + 256)
        normed, _ = norm(x_ref[part].astype(F32))
        low = (normed * gain + bias).astype(BF16)
        h_ref[part] = low
        q_ref[part] = (mm(low, w_ref[0]) + q_bias).astype(BF16) * BF16(HEAD**-0.5)
        k_ref[part] = mm(low, w_ref[1]).astype(BF16)
        v_ref[part] = (mm(low, w_ref[2]) + v_bias).astype(BF16)


def split_heads(values):
    low = lax.broadcasted_iota(jnp.int32, values.shape, 1) < HEAD
    zero = jnp.zeros_like(values)
    return jnp.concatenate([jnp.where(low, values, zero), jnp.where(low, zero, values)], axis=0)


def join_heads(values):
    half = values.shape[0] // 2
    low = lax.broadcasted_iota(jnp.int32, (half, PAIR), 1) < HEAD
    return jnp.where(low, values[:half], values[half:])


def softmax(scores):
    expo = jnp.exp(scores - jnp.max(scores, axis=-1, keepdims=True))
    return expo / jnp.sum(expo, axis=-1, keepdims=True)


def attend(query, key, value):
    probs = softmax(mm_right(split_heads(query), key))
    return join_heads(mm(probs.astype(BF16), value)).astype(BF16)


def window_kernel(info, q0, k0, v0, q1, k1, v1, c_ref):
    for slot, (q, k, v) in enumerate(((q0, k0, v0), (q1, k1, v1))):
        start = pl.multiple_of(info[slot], ALIGN)
        for at in range(0, q.shape[1], PAIR):
            cols = slice(at, at + PAIR)
            c_ref[slot, :, cols] = attend(q[pl.ds(start, WIN), cols], k[:, cols], v[:, cols])


def whole_kernel(q0, k0, v0, q1, k1, v1, c_ref):
    rows = q0.shape[0]
    for slot, (q, k, v) in enumerate(((q0, k0, v0), (q1, k1, v1))):
        for at in range(0, q.shape[1], PAIR):
            cols = slice(at, at + PAIR)
            for row in range(0, rows, 256):
                part = slice(row, row + 256)
                c_ref[slot, part, cols] = attend(q[part, cols], k[:, cols], v[:, cols])


def gelu_parts(pre):
    cdf = 0.5 + 0.5 * lax.erf(pre * ROOT_HALF)
    return pre * cdf, cdf


def hidden_kernel(
    info, x0, x1, c_here, c_there, mix_here, mix_there, p_ref, we, be, wc, t0, t1,
    r_ref, h_ref, act_ref, gp_ref, g_ref, gout_ref, gb_ref,
):
    gain, bias = p_ref[GAIN2 : GAIN2 + 1], p_ref[BIAS2 : BIAS2 + 1]
    hidden = we.shape[1]
    for slot, x in enumerate((x0, x1)):
        start = pl.multiple_of(info[slot], ALIGN)
        branch = mm(c_here[slot], mix_here[...]) + mm(c_there[1 - slot], mix_there[...])
        resid = x[pl.ds(start, WIN)].astype(F32) + branch + p_ref[MIXB : MIXB + 1]
        normed, _ = norm(resid)
        part = slice(slot * WIN, (slot + 1) * WIN)
        r_ref[part] = resid
        h_ref[part] = (normed * gain + bias).astype(BF16)
    h = h_ref[...]
    cot = jnp.concatenate([t0[...], t1[...]], axis=0)
    total = jnp.zeros(g_ref.shape, F32)
    step = 512
    for at in range(0, hidden, step):
        cols = slice(at, at + step)
        pre = mm(h, we[:, cols]) + be[:, cols].astype(F32)
        act, cdf = gelu_parts(pre)
        act_ref[:, cols] = act.astype(BF16)
        slope = cdf + pre * (jnp.exp(-0.5 * pre * pre) * GAUSS)
        grad_pre = (mm_right(cot, wc[cols]) * slope).astype(BF16)
        gp_ref[:, cols] = grad_pre
        gb_ref[:, cols] = jnp.sum(grad_pre.astype(F32), axis=0, keepdims=True)
        total = total + mm_right(grad_pre, we[:, cols])
    g_ref[...] = total
    gout_ref[...] = total.astype(BF16)


def place(position):
    return ((position >> 3) & 1) | (((position >> 2) & 1) << 1) | (
        ((position >> 1) & 1) << 2
    ) | ((position & 1) << 3)


def spread(me, full, keep, send):
    size = full.shape[0] // PARTS
    for position in range(PARTS):
        block = pl.multiple_of((me ^ place(position)) * size, ALIGN)
        out, at = (keep, position) if position < PARTS // 2 else (send, position - PARTS // 2)
        out[at * size : (at + 1) * size] = full[pl.ds(block, size)]


def outer_kernel(info, act, gp, h, t0, t1, keep_c, send_c, keep_e, send_e, full_c, full_e):
    cot = jnp.concatenate([t0[...], t1[...]], axis=0)
    step = 256
    for at in range(0, act.shape[1], step):
        full_c[at : at + step] = mm_left(act[:, at : at + step], cot).astype(BF16)
    spread(info[6], full_c, keep_c, send_c)
    for at in range(0, h.shape[1], step):
        full_e[at : at + step] = mm_left(h[:, at : at + step], gp[...]).astype(BF16)
    spread(info[6], full_e, keep_e, send_e)


def back_kernel(
    info, g_here, g_there, r_ref, t0, t1, p_ref, c_here, mix, q0, k0, v0, q1, k1, v1,
    gr_ref, gm_ref, dq_ref, dk0, dv0, dk1, dv1, s_ref,
):
    gain = p_ref[GAIN2 : GAIN2 + 1]
    width = mix.shape[0]
    sums = [jnp.zeros((1, gain.shape[1]), F32) for _ in range(4)]
    low_parts = []
    for slot, cot_ref in enumerate((t0, t1)):
        part = slice(slot * WIN, (slot + 1) * WIN)
        other = slice((1 - slot) * WIN, (2 - slot) * WIN)
        grad = g_here[part] + g_there[other].astype(F32)
        normed, inverse = norm(r_ref[part])
        cot = cot_ref[...].astype(F32)
        resid = cot + norm_back(grad * gain, normed, inverse)
        if slot == 0:
            gr_ref[...] = resid
        low_parts.append(resid.astype(BF16))
        for at, value in enumerate((grad * normed, grad, resid, cot)):
            sums[at] = sums[at] + jnp.sum(value, axis=0, keepdims=True)
    for at in range(4):
        s_ref[at : at + 1] = sums[at]
    s_ref[4:] = jnp.zeros((s_ref.shape[0] - 4, s_ref.shape[1]), F32)
    low = jnp.concatenate(low_parts, axis=0)
    ctx = jnp.concatenate([c_here[0], c_here[1]], axis=0)
    for half in range(2):
        cols = slice(half * width, (half + 1) * width)
        gm_ref[half * width : (half + 1) * width] = mm_left(ctx, low[:, cols]).astype(BF16)
    grad_ctx = mm_right(low, mix[...]).astype(BF16)
    refs = ((q0, k0, v0, dk0, dv0), (q1, k1, v1, dk1, dv1))
    for at in range(0, width, PAIR):
        cols = slice(at, at + PAIR)
        q_sum = jnp.zeros((1, PAIR), F32)
        v_sum = jnp.zeros((1, PAIR), F32)
        for slot, (q, k, v, dk, dv) in enumerate(refs):
            start = pl.multiple_of(info[slot], ALIGN)
            query = split_heads(q[pl.ds(start, WIN), cols])
            grads = split_heads(grad_ctx[slot * WIN : (slot + 1) * WIN, cols])
            key, value = k[:, cols], v[:, cols]
            probs = softmax(mm_right(query, key))
            slopes = mm_right(grads, value)
            inner = jnp.sum(probs * slopes, axis=-1, keepdims=True)
            grad_scores = (probs * (slopes - inner)).astype(BF16)
            grad_value = mm_left(probs.astype(BF16), grads).astype(BF16)
            dv[:, cols] = grad_value
            dk[:, cols] = mm_left(grad_scores, query).astype(BF16)
            grad_query = (join_heads(mm(grad_scores, key)) * HEAD**-0.5).astype(BF16)
            dq_ref[slot, :, cols] = grad_query
            q_sum = q_sum + jnp.sum(grad_query.astype(F32), axis=0, keepdims=True)
            v_sum = v_sum + jnp.sum(grad_value.astype(F32), axis=0, keepdims=True)
        s_ref[4:5, cols] = q_sum
        s_ref[4:5, at + width : at + width + PAIR] = v_sum


def weights_kernel(info, h0, h1, dq, dk0, dv0, dk1, dv1, gm, keep, send, full):
    width = dk0.shape[1]
    wide = h0.shape[1]
    starts = [pl.multiple_of(info[slot], ALIGN) for slot in range(2)]
    rows = jnp.concatenate([h0[pl.ds(starts[0], WIN)], h1[pl.ds(starts[1], WIN)]], axis=0)
    full[:wide] = mm_left(rows, jnp.concatenate([dq[0], dq[1]], axis=0)).astype(BF16)
    for at, (d0, d1) in enumerate(((dk0, dk1), (dv0, dv1))):
        total = mm_left(h0[...], d0[...]) + mm_left(h1[...], d1[...])
        full[(at + 1) * wide : (at + 2) * wide] = total.astype(BF16)
    full[3 * wide :] = gm[...]
    spread(info[6], full, keep, send)


def first_kernel(
    info, x0, x1, p_ref, w_ref, dq, dk0, dv0, dk1, dv1, s_hidden, s_back,
    own_ref, out_ref, shared_ref, s_ref,
):
    rows = x0.shape[0]
    gain_sum = jnp.zeros((1, x0.shape[1]), F32)
    bias_sum = jnp.zeros((1, x0.shape[1]), F32)
    for slot, (x, dk, dv) in ((1, (x1, dk1, dv1)), (0, (x0, dk0, dv0))):
        start = pl.multiple_of(info[slot], ALIGN)
        own_ref[...] = mm_right(dk[...], w_ref[1]) + mm_right(dv[...], w_ref[2])
        own_ref[pl.ds(start, WIN)] += mm_right(dq[slot], w_ref[0])
        for at in range(0, rows, 256):
            part = slice(at, at + 256)
            grad = own_ref[part]
            normed, _ = norm(x[part].astype(F32))
            gain_sum = gain_sum + jnp.sum(grad * normed, axis=0, keepdims=True)
            bias_sum = bias_sum + jnp.sum(grad, axis=0, keepdims=True)
            if slot == 1:
                out_ref[part] = grad.astype(BF16)
    shared_ref[...] = jnp.zeros_like(shared_ref)
    shared_ref[0:1] = gain_sum
    shared_ref[1:2] = bias_sum
    wide = s_ref.shape[1]
    s_ref[0:8] = s_back[...]
    s_ref[8:16] = jnp.zeros((8, wide), F32)
    for at in range(s_hidden.shape[1] // wide):
        s_ref[8 + at : 9 + at] = s_hidden[:, at * wide : (at + 1) * wide]


def input_kernel(info, x, p_ref, own, there, gr, out_ref):
    gain = p_ref[GAIN1 : GAIN1 + 1]
    for at in range(0, x.shape[0], 256):
        part = slice(at, at + 256)
        normed, inverse = norm(x[part].astype(F32))
        grad = own[part] + there[part].astype(F32)
        out_ref[part] = norm_back(grad * gain, normed, inverse)
    start = pl.multiple_of(info[0], ALIGN)
    out_ref[pl.ds(start, WIN)] += gr[...]


def forward_rows(x, c_here, c_there, mix_here, mix_there, p_ref, we, be, wc):
    branch = mm(c_here, mix_here[...]) + mm(c_there, mix_there[...])
    resid = x.astype(F32) + branch + p_ref[MIXB : MIXB + 1]
    normed, _ = norm(resid)
    h = (normed * p_ref[GAIN2 : GAIN2 + 1] + p_ref[BIAS2 : BIAS2 + 1]).astype(BF16)
    total = jnp.zeros(resid.shape, F32)
    step = 512
    for at in range(0, we.shape[1], step):
        cols = slice(at, at + step)
        act, _ = gelu_parts(mm(h, we[:, cols]) + be[:, cols].astype(F32))
        total = total + mm(act.astype(BF16), wc[cols])
    return resid, total


def forward_kernel(slot, x, c_here, c_there, mix_here, mix_there, p_ref, we, be, wc, out_ref):
    for at in range(0, x.shape[0], 256):
        part = slice(at, at + 256)
        resid, total = forward_rows(
            x[part], c_here[slot, part], c_there[1 - slot, part],
            mix_here, mix_there, p_ref, we, be, wc,
        )
        if slot == 0:
            out_ref[part] = resid + total + p_ref[OUTB : OUTB + 1]
        else:
            out_ref[part] = total.astype(BF16)


def finish_kernel(base, there, out_ref):
    out_ref[...] = (base[...] + there[...].astype(F32)).astype(BF16)


def gather_rows(refs):
    rows = []
    for ref in refs:
        rows.append(ref)
    return rows


def assemble_kernel(info, low, x, core, out_ref):
    size = out_ref.shape[0] // PARTS
    for position in range(PARTS):
        block = pl.multiple_of((info[6] ^ place(position)) * size, ALIGN)
        source, at = pick(position, low, x, core)
        out_ref[pl.ds(block, size)] = source[at * size : (at + 1) * size].astype(F32)


def pick(position, low, x, core):
    if position < 4:
        return low, position
    if position < 8:
        return x, position - 4
    return core, position - 8


def assemble_mix_kernel(info, low, x, core, proj_ref, mix_ref):
    size = (low.shape[0] * 4) // PARTS
    width = mix_ref.shape[0]
    cut = proj_ref.shape[0] // size
    for position in range(PARTS):
        block = info[6] ^ place(position)
        source, at = pick(position, low, x, core)
        value = source[at * size : (at + 1) * size].astype(F32)

        @pl.when(block < cut)
        def _():
            proj_ref[pl.ds(pl.multiple_of(block * size, ALIGN), size)] = value

        @pl.when(block >= cut)
        def _():
            rest = (block - cut) * size
            half = rest // width
            row = pl.multiple_of(rest - half * width, ALIGN)
            col = pl.multiple_of(half * width, PAIR)
            mix_ref[pl.ds(row, size), pl.ds(col, width)] = value


def flip(value, mask):
    count = lax.axis_size("dp")
    return lax.ppermute(value, "dp", [(at, at ^ mask) for at in range(count)])


def swap(value):
    return lax.ppermute(value, "tensor", [(0, 1), (1, 0)])


def add_low(a, b):
    return (a.astype(F32) + b.astype(F32)).astype(BF16)


def all_reduce_blocks(keep, send):
    total = add_low(keep, flip(send, 1))
    for mask in (2, 4, 8):
        half = total.shape[0] // 2
        total = add_low(total[:half], flip(total[half:], mask))
    mask = PARTS
    while mask < lax.axis_size("dp"):
        total = add_low(total, flip(total, mask))
        mask *= 2
    for mask in (8, 4):
        total = jnp.concatenate([total, flip(total, mask)], axis=0)
    x = flip(total, 2)
    core = flip(jnp.concatenate([total, x], axis=0), 1)
    return total, x, core


def body(
    inputs, out_grad, span_starts, span_lengths, norm1_gain, norm1_bias, projections,
    query_value_bias, mix_weight, mix_bias, norm2_gain, norm2_bias, expand_weight, expand_bias,
    contract_weight, contract_bias,
):
    rows, wide = inputs.shape
    width = projections.shape[2]
    hidden = expand_weight.shape[1]
    side = lax.axis_index("tensor")
    here = lax.axis_index("dp") % PARTS
    starts = jnp.where(side == 0, span_starts, span_starts[::-1])
    lengths = jnp.where(side == 0, span_lengths, span_lengths[::-1])
    windows = jnp.minimum(starts // RATE // ALIGN * ALIGN, rows - WIN)
    info = jnp.concatenate([windows, starts, starts + lengths, here[None], here[None]])

    other = swap(inputs)
    at = (windows[0] + jnp.arange(WIN, dtype=jnp.int32)) * RATE
    masked = (at < starts[0] + lengths[0]) & (at + RATE > starts[0])
    piece = lax.dynamic_slice_in_dim(out_grad, windows[0], WIN)
    cot0 = jnp.where(masked[:, None], piece, jnp.zeros_like(piece))
    cot1 = swap(cot0)
    mix_other = swap(mix_weight)

    def row(vector):
        return jnp.pad(vector.astype(F32), (0, wide - vector.shape[0]))[None]

    packed = jnp.concatenate(
        [row(v) for v in (norm1_gain, norm1_bias, mix_bias, norm2_gain, norm2_bias, contract_bias)]
        + [row(query_value_bias[0]), row(query_value_bias[1])]
    )
    expand_row = expand_bias[None]

    low_rows = struct((rows, wide), BF16)
    low_heads = struct((rows, width), BF16)

    def project(x):
        return call(
            project_kernel, (low_rows, low_heads, low_heads, low_heads), "project",
            6 * rows * wide * width, (x, packed, projections),
        )

    h0, q0, k0, v0 = project(inputs)
    h1, q1, k1, v1 = project(other)
    attn = (q0, k0, v0, q1, k1, v1)
    (ctx,) = call(
        window_kernel, (struct((2, WIN, width), BF16),), "window",
        8 * WIN * rows * width, (info,) + attn, smem=1,
    )
    ctx_there = swap(ctx)
    wins = (2 * WIN, wide)
    resid, h_two, act, grad_pre, g_here, g_out, s_hidden = call(
        hidden_kernel,
        (
            struct(wins, F32), struct(wins, BF16), struct((2 * WIN, hidden), BF16),
            struct((2 * WIN, hidden), BF16), struct(wins, F32), struct(wins, BF16),
            struct((1, hidden), F32),
        ),
        "hidden", 12 * WIN * wide * hidden,
        (
            info, inputs, other, ctx, ctx_there, mix_weight, mix_other, packed, expand_weight,
            expand_row, contract_weight, cot0, cot1,
        ),
        smem=1,
    )
    g_there = swap(g_out)
    keep_c, send_c, keep_e, send_e = call(
        outer_kernel,
        (
            struct((hidden // 2, wide), BF16), struct((hidden // 2, wide), BF16),
            struct((wide // 2, hidden), BF16), struct((wide // 2, hidden), BF16),
        ),
        "outer", 8 * WIN * wide * hidden,
        (info, act, grad_pre, h_two, cot0, cot1),
        scratch=(pltpu.VMEM((hidden, wide), BF16), pltpu.VMEM((wide, hidden), BF16)), smem=1,
    )
    blocks_c = all_reduce_blocks(keep_c, send_c)
    blocks_e = all_reduce_blocks(keep_e, send_e)
    grad_resid, grad_mix, dq, dk0, dv0, dk1, dv1, s_back = call(
        back_kernel,
        (
            struct((WIN, wide), F32), struct((2 * width, width), BF16),
            struct((2, WIN, width), BF16), low_heads, low_heads, low_heads, low_heads,
            struct((8, wide), F32),
        ),
        "back", 20 * WIN * rows * width,
        (info, g_here, g_there, resid, cot0, cot1, packed, ctx, mix_weight) + attn, smem=1,
    )
    stacked = (4 * wide) // 2
    keep_a, send_a = call(
        weights_kernel, (struct((stacked, width), BF16), struct((stacked, width), BF16)),
        "weights", 10 * rows * wide * width,
        (info, h0, h1, dq, dk0, dv0, dk1, dv1, grad_mix),
        scratch=(pltpu.VMEM((2 * stacked, width), BF16),), smem=1,
    )
    blocks_a = all_reduce_blocks(keep_a, send_a)
    own, out, shared, small = call(
        first_kernel,
        (
            struct((rows, wide), F32), low_rows, struct((8, wide), F32),
            struct((16, wide), F32),
        ),
        "first", 10 * rows * wide * width,
        (info, inputs, other, packed, projections, dq, dk0, dv0, dk1, dv1, s_hidden, s_back),
        smem=1,
    )
    there = swap(out)
    (input_grad,) = call(
        input_kernel, (struct((rows, wide), F32),), "input", 0,
        (info, inputs, packed, own, there, grad_resid), smem=1,
    )

    (ctx_whole,) = call(
        whole_kernel, (struct((2, rows, width), BF16),), "whole", 8 * rows * rows * width, attn
    )
    ctx_whole_there = swap(ctx_whole)

    def forward(slot, x, kind):
        return call(
            partial(forward_kernel, slot), (struct((rows, wide), kind),), "forward",
            4 * rows * wide * hidden,
            (
                x, ctx_whole, ctx_whole_there, mix_weight, mix_other, packed, expand_weight,
                expand_row, contract_weight,
            ),
        )[0]

    forward_out = forward(1, other, BF16)
    forward_there = swap(forward_out)
    base = forward(0, inputs, F32)
    (layer_out,) = call(
        finish_kernel, (struct((rows, wide), BF16),), "finish", 0, (base, forward_there)
    )

    small = jnp.concatenate([shared + swap(shared), small])
    mask = 1
    while mask < lax.axis_size("dp"):
        small = small + flip(small, mask)
        mask *= 2

    def assemble(blocks, shape):
        return call(assemble_kernel, (struct(shape, F32),), "assemble", 0, (info,) + blocks, smem=1)[0]

    grad_contract = assemble(blocks_c, (hidden, wide))
    grad_expand = assemble(blocks_e, (wide, hidden))
    grad_proj, grad_mix_weight = call(
        assemble_mix_kernel, (struct((3 * wide, width), F32), struct((width, wide), F32)),
        "assemble_mix", 0, (info,) + blocks_a, smem=1,
    )
    return (
        layer_out,
        input_grad,
        small[0],
        small[1],
        grad_proj.reshape(3, wide, width),
        small[12].reshape(2, width),
        grad_mix_weight,
        small[10],
        small[8],
        small[9],
        grad_expand,
        small[16 : 16 + hidden // wide].reshape(hidden),
        grad_contract,
        small[11],
    )


def solution(mesh):
    rows = P(("dp", "tensor"), None)
    return jax.shard_map(
        body,
        mesh=mesh,
        in_specs=(
            rows, rows, P("dp"), P("dp"), P(), P(), P(None, None, "tensor"), P(None, "tensor"),
            P("tensor", None), P(), P(), P(), P(None, "tensor"), P("tensor"), P("tensor", None),
            P(),
        ),
        out_specs=(
            rows, rows, P(), P(), P(None, None, "tensor"), P(None, "tensor"), P("tensor", None),
            P(), P(), P(), P(None, "tensor"), P("tensor"), P("tensor", None), P(),
        ),
        check_vma=False,
    )
```

```python
from functools import partial

import jax
import jax.numpy as jnp
from jax import lax
from jax.experimental import pallas as pl
from jax.experimental.pallas import tpu as pltpu
from jax.sharding import PartitionSpec as P

RATE = 4
HEAD = 64
PAIR = 2 * HEAD
EPS = 1e-12
WIN = 144
ALIGN = 16
OWN_LIMIT = 56
PARTS = 16
MASKS_C = (2, 4, 8)
MASKS_E = (4, 2, 8)
MASKS_A = (1, 4, 2, 8)
MASKS_B = (1, 2, 4, 8)
F32 = jnp.float32
BF16 = jnp.bfloat16
MIB = 1 << 20
ROOT_HALF = 0.7071067811865476
GAUSS = 0.3989422804014327

GAIN1, BIAS1, MIXB, GAIN2, BIAS2, OUTB, QVB, EXPB = range(8)
STARTS, LENGTHS, SIDE, HERE = 0, 2, 4, 5


def mm(a, b):
    return lax.dot_general(a, b, (((1,), (0,)), ((), ())), preferred_element_type=F32)


def mm_right(a, b):
    return lax.dot_general(a, b, (((1,), (1,)), ((), ())), preferred_element_type=F32)


def mm_left(a, b):
    return lax.dot_general(a, b, (((0,), (0,)), ((), ())), preferred_element_type=F32)


def norm(values):
    mean = jnp.mean(values, axis=-1, keepdims=True)
    centred = values - mean
    var = jnp.mean(centred * centred, axis=-1, keepdims=True)
    inverse = lax.rsqrt(var + EPS)
    return centred * inverse, inverse


def norm_back(scaled, normed, inverse):
    inner = jnp.mean(scaled, axis=-1, keepdims=True)
    cross = jnp.mean(scaled * normed, axis=-1, keepdims=True)
    return inverse * (scaled - inner - normed * cross)


class Fetched:
    def __init__(self, source, buffer, sem):
        self.buffer = buffer
        self.copy = pltpu.make_async_copy(source, buffer, sem)
        self.copy.start()

    def get(self):
        if self.copy is not None:
            self.copy.wait()
            self.copy = None
        return self.buffer


class Sent:
    def __init__(self, target, buffer, sem):
        self.buffer = buffer
        self.copy = pltpu.make_async_copy(buffer, target, sem)
        self.started = False

    def send(self):
        if not self.started:
            self.copy.start()
            self.started = True

    def finish(self):
        self.send()
        self.copy.wait()


def call(kernel, name, time, args, outs, scratch=(), limit=24):
    places = {
        "s": pl.BlockSpec(memory_space=pltpu.SMEM), "v": pl.BlockSpec(memory_space=pltpu.VMEM),
        "h": pl.BlockSpec(memory_space=pltpu.HBM), "r": pl.BlockSpec(memory_space=pltpu.HBM),
    }
    buffers = []
    for place, value in [*args, *outs]:
        if place == "h":
            buffers += [pltpu.VMEM(value.shape, value.dtype), pltpu.SemaphoreType.DMA]

    def whole(*refs):
        moving = list(refs[len(args) + len(outs) : len(args) + len(outs) + len(buffers)])
        given, results = [], []
        for at, (place, _) in enumerate(args):
            ref = refs[at]
            given.append(Fetched(ref, moving.pop(0), moving.pop(0)) if place == "h" else ref)
        for at, (place, _) in enumerate(outs):
            ref = refs[len(args) + at]
            results.append(Sent(ref, moving.pop(0), moving.pop(0)) if place == "h" else ref)
        kernel(*given, *results, *refs[len(args) + len(outs) + len(buffers) :])
        for value in given:
            if isinstance(value, Fetched):
                value.get()
        for value in results:
            if isinstance(value, Sent):
                value.send()
        for value in results:
            if isinstance(value, Sent):
                value.finish()

    return pl.pallas_call(
        whole,
        out_shape=tuple(value for _, value in outs),
        in_specs=[places[place] for place, _ in args],
        out_specs=tuple(places[place] for place, _ in outs),
        scratch_shapes=buffers + list(scratch),
        compiler_params=pltpu.CompilerParams(vmem_limit_bytes=limit * MIB),
        cost_estimate=pl.CostEstimate(
            flops=int(time * 5e8), bytes_accessed=int(time * 5e5), transcendentals=0
        ),
        name=name,
    )(*(value for _, value in args))


def struct(shape, kind):
    return jax.ShapeDtypeStruct(shape, kind)


def window(info, slot, rows):
    side = info[SIDE]
    first = info[STARTS + (side if slot == 0 else 1 - side)]
    return pl.multiple_of(jnp.minimum(first // (RATE * ALIGN) * ALIGN, rows - WIN), ALIGN)


def project_rows(x, p_ref, w, h, q, k, v):
    rows = x.shape[0]
    width = q.buffer.shape[1]
    gain, bias = p_ref[GAIN1 : GAIN1 + 1], p_ref[BIAS1 : BIAS1 + 1]
    q_bias, v_bias = p_ref[QVB : QVB + 1, :width], p_ref[QVB : QVB + 1, width : 2 * width]
    for at in range(0, rows, 256):
        part = slice(at, at + 256)
        normed, _ = norm(x[part].astype(F32))
        low = (normed * gain + bias).astype(BF16)
        h.buffer[part] = low
        weights = w.get()
        q.buffer[part] = (mm(low, weights[0]) + q_bias).astype(BF16) * BF16(HEAD**-0.5)
        k.buffer[part] = mm(low, weights[1]).astype(BF16)
        v.buffer[part] = (mm(low, weights[2]) + v_bias).astype(BF16)
    for sent in (h, q, k, v):
        sent.send()


def split_heads(values):
    low = lax.broadcasted_iota(jnp.int32, values.shape, 1) < HEAD
    zero = jnp.zeros_like(values)
    return jnp.concatenate([jnp.where(low, values, zero), jnp.where(low, zero, values)], axis=0)


def join_heads(values):
    half = values.shape[0] // 2
    low = lax.broadcasted_iota(jnp.int32, (half, PAIR), 1) < HEAD
    return jnp.where(low, values[:half], values[half:])


def softmax(scores):
    expo = jnp.exp(scores - jnp.max(scores, axis=-1, keepdims=True))
    return expo / jnp.sum(expo, axis=-1, keepdims=True)


def attend(query, key, value):
    probs = softmax(mm_right(split_heads(query), key))
    return join_heads(mm(probs.astype(BF16), value)).astype(BF16)


def attend_rows(q, k, v, store):
    for at in range(0, q.shape[1], PAIR):
        cols = slice(at, at + PAIR)
        for row in range(0, q.shape[0], 256):
            part = slice(row, row + 256)
            store(part, cols, attend(q[part, cols], k[:, cols], v[:, cols]))


def own_kernel(
    info, x, g1, b1, mb, g2, b2, ob, qv, eb, w, grad, h, q, k, v, c, win_ref, cot_ref, p_ref,
    piece, sem,
):
    rows, wide = x.buffer.shape
    width = qv.shape[1]
    for at, vector in enumerate((g1, b1, mb, g2, b2, ob)):
        p_ref[at : at + 1] = vector[...].astype(F32).reshape(1, wide)
    p_ref[QVB : QVB + 1, :width] = qv[0:1].astype(F32)
    p_ref[QVB : QVB + 1, width : 2 * width] = qv[1:2].astype(F32)
    long = eb[...].astype(F32)
    for at in range(eb.shape[0] // wide):
        p_ref[EXPB + at : EXPB + at + 1] = long[at * wide : (at + 1) * wide].reshape(1, wide)
    start = window(info, 0, rows)
    copy = pltpu.make_async_copy(grad.at[pl.ds(start, WIN)], piece, sem)
    copy.start()
    project_rows(x.get(), p_ref, w, h, q, k, v)
    copy.wait()
    side = info[SIDE]
    first = info[STARTS + side]
    last = first + info[LENGTHS + side]
    spot = (start + lax.broadcasted_iota(jnp.int32, piece.shape, 0)) * RATE
    kept = jnp.where((spot < last) & (spot + RATE > first), piece[...].astype(F32), 0.0)
    cot_ref[...] = kept.astype(BF16)

    def store(part, cols, value):
        c.buffer[part, cols] = value

    attend_rows(q.buffer, k.buffer, v.buffer, store)
    win_ref[...] = c.buffer[pl.ds(start, WIN)]


def other_kernel(info, x_ref, p_ref, w, win_ref, h, q, k, v, c_ref):
    project_rows(x_ref, p_ref, w, h, q, k, v)
    start = window(info, 1, x_ref.shape[0])
    c_ref[0] = win_ref[...]
    for at in range(0, q.buffer.shape[1], PAIR):
        cols = slice(at, at + PAIR)
        query = q.buffer[pl.ds(start, WIN), cols]
        c_ref[1, :, cols] = attend(query, k.buffer[:, cols], v.buffer[:, cols])


def whole_kernel(q, k, v, own, c):
    def store(part, cols, value):
        c.buffer[1, part, cols] = value

    c.buffer[0] = own.get()[...]
    attend_rows(q.get(), k.get(), v.get(), store)


def gelu_parts(pre):
    cdf = 0.5 + 0.5 * lax.erf(pre * ROOT_HALF)
    return pre * cdf, cdf


def hidden_kernel(
    info, x0, x1, c_here, c_there, mix_here, m0, m1, m2, p_ref, we, wc, t0, t1,
    r_ref, h_ref, act_ref, gp_ref, g_ref, gout_ref, gb_ref, act_far, gp_far, mix_there,
    act_full, gp_full,
):
    gain, bias = p_ref[GAIN2 : GAIN2 + 1], p_ref[BIAS2 : BIAS2 + 1]
    wide, hidden = we.buffer.shape
    quarter = m0.shape[0]
    spot = info[HERE] & 3
    for at, piece in enumerate((m0[...], m1[...], m2[:quarter], m2[quarter:])):
        place_at = pl.multiple_of((spot ^ (0, 2, 1, 3)[at]) * quarter, ALIGN)
        mix_there.buffer[pl.ds(place_at, quarter)] = piece
    mix_there.send()
    for slot, x in enumerate((x0, x1)):
        rows = x.get() if slot == 0 else x
        start = window(info, slot, rows.shape[0])
        branch = mm(c_here[slot], mix_here.get()[...])
        branch = branch + mm(c_there[1 - slot], mix_there.buffer[...])
        resid = rows[pl.ds(start, WIN)].astype(F32) + branch + p_ref[MIXB : MIXB + 1]
        normed, _ = norm(resid)
        part = slice(slot * WIN, (slot + 1) * WIN)
        r_ref[part] = resid
        h_ref[part] = (normed * gain + bias).astype(BF16)
    h = h_ref[...]
    cot = jnp.concatenate([t0[...], t1[...]], axis=0)
    total = jnp.zeros(g_ref.shape, F32)
    for at in range(hidden // wide):
        cols = slice(at * wide, (at + 1) * wide)
        up = we.get()[:, cols]
        pre = mm(h, up) + p_ref[EXPB + at : EXPB + at + 1]
        act, cdf = gelu_parts(pre)
        act_full[:, cols] = act.astype(BF16)
        slope = cdf + pre * (jnp.exp(-0.5 * pre * pre) * GAUSS)
        grad_pre = (mm_right(cot, wc.get()[cols]) * slope).astype(BF16)
        gp_full[:, cols] = grad_pre
        gb_ref[:, cols] = jnp.sum(grad_pre.astype(F32), axis=0, keepdims=True)
        total = total + mm_right(grad_pre, up)
    g_ref[...] = total
    gout_ref[...] = total.astype(BF16)
    half = hidden // 2
    core = info[HERE] & 1
    own = pl.ds(pl.multiple_of(core * half, PAIR), half)
    their = pl.ds(pl.multiple_of((1 - core) * half, PAIR), half)
    act_ref[...] = act_full[:, own]
    gp_ref[...] = gp_full[:, own]
    act_far[...] = act_full[:, their]
    gp_far[...] = gp_full[:, their]


def owner(device, position, masks):
    splits = masks[:-1]
    bits = 0
    for mask in splits:
        bits = bits * 2 + (device // mask) % 2
    return bits ^ position


def spread(device, masks, full, keep, send):
    parts = 1 << (len(masks) - 1)
    size = full.shape[0] // parts
    for position in range(parts):
        block = pl.multiple_of(owner(device, position, masks) * size, ALIGN)
        out, at = (keep, position) if position < parts // 2 else (send, position - parts // 2)
        out[at * size : (at + 1) * size] = full[pl.ds(block, size)]


def outer_kernel(
    masks_c, masks_e, info, act, gp, h, act_far, gp_far, h_far, t0, t1, t_far,
    keep_c, send_c, keep_e, send_e, full,
):
    step = 256

    def product(left, right):
        for at in range(0, full.shape[0], step):
            total = jnp.zeros((step, full.shape[1]), F32)
            for rows, others in zip(left, right):
                total = total + mm_left(rows[:, at : at + step], others)
            full[at : at + step] = total.astype(BF16)

    cot = jnp.concatenate([t0[...], t1[...]], axis=0)
    product((act, act_far), (cot, t_far[...]))
    spread(info[HERE], masks_c, full, keep_c, send_c)
    product((h, h_far), (gp[...], gp_far[...]))
    spread(info[HERE], masks_e, full, keep_e, send_e)


def back_kernel(
    info, g_here, g_there, r_ref, t0, t1, p_ref, c_here, mix, q0, k0, v0, q1, k1, v1,
    gr, gm_ref, dq_ref, dk0, dv0, dk1, dv1, s_ref,
):
    gain = p_ref[GAIN2 : GAIN2 + 1]
    width = mix.buffer.shape[0]
    sums = [jnp.zeros((1, gain.shape[1]), F32) for _ in range(4)]
    low_parts = []
    for slot, cot_ref in enumerate((t0, t1)):
        part = slice(slot * WIN, (slot + 1) * WIN)
        other = slice((1 - slot) * WIN, (2 - slot) * WIN)
        grad = g_here[part] + g_there[other].astype(F32)
        normed, inverse = norm(r_ref[part])
        cot = cot_ref[...].astype(F32)
        resid = cot + norm_back(grad * gain, normed, inverse)
        if slot == 0:
            gr.buffer[...] = resid
            gr.send()
        low_parts.append(resid.astype(BF16))
        for at, value in enumerate((grad * normed, grad, resid, cot)):
            sums[at] = sums[at] + jnp.sum(value, axis=0, keepdims=True)
    for at in range(4):
        s_ref[at : at + 1] = sums[at]
    s_ref[4:] = jnp.zeros((s_ref.shape[0] - 4, s_ref.shape[1]), F32)
    low = jnp.concatenate(low_parts, axis=0)
    ctx = jnp.concatenate([c_here[0], c_here[1]], axis=0)
    for half in range(2):
        cols = slice(half * width, (half + 1) * width)
        gm_ref[half * width : (half + 1) * width] = mm_left(ctx, low[:, cols]).astype(BF16)
    grad_ctx = mm_right(low, mix.get()[...]).astype(BF16)
    refs = ((q0, k0, v0, dk0, dv0), (q1, k1, v1, dk1, dv1))
    for at in range(0, width, PAIR):
        cols = slice(at, at + PAIR)
        q_sum = jnp.zeros((1, PAIR), F32)
        v_sum = jnp.zeros((1, PAIR), F32)
        for slot, (q, k, v, dk, dv) in enumerate(refs):
            q, k, v = q.get(), k.get(), v.get()
            start = window(info, slot, q.shape[0])
            query = split_heads(q[pl.ds(start, WIN), cols])
            grads = split_heads(grad_ctx[slot * WIN : (slot + 1) * WIN, cols])
            key, value = k[:, cols], v[:, cols]
            probs = softmax(mm_right(query, key))
            slopes = mm_right(grads, value)
            inner = jnp.sum(probs * slopes, axis=-1, keepdims=True)
            grad_scores = (probs * (slopes - inner)).astype(BF16)
            grad_value = mm_left(probs.astype(BF16), grads).astype(BF16)
            dv[:, cols] = grad_value
            dk[:, cols] = mm_left(grad_scores, query).astype(BF16)
            grad_query = (join_heads(mm(grad_scores, key)) * HEAD**-0.5).astype(BF16)
            dq_ref[slot, :, cols] = grad_query
            q_sum = q_sum + jnp.sum(grad_query.astype(F32), axis=0, keepdims=True)
            v_sum = v_sum + jnp.sum(grad_value.astype(F32), axis=0, keepdims=True)
        s_ref[4:5, cols] = q_sum
        s_ref[4:5, at + width : at + width + PAIR] = v_sum


def spread_rows(info, masks, full, keep, send):
    spread(info[HERE], masks, full, keep, send)


def query_key_kernel(masks, info, h0, h1, dq, dk0, dk1, keep, send, full):
    h0, h1 = h0.get(), h1.get()
    wide = h0.shape[1]
    starts = [window(info, slot, h0.shape[0]) for slot in range(2)]
    rows = jnp.concatenate([h0[pl.ds(starts[0], WIN)], h1[pl.ds(starts[1], WIN)]], axis=0)
    full[:wide] = mm_left(rows, jnp.concatenate([dq[0], dq[1]], axis=0)).astype(BF16)
    full[wide:] = (mm_left(h0[...], dk0[...]) + mm_left(h1[...], dk1[...])).astype(BF16)
    spread_rows(info, masks, full, keep, send)


def value_mix_kernel(masks, info, h0, h1, dv0, dv1, gm, keep, send, full):
    h0, h1 = h0.get(), h1.get()
    wide = h0.shape[1]
    full[:wide] = (mm_left(h0[...], dv0[...]) + mm_left(h1[...], dv1[...])).astype(BF16)
    full[wide:] = gm[...]
    spread_rows(info, masks, full, keep, send)


def first_kernel(
    info, x0, x1, p_ref, w, dq, dk0, dv0, dk1, dv1, s_hidden, s_back,
    own, out_ref, shared_ref, s_ref, grads,
):
    rows, wide = x1.shape
    gain_sum = jnp.zeros((1, wide), F32)
    bias_sum = jnp.zeros((1, wide), F32)
    for slot, dk, dv in ((1, dk1, dv1), (0, dk0, dv0)):
        weights = w.get()
        kept = own.buffer if slot == 0 else grads
        x = x0.get() if slot == 0 else x1
        start = window(info, slot, rows)
        kept[...] = mm_right(dk[...], weights[1]) + mm_right(dv[...], weights[2])
        kept[pl.ds(start, WIN)] += mm_right(dq[slot], weights[0])
        for at in range(0, rows, 256):
            part = slice(at, at + 256)
            grad = kept[part]
            normed, _ = norm(x[part].astype(F32))
            gain_sum = gain_sum + jnp.sum(grad * normed, axis=0, keepdims=True)
            bias_sum = bias_sum + jnp.sum(grad, axis=0, keepdims=True)
            if slot == 1:
                out_ref[part] = grad.astype(BF16)
    width = shared_ref.shape[1]
    shared_ref[...] = jnp.zeros_like(shared_ref)
    s_ref[...] = jnp.zeros_like(s_ref)
    for half in range(wide // width):
        cols = slice(half * width, (half + 1) * width)
        shared_ref[half : half + 1] = gain_sum[:, cols]
        shared_ref[2 + half : 3 + half] = bias_sum[:, cols]
        for at in range(5):
            s_ref[2 * at + half : 2 * at + half + 1] = s_back[at : at + 1, cols]
    for at in range(s_hidden.shape[1] // width):
        s_ref[10 + at : 11 + at] = s_hidden[:, at * width : (at + 1) * width]


def input_kernel(info, x, p_ref, own, there, gr, out):
    gain = p_ref[GAIN1 : GAIN1 + 1]
    x = x.get()
    rows = x.shape[0]
    for at in range(0, rows, 256):
        part = slice(at, at + 256)
        normed, inverse = norm(x[part].astype(F32))
        grad = own.get()[part] + there[part].astype(F32)
        out.buffer[part] = norm_back(grad * gain, normed, inverse)
    out.buffer[pl.ds(window(info, 0, rows), WIN)] += gr.get()[...]


def forward_kernel(slot, x, c_here, c_there, mix_here, mix_there, p_ref, we, wc, out):
    rows = x.get() if slot == 0 else x
    wide, hidden = we.buffer.shape
    for at in range(0, rows.shape[0], 256):
        part = slice(at, at + 256)
        branch = mm(c_here.get()[slot, part], mix_here.get()[...])
        branch = branch + mm(c_there[1 - slot, part], mix_there.get()[...])
        resid = rows[part].astype(F32) + branch + p_ref[MIXB : MIXB + 1]
        normed, _ = norm(resid)
        h = (normed * p_ref[GAIN2 : GAIN2 + 1] + p_ref[BIAS2 : BIAS2 + 1]).astype(BF16)
        total = jnp.zeros(resid.shape, F32)
        for row in range(hidden // wide):
            cols = slice(row * wide, (row + 1) * wide)
            act, _ = gelu_parts(mm(h, we.get()[:, cols]) + p_ref[EXPB + row : EXPB + row + 1])
            total = total + mm(act.astype(BF16), wc.get()[cols])
        if slot == 0:
            out.buffer[part] = resid + total + p_ref[OUTB : OUTB + 1]
        else:
            out[part] = total.astype(BF16)


def finish_kernel(base, there, out):
    out.buffer[...] = (base.get()[...] + there[...].astype(F32)).astype(BF16)


def pick(position, near, far, size, parts):
    half = parts // 2
    source, at = (near, position) if position < half else (far, position - half)
    return source[at * size : (at + 1) * size].astype(F32)


def assemble_kernel(masks, along, info, near, far, out, made, sems):
    rows, cols = near.shape
    parts = 1 << (len(masks) - 1)
    size = rows // parts
    core = info[HERE] & 1
    copies = []
    for at, (side, source) in enumerate(((core, near), (1 - core, far))):
        for position in range(parts):
            block = owner(info[HERE], position, masks) * size
            if along == 0:
                spot = pl.ds(pl.multiple_of(side * rows + block, ALIGN), size)
            else:
                spot = (
                    pl.ds(pl.multiple_of(block, ALIGN), size),
                    pl.ds(pl.multiple_of(side * cols, PAIR), cols),
                )
            index = at * parts + position
            made[index] = source[position * size : (position + 1) * size].astype(F32)
            copies.append(pltpu.make_async_copy(made.at[index], out.at[spot], sems.at[index]))
            copies[-1].start()
    for copy in copies:
        copy.wait()


def assemble_attention_kernel(
    masks_a, masks_b, info, near_a, far_a, near_b, far_b, extra, proj, mix, qvb, long, *rest
):
    *vectors, made, sems = rest
    size, width = made.shape[1:]
    parts = made.shape[0] // 2
    copies = []
    for position in range(parts):
        block = owner(info[HERE], position, masks_a) * size
        spot = pl.ds(pl.multiple_of(block, ALIGN), size)
        made[position] = pick(position, near_a, far_a, size, parts)
        copies.append(pltpu.make_async_copy(made.at[position], proj.at[spot], sems.at[position]))
        copies[-1].start()
    base = parts * size
    cut = (proj.shape[0] - base) // size
    for position in range(parts):
        index = parts + position
        block = owner(info[HERE], position, masks_b)
        made[index] = pick(position, near_b, far_b, size, parts)

        @pl.when(block < cut)
        def _():
            spot = pl.ds(pl.multiple_of(base + block * size, ALIGN), size)
            pltpu.make_async_copy(made.at[index], proj.at[spot], sems.at[index]).start()

        @pl.when(block >= cut)
        def _():
            left = (block - cut) * size
            half = left // width
            row = pl.multiple_of(left - half * width, ALIGN)
            col = pl.multiple_of(half * width, PAIR)
            spot = (pl.ds(row, size), pl.ds(col, width))
            pltpu.make_async_copy(made.at[index], mix.at[spot], sems.at[index]).start()

        copies.append(
            pltpu.make_async_copy(made.at[index], proj.at[pl.ds(0, size)], sems.at[index])
        )
    rows, more = near_b.shape[0], extra.shape[0]
    total = extra[...] + far_b[rows : rows + more].astype(F32)
    total = total + far_b[rows + more : rows + 2 * more].astype(F32)
    for vector, at in zip(vectors, (0, 2, 8, 10, 12, 14)):
        vector[:width] = total[at].reshape(width)
        vector[width:] = total[at + 1].reshape(width)
    qvb[...] = total[16:18]
    for at in range(long.shape[0] // width):
        long[at * width : (at + 1) * width] = total[18 + at].reshape(width)
    for copy in copies:
        copy.wait()


def flip(value, mask):
    count = lax.axis_size("dp")
    return lax.ppermute(value, "dp", [(at, at ^ mask) for at in range(count)])


def swap(value):
    return lax.ppermute(value, "tensor", [(0, 1), (1, 0)])


def add_low(a, b):
    return (a.astype(F32) + b.astype(F32)).astype(BF16)


class Order:
    def __init__(self):
        self.last = None

    def tie(self, value, *others):
        return lax.optimization_barrier((value,) + others)[0]

    def run(self, step, first, *rest):
        if self.last is not None:
            first = self.tie(first, self.last)
        out = step(first, *rest)
        self.last = out[0] if isinstance(out, tuple) else out
        return out


class Reduction:
    def __init__(self, order, keep, send, masks):
        self.order, self.masks, self.at = order, masks, 0
        self.keep, self.coming = keep, flip(send, masks[0])
        self.joins = [*masks[:-1]] if 1 in masks else [1, *masks[:-1]]
        self.extra = None

    def send(self, mask):
        value = self.total
        if self.extra is not None:
            high = self.extra.astype(BF16)
            low = (self.extra - high.astype(F32)).astype(BF16)
            value = jnp.concatenate([value, high, low])
        self.coming = flip(value, mask)

    def take(self, merge):
        if self.extra is None:
            self.total = self.order.run(lambda coming, held: merge(held, coming), self.coming, self.total)
            return

        def both(coming, held, extra):
            size, more = held.shape[0], extra.shape[0]
            parts = [coming[size + at * more : size + (at + 1) * more] for at in range(2)]
            extra = extra + parts[0].astype(F32) + parts[1].astype(F32)
            return merge(held, coming[:size]), extra

        self.total, self.extra = self.order.run(both, self.coming, self.total, self.extra)

    def step(self):
        splits = len(self.masks) - 1
        self.at += 1
        if self.at <= splits:
            total = self.order.run(add_low, self.coming, self.keep)
            if self.at < splits:
                half = total.shape[0] // 2
                self.keep, self.coming = total[:half], flip(total[half:], self.masks[self.at])
                return
            self.total = total
            self.send(self.masks[-1])
            return
        if self.at == splits + 1:
            self.take(add_low)
            mask = PARTS
            while mask < lax.axis_size("dp"):
                self.total = add_low(self.total, flip(self.total, mask))
                if self.extra is not None:
                    self.extra = self.extra + flip(self.extra, mask)
                mask *= 2
        else:
            self.take(lambda held, coming: jnp.concatenate([held, coming]))
        self.send(self.joins.pop())

    def blocks(self):
        while self.joins:
            self.step()
        return self.total, self.coming


def body(
    inputs, out_grad, span_starts, span_lengths, norm1_gain, norm1_bias, projections,
    query_value_bias, mix_weight, mix_bias, norm2_gain, norm2_bias, expand_weight, expand_bias,
    contract_weight, contract_bias,
):
    rows, wide = inputs.shape
    width = projections.shape[2]
    hidden = expand_weight.shape[1]
    side = lax.axis_index("tensor")
    here = lax.axis_index("dp") % PARTS
    info = jnp.concatenate([span_starts, span_lengths, side[None], here[None]])
    order = Order()
    run = order.run

    other = swap(inputs)
    vectors = (
        norm1_gain, norm1_bias, mix_bias, norm2_gain, norm2_bias, contract_bias,
        query_value_bias, expand_bias,
    )
    quarter = width // 4
    mix_part = lax.dynamic_slice_in_dim(mix_weight, (here & 3) * quarter, quarter)

    low_rows = struct((rows, wide), BF16)
    full_rows = struct((rows, wide), F32)
    low_heads = struct((rows, width), BF16)
    wins = struct((2 * WIN, wide), BF16)
    full_wins = struct((2 * WIN, wide), F32)
    win_heads = struct((2, WIN, width), BF16)
    projected = [("h", low_rows), ("h", low_heads), ("h", low_heads), ("h", low_heads)]

    h0, q0, k0, v0, ctx_own, window_own, cot0, packed = run(
        lambda x: call(
            own_kernel, "own", 5,
            [("s", info), ("h", x)] + [("v", vector) for vector in vectors]
            + [("h", projections), ("r", out_grad)],
            projected
            + [
                ("h", low_heads), ("v", struct((WIN, width), BF16)),
                ("v", struct((WIN, wide), BF16)), ("v", struct((EXPB + hidden // wide, wide), F32)),
            ],
            [pltpu.VMEM((WIN, wide), BF16), pltpu.SemaphoreType.DMA], limit=OWN_LIMIT,
        ),
        inputs,
    )
    other = order.tie(other, cot0)
    mix0 = swap(order.tie(mix_part, other))
    cot1 = swap(order.tie(cot0, other))
    h1, q1, k1, v1, ctx = run(
        lambda x: call(
            other_kernel, "other", 3,
            [("s", info), ("v", x), ("v", packed), ("h", projections), ("v", window_own)],
            projected + [("v", win_heads)],
        ),
        other,
    )
    ctx_there = swap(ctx)
    mix1 = flip(order.tie(mix0, ctx), 2)
    mix2 = flip(jnp.concatenate([mix0, mix1]), 1)
    half = hidden // 2
    low_half = struct((2 * WIN, half), BF16)
    resid, h_two, act, grad_pre, g_here, g_out, s_hidden, *far, mix_other = run(
        lambda there: call(
            hidden_kernel, "hidden", 4.6,
            [
                ("s", info), ("h", inputs), ("v", other), ("v", ctx), ("v", there),
                ("h", mix_weight), ("v", mix0), ("v", mix1), ("v", mix2), ("v", packed),
                ("h", expand_weight), ("h", contract_weight), ("v", cot0), ("v", cot1),
            ],
            [
                ("v", full_wins), ("v", wins), ("v", low_half), ("v", low_half), ("v", full_wins),
                ("v", wins), ("v", struct((1, hidden), F32)), ("v", low_half), ("v", low_half),
                ("h", struct((width, wide), BF16)),
            ],
            [pltpu.VMEM((2 * WIN, hidden), BF16)] * 2,
        ),
        ctx_there,
    )
    g_there = swap(g_out)
    act_far, gp_far, h_far = (flip(factor, 1) for factor in (*far, h_two))
    cot_far = flip(jnp.concatenate([cot0, cot1]), 1)
    (ctx_whole,) = run(
        lambda q: call(
            whole_kernel, "whole", 2.7, [("h", q), ("h", k1), ("h", v1), ("h", ctx_own)],
            [("h", struct((2, rows, width), BF16))],
        ),
        q1,
    )
    half_c, half_e = struct((half // 2, wide), BF16), struct((wide // 2, half), BF16)
    keep_c, send_c, keep_e, send_e = run(
        lambda h_far: call(
            partial(outer_kernel, MASKS_C, MASKS_E), "outer", 3.5,
            [("s", info)]
            + [("v", value) for value in (act, grad_pre, h_two, act_far, gp_far, h_far)]
            + [("v", value) for value in (cot0, cot1, cot_far)],
            [("v", half_c), ("v", half_c), ("v", half_e), ("v", half_e)],
            [pltpu.VMEM((half, wide), BF16)],
        ),
        h_far,
    )
    part_c = Reduction(order, keep_c, send_c, MASKS_C)
    part_e = Reduction(order, keep_e, send_e, MASKS_E)
    ctx_whole_there = swap(order.tie(ctx_whole, g_there))
    grad_resid, grad_mix, dq, dk0, dv0, dk1, dv1, s_back = run(
        lambda there: call(
            back_kernel, "back", 7,
            [("s", info)]
            + [("v", value) for value in (g_here, there, resid, cot0, cot1, packed, ctx)]
            + [("h", value) for value in (mix_weight, q0, k0, v0, q1, k1, v1)],
            [
                ("h", struct((WIN, wide), F32)), ("v", struct((2 * width, width), BF16)),
                ("v", win_heads), ("v", low_heads), ("v", low_heads), ("v", low_heads),
                ("v", low_heads), ("v", struct((8, wide), F32)),
            ],
        ),
        g_there,
    )
    full_part = pltpu.VMEM((2 * wide, width), BF16)
    half_part = [("v", struct((wide, width), BF16))] * 2
    keep_b, send_b = run(
        lambda d: call(
            partial(value_mix_kernel, MASKS_B), "value_mix", 1.5,
            [("s", info), ("h", h0), ("h", h1)] + [("v", value) for value in (d, dv1, grad_mix)],
            half_part, [full_part],
        ),
        dv0,
    )
    part_b = Reduction(order, keep_b, send_b, MASKS_B)
    keep_a, send_a = run(
        lambda d: call(
            partial(query_key_kernel, MASKS_A), "query_key", 1.5,
            [("s", info), ("h", h0), ("h", h1)] + [("v", value) for value in (d, dk0, dk1)],
            half_part, [full_part],
        ),
        dq,
    )
    part_a = Reduction(order, keep_a, send_a, MASKS_A)
    part_c.step()
    part_e.step()
    part_b.step()
    part_a.step()
    own, out, shared, small = run(
        lambda d: call(
            first_kernel, "first", 4,
            [("s", info), ("h", inputs), ("v", other), ("v", packed), ("h", projections)]
            + [("v", value) for value in (d, dk0, dv0, dk1, dv1, s_hidden, s_back)],
            [
                ("h", full_rows), ("v", low_rows), ("v", struct((8, width), F32)),
                ("v", struct((24, width), F32)),
            ],
            [pltpu.VMEM((rows, wide), F32)],
        ),
        dq,
    )
    there = swap(out)
    shared_there = swap(shared)
    part_c.step()
    part_e.step()

    def forward(slot, x):
        return run(
            lambda far: call(
                partial(forward_kernel, slot), "forward", 5,
                [
                    ("h" if slot == 0 else "v", x), ("h", ctx_whole), ("v", far),
                    ("h", mix_weight), ("h", mix_other), ("v", packed), ("h", expand_weight),
                    ("h", contract_weight),
                ],
                [("h", full_rows) if slot == 0 else ("v", low_rows)],
            ),
            ctx_whole_there,
        )[0]

    forward_out = forward(1, other)
    forward_there = swap(forward_out)
    part_a.step()
    part_b.step()
    base = forward(0, inputs)
    part_c.step()
    small = jnp.concatenate([run(jnp.add, shared_there, shared), small])
    part_b.extra = small
    part_a.step()
    part_b.step()
    part_e.step()
    (layer_out,) = run(
        lambda far: call(
            finish_kernel, "finish", 1, [("h", base), ("v", far)], [("h", low_rows)]
        ),
        forward_there,
    )
    part_e.step()
    part_a.step()
    part_c.step()
    part_b.step()
    (input_grad,) = run(
        lambda far: call(
            input_kernel, "input", 3,
            [("s", info), ("h", inputs), ("v", packed), ("h", own), ("v", far), ("h", grad_resid)],
            [("h", full_rows)],
        ),
        there,
    )
    part_a.step()
    part_b.step()

    def assemble(group, masks, shape, along):
        near, far = group.blocks()
        count = 1 << len(masks)
        size = 2 * near.shape[0] // count
        return run(
            lambda far: call(
                partial(assemble_kernel, masks, along), "assemble", 3,
                [("s", info), ("v", near), ("v", far)], [("r", struct(shape, F32))],
                [
                    pltpu.VMEM((count, size, near.shape[1]), F32),
                    pltpu.SemaphoreType.DMA((count,)),
                ],
            ),
            far,
        )[0]

    grad_contract = assemble(part_c, MASKS_C, (hidden, wide), 0)
    grad_expand = assemble(part_e, MASKS_E, (wide, hidden), 1)
    near_a, far_a = part_a.blocks()
    near_b, far_b = part_b.blocks()
    count = 1 << len(MASKS_A)
    size = 4 * near_a.shape[0] // count
    vector = ("v", struct((wide,), F32))
    (
        grad_proj, grad_mix_weight, grad_qv_bias, grad_expand_bias, grad_gain_one, grad_bias_one,
        grad_gain_two, grad_bias_two, grad_mix_bias, grad_contract_bias,
    ) = run(
        lambda far: call(
            partial(assemble_attention_kernel, MASKS_A, MASKS_B), "assemble_attention", 3,
            [("s", info), ("v", near_a), ("v", far_a), ("v", near_b), ("v", far), ("v", part_b.extra)],
            [
                ("r", struct((3 * wide, width), F32)), ("r", struct((width, wide), F32)),
                ("v", struct((2, width), F32)), ("v", struct((hidden,), F32)),
            ]
            + [vector] * 6,
            [pltpu.VMEM((count, size, width), F32), pltpu.SemaphoreType.DMA((count,))],
        ),
        far_b,
    )
    return (
        layer_out, input_grad, grad_gain_one, grad_bias_one, grad_proj.reshape(3, wide, width),
        grad_qv_bias, grad_mix_weight, grad_mix_bias, grad_gain_two, grad_bias_two, grad_expand,
        grad_expand_bias, grad_contract, grad_contract_bias,
    )


def solution(mesh):
    rows = P(("dp", "tensor"), None)
    return jax.shard_map(
        body,
        mesh=mesh,
        in_specs=(
            rows, rows, P("dp"), P("dp"), P(), P(), P(None, None, "tensor"), P(None, "tensor"),
            P("tensor", None), P(), P(), P(), P(None, "tensor"), P("tensor"), P("tensor", None),
            P(),
        ),
        out_specs=(
            rows, rows, P(), P(), P(None, None, "tensor"), P(None, "tensor"), P("tensor", None),
            P(), P(), P(), P(None, "tensor"), P("tensor"), P("tensor", None), P(),
        ),
        check_vma=False,
    )
```

```python
from functools import partial

import jax
import jax.numpy as jnp
from jax import lax
from jax.experimental import pallas as pl
from jax.experimental.pallas import tpu as pltpu
from jax.sharding import PartitionSpec as P

RATE = 4
HEAD = 64
PAIR = 2 * HEAD
EPS = 1e-12
WIN = 144
ALIGN = 16
PREPARE_LIMIT = 56
PARTS = 16
MASKS = dict(c=(2, 4, 8), e=(4, 2, 8), a=(1, 4, 2, 8), b=(1, 2, 4, 8), mix=(1, 2, 0))
F32 = jnp.float32
BF16 = jnp.bfloat16
MIB = 1 << 20
ROOT_HALF = 0.7071067811865476
GAUSS = 0.3989422804014327

TIMES = dict(
    prepare=0.05, own=4, other=0.05, hidden=32, whole=8, outer=1, back=9.8, value_mix=5.6, query_key=8,
    first=2.8, forward=1.225, finish=0.5, input=64, assemble=4, assemble_attention=8,
)
STEPS = (
    "whole", "outer", "back", "c", "vm", "e", "cw", "qk", "b", "c", "first", "a", "fwd1", "e",
    "fwd0", "b", "a", "c", "a", "sm", "b", "e", "finish", "c", "e", "a", "b", "c", "a", "b",
    "input", "e", "asm_c", "b", "a", "asm_e", "asm_ab",
)
PIECES = 1

GAIN1, BIAS1, MIXB, GAIN2, BIAS2, OUTB, QVB, EXPB = range(8)
STARTS, LENGTHS, SIDE, HERE = 0, 2, 4, 5


def mm(a, b):
    return lax.dot_general(a, b, (((1,), (0,)), ((), ())), preferred_element_type=F32)


def mm_right(a, b):
    return lax.dot_general(a, b, (((1,), (1,)), ((), ())), preferred_element_type=F32)


def mm_left(a, b):
    return lax.dot_general(a, b, (((0,), (0,)), ((), ())), preferred_element_type=F32)


def norm(values):
    mean = jnp.mean(values, axis=-1, keepdims=True)
    centred = values - mean
    var = jnp.mean(centred * centred, axis=-1, keepdims=True)
    inverse = lax.rsqrt(var + EPS)
    return centred * inverse, inverse


def norm_back(scaled, normed, inverse):
    inner = jnp.mean(scaled, axis=-1, keepdims=True)
    cross = jnp.mean(scaled * normed, axis=-1, keepdims=True)
    return inverse * (scaled - inner - normed * cross)


class Fetched:
    def __init__(self, source, buffer, sem):
        self.buffer = buffer
        self.copy = pltpu.make_async_copy(source, buffer, sem)
        self.copy.start()

    def get(self):
        if self.copy is not None:
            self.copy.wait()
            self.copy = None
        return self.buffer


class Present:
    def __init__(self, ref):
        self.buffer = ref

    def get(self):
        return self.buffer


class Sent:
    def __init__(self, target, buffer, sem):
        self.buffer = buffer
        self.copy = pltpu.make_async_copy(buffer, target, sem)
        self.started = False

    def send(self):
        if not self.started:
            self.copy.start()
            self.started = True

    def finish(self):
        self.send()
        self.copy.wait()


def call(kernel, name, args, outs, scratch=(), limit=18):
    places = {
        "s": pl.BlockSpec(memory_space=pltpu.SMEM), "v": pl.BlockSpec(memory_space=pltpu.VMEM),
        "p": pl.BlockSpec(memory_space=pltpu.VMEM), "h": pl.BlockSpec(memory_space=pltpu.HBM),
        "r": pl.BlockSpec(memory_space=pltpu.HBM),
    }
    buffers = []
    for place, value in [*args, *outs]:
        if place == "h":
            buffers += [pltpu.VMEM(value.shape, value.dtype), pltpu.SemaphoreType.DMA]

    def whole(*refs):
        moving = list(refs[len(args) + len(outs) : len(args) + len(outs) + len(buffers)])
        given, results = [], []
        for at, (place, _) in enumerate(args):
            ref = refs[at]
            if place == "h":
                ref = Fetched(ref, moving.pop(0), moving.pop(0))
            elif place == "p":
                ref = Present(ref)
            given.append(ref)
        for at, (place, _) in enumerate(outs):
            ref = refs[len(args) + at]
            results.append(Sent(ref, moving.pop(0), moving.pop(0)) if place == "h" else ref)
        kernel(*given, *results, *refs[len(args) + len(outs) + len(buffers) :])
        for value in given:
            if isinstance(value, Fetched):
                value.get()
        for value in results:
            if isinstance(value, Sent):
                value.send()
        for value in results:
            if isinstance(value, Sent):
                value.finish()

    return pl.pallas_call(
        whole,
        out_shape=tuple(value for _, value in outs),
        in_specs=[places[place] for place, _ in args],
        out_specs=tuple(places[place] for place, _ in outs),
        scratch_shapes=buffers + list(scratch),
        compiler_params=pltpu.CompilerParams(vmem_limit_bytes=limit * MIB),
        cost_estimate=pl.CostEstimate(
            flops=int(TIMES[name] * 5e8), bytes_accessed=int(TIMES[name] * 5e5), transcendentals=0
        ),
        name=name,
    )(*(value for _, value in args))


def struct(shape, kind):
    return jax.ShapeDtypeStruct(shape, kind)


def window(info, slot, rows):
    side = info[SIDE]
    first = info[STARTS + (side if slot == 0 else 1 - side)]
    return pl.multiple_of(jnp.minimum(first // (RATE * ALIGN) * ALIGN, rows - WIN), ALIGN)


def project_rows(x, p_ref, w, h, q, k, v):
    rows = x.shape[0]
    width = q.buffer.shape[1]
    gain, bias = p_ref[GAIN1 : GAIN1 + 1], p_ref[BIAS1 : BIAS1 + 1]
    q_bias, v_bias = p_ref[QVB : QVB + 1, :width], p_ref[QVB : QVB + 1, width : 2 * width]
    for at in range(0, rows, 256):
        part = slice(at, at + 256)
        normed, _ = norm(x[part].astype(F32))
        low = (normed * gain + bias).astype(BF16)
        h.buffer[part] = low
        weights = w.get()
        q.buffer[part] = (mm(low, weights[0]) + q_bias).astype(BF16) * BF16(HEAD**-0.5)
        k.buffer[part] = mm(low, weights[1]).astype(BF16)
        v.buffer[part] = (mm(low, weights[2]) + v_bias).astype(BF16)
    for sent in (h, q, k, v):
        sent.send()


def split_heads(values):
    low = lax.broadcasted_iota(jnp.int32, values.shape, 1) < HEAD
    zero = jnp.zeros_like(values)
    return jnp.concatenate([jnp.where(low, values, zero), jnp.where(low, zero, values)], axis=0)


def join_heads(values):
    half = values.shape[0] // 2
    low = lax.broadcasted_iota(jnp.int32, (half, PAIR), 1) < HEAD
    return jnp.where(low, values[:half], values[half:])


def softmax(scores):
    expo = jnp.exp(scores - jnp.max(scores, axis=-1, keepdims=True))
    return expo / jnp.sum(expo, axis=-1, keepdims=True)


def attend(query, key, value):
    probs = softmax(mm_right(split_heads(query), key))
    return join_heads(mm(probs.astype(BF16), value)).astype(BF16)


def attend_window(start, q, k, v, c_ref, slot, log_ref):
    for at in range(0, q.shape[1], PAIR):
        cols = slice(at, at + PAIR)
        scores = mm_right(split_heads(q[pl.ds(start, WIN), cols]), k[:, cols])
        top = jnp.max(scores, axis=-1, keepdims=True)
        expo = jnp.exp(scores - top)
        total = jnp.sum(expo, axis=-1, keepdims=True)
        lane = lax.broadcasted_iota(jnp.int32, log_ref.shape, 1)
        log_ref[...] = jnp.where(lane == at // PAIR, top + jnp.log(total), log_ref[...])
        probs = (expo / total).astype(BF16)
        c_ref[slot, :, cols] = join_heads(mm(probs, v[:, cols])).astype(BF16)


def attend_rows(q, k, v, store):
    for at in range(0, q.shape[1], PAIR):
        cols = slice(at, at + PAIR)
        for row in range(0, q.shape[0], 256):
            part = slice(row, row + 256)
            store(part, cols, attend(q[part, cols], k[:, cols], v[:, cols]))


def prepare_kernel(info, g1, b1, mb, g2, b2, ob, qv, eb, grad, p_ref, cot_ref, piece, sem):
    wide, width = grad.shape[1], qv.shape[1]
    start = window(info, 0, grad.shape[0])
    copy = pltpu.make_async_copy(grad.at[pl.ds(start, WIN)], piece, sem)
    copy.start()
    for at, vector in enumerate((g1, b1, mb, g2, b2, ob)):
        p_ref[at : at + 1] = vector[...].astype(F32).reshape(1, wide)
    p_ref[QVB : QVB + 1, :width] = qv[0:1].astype(F32)
    p_ref[QVB : QVB + 1, width : 2 * width] = qv[1:2].astype(F32)
    long = eb[...].astype(F32)
    for at in range(eb.shape[0] // wide):
        p_ref[EXPB + at : EXPB + at + 1] = long[at * wide : (at + 1) * wide].reshape(1, wide)
    copy.wait()
    side = info[SIDE]
    first = info[STARTS + side]
    last = first + info[LENGTHS + side]
    spot = (start + lax.broadcasted_iota(jnp.int32, piece.shape, 0)) * RATE
    kept = jnp.where((spot < last) & (spot + RATE > first), piece[...].astype(F32), 0.0)
    cot_ref[...] = kept.astype(BF16)


def own_kernel(info, x, p_ref, w, h, q, k, v, c, win_ref, log_ref):
    project_rows(x, p_ref, w, h, q, k, v)

    def store(part, cols, value):
        c.buffer[part, cols] = value

    start = window(info, 0, x.shape[0])
    attend_window(start, q.buffer, k.buffer, v.buffer, win_ref, 0, log_ref.buffer)
    attend_rows(q.buffer, k.buffer, v.buffer, store)


def other_kernel(info, x_ref, p_ref, w, win_ref, h, q, k, v, c_ref, log_ref):
    project_rows(x_ref, p_ref, w, h, q, k, v)
    start = window(info, 1, x_ref.shape[0])
    c_ref[0] = win_ref[0]
    attend_window(start, q.buffer, k.buffer, v.buffer, c_ref, 1, log_ref.buffer)


def whole_kernel(q, k, v, own, c):
    def store(part, cols, value):
        c.buffer[1, part, cols] = value

    c.buffer[0] = own.get()[...]
    attend_rows(q.get(), k.get(), v.get(), store)


def gelu_parts(pre):
    cdf = 0.5 + 0.5 * lax.erf(pre * ROOT_HALF)
    return pre * cdf, cdf


def hidden_kernel(
    masks, info, x0, x1, c_here, c_there, mix_here, mix_near, mix_far, p_ref, we, wc, cots,
    r_ref, h_ref, act_ref, gp_ref, g_ref, gout_ref, gb_ref, act_far, gp_far, mix_there,
    act_full, gp_full,
):
    gain, bias = p_ref[GAIN2 : GAIN2 + 1], p_ref[BIAS2 : BIAS2 + 1]
    wide, hidden = we.buffer.shape
    parts = 1 << (len(masks) - 1)
    size = 2 * mix_near.shape[0] // parts
    for position in range(parts):
        spot = pl.multiple_of(owner(info[HERE], position, masks) * size, ALIGN)
        source, at = (mix_near, position) if position < parts // 2 else (mix_far, position - parts // 2)
        mix_there.buffer[pl.ds(spot, size)] = source[at * size : (at + 1) * size]
    mix_there.send()
    for slot, x in enumerate((x0, x1)):
        rows = x.get() if slot == 0 else x
        start = window(info, slot, rows.shape[0])
        branch = mm(c_here[slot], mix_here.get()[...])
        branch = branch + mm(c_there[1 - slot], mix_there.buffer[...])
        resid = rows[pl.ds(start, WIN)].astype(F32) + branch + p_ref[MIXB : MIXB + 1]
        normed, _ = norm(resid)
        part = slice(slot * WIN, (slot + 1) * WIN)
        r_ref[part] = resid
        h_ref[part] = (normed * gain + bias).astype(BF16)
    h = h_ref[...]
    cot = cots[...]
    total = jnp.zeros(g_ref.shape, F32)
    for at in range(hidden // wide):
        cols = slice(at * wide, (at + 1) * wide)
        up = we.get()[:, cols]
        pre = mm(h, up) + p_ref[EXPB + at : EXPB + at + 1]
        act, cdf = gelu_parts(pre)
        act_full[:, cols] = act.astype(BF16)
        slope = cdf + pre * (jnp.exp(-0.5 * pre * pre) * GAUSS)
        grad_pre = (mm_right(cot, wc.get()[cols]) * slope).astype(BF16)
        gp_full[:, cols] = grad_pre
        gb_ref[:, cols] = jnp.sum(grad_pre.astype(F32), axis=0, keepdims=True)
        total = total + mm_right(grad_pre, up)
    g_ref[...] = total
    gout_ref[...] = total.astype(BF16)
    half = hidden // 2
    core = info[HERE] & 1
    own = pl.ds(pl.multiple_of(core * half, PAIR), half)
    their = pl.ds(pl.multiple_of((1 - core) * half, PAIR), half)
    act_ref[...] = act_full[:, own]
    gp_ref[...] = gp_full[:, own]
    act_far[...] = act_full[:, their]
    gp_far[...] = gp_full[:, their]


def owner(device, position, masks):
    splits = masks[:-1]
    bits = 0
    for mask in splits:
        bits = bits * 2 + (device // mask) % 2
    return bits ^ position


def spread(device, masks, full, keep, send):
    parts = 1 << (len(masks) - 1)
    size = full.shape[0] // parts
    for position in range(parts):
        block = pl.multiple_of(owner(device, position, masks) * size, ALIGN)
        out, at = (keep, position) if position < parts // 2 else (send, position - parts // 2)
        out[at * size : (at + 1) * size] = full[pl.ds(block, size)]


def outer_kernel(
    masks_c, masks_e, info, act, gp, h, act_far, gp_far, h_far, cots, cots_far,
    keep_c, send_c, keep_e, send_e, full,
):
    step = 256

    def product(left, right):
        for at in range(0, full.shape[0], step):
            total = jnp.zeros((step, full.shape[1]), F32)
            for rows, others in zip(left, right):
                total = total + mm_left(rows[:, at : at + step], others)
            full[at : at + step] = total.astype(BF16)

    product((act, act_far), (cots[...], cots_far[...]))
    spread(info[HERE], masks_c, full, keep_c, send_c)
    product((h, h_far), (gp[...], gp_far[...]))
    spread(info[HERE], masks_e, full, keep_e, send_e)


def back_kernel(
    info, g_here, g_there, r_ref, cots, p_ref, c_here, mix, q0, k0, v0, q1, k1, v1, log0, log1,
    gr, gm_ref, dq_ref, dk0, dv0, dk1, dv1, s_ref,
):
    gain = p_ref[GAIN2 : GAIN2 + 1]
    width = mix.buffer.shape[0]
    sums = [jnp.zeros((1, gain.shape[1]), F32) for _ in range(4)]
    low_parts = []
    for slot in range(2):
        part = slice(slot * WIN, (slot + 1) * WIN)
        other = slice((1 - slot) * WIN, (2 - slot) * WIN)
        grad = g_here[part] + g_there[other].astype(F32)
        normed, inverse = norm(r_ref[part])
        cot = cots[part].astype(F32)
        resid = cot + norm_back(grad * gain, normed, inverse)
        if slot == 0:
            gr.buffer[...] = resid
            gr.send()
        low_parts.append(resid.astype(BF16))
        for at, value in enumerate((grad * normed, grad, resid, cot)):
            sums[at] = sums[at] + jnp.sum(value, axis=0, keepdims=True)
    for at in range(4):
        s_ref[at : at + 1] = sums[at]
    s_ref[4:] = jnp.zeros((s_ref.shape[0] - 4, s_ref.shape[1]), F32)
    low = jnp.concatenate(low_parts, axis=0)
    ctx = jnp.concatenate([c_here[0], c_here[1]], axis=0)
    for half in range(2):
        cols = slice(half * width, (half + 1) * width)
        gm_ref[half * width : (half + 1) * width] = mm_left(ctx, low[:, cols]).astype(BF16)
    grad_ctx = mm_right(low, mix.get()[...]).astype(BF16)
    refs = ((q0, k0, v0, log0, dk0, dv0), (q1, k1, v1, log1, dk1, dv1))
    for at in range(0, width, PAIR):
        cols = slice(at, at + PAIR)
        q_sum = jnp.zeros((1, PAIR), F32)
        v_sum = jnp.zeros((1, PAIR), F32)
        for slot, (q, k, v, log, dk, dv) in enumerate(refs):
            q, k, v = q.get(), k.get(), v.get()
            start = window(info, slot, q.shape[0])
            query = split_heads(q[pl.ds(start, WIN), cols])
            grads = split_heads(grad_ctx[slot * WIN : (slot + 1) * WIN, cols])
            key, value = k[:, cols], v[:, cols]
            scores = mm_right(query, key)
            shift = log.get()[:, at // PAIR : at // PAIR + 1]
            probs = jnp.exp(scores - shift)
            slopes = mm_right(grads, value)
            inner = jnp.sum(probs * slopes, axis=-1, keepdims=True)
            grad_scores = (probs * (slopes - inner)).astype(BF16)
            grad_value = mm_left(grads, probs.astype(BF16)).T.astype(BF16)
            dv[:, cols] = grad_value
            dk[:, cols] = mm_left(query, grad_scores).T.astype(BF16)
            grad_query = (join_heads(mm(grad_scores, key)) * HEAD**-0.5).astype(BF16)
            dq_ref[slot, :, cols] = grad_query
            q_sum = q_sum + jnp.sum(grad_query.astype(F32), axis=0, keepdims=True)
            v_sum = v_sum + jnp.sum(grad_value.astype(F32), axis=0, keepdims=True)
        s_ref[4:5, cols] = q_sum
        s_ref[4:5, at + width : at + width + PAIR] = v_sum


def spread_rows(info, masks, full, keep, send):
    spread(info[HERE], masks, full, keep, send)


def query_key_kernel(masks, info, h0, h1, dq, dk0, dk1, keep, send, full):
    h0, h1 = h0.get(), h1.get()
    wide = h0.shape[1]
    starts = [window(info, slot, h0.shape[0]) for slot in range(2)]
    rows = jnp.concatenate([h0[pl.ds(starts[0], WIN)], h1[pl.ds(starts[1], WIN)]], axis=0)
    full[:wide] = mm_left(rows, jnp.concatenate([dq[0], dq[1]], axis=0)).astype(BF16)
    full[wide:] = (mm_left(h0[...], dk0[...]) + mm_left(h1[...], dk1[...])).astype(BF16)
    spread_rows(info, masks, full, keep, send)


def value_mix_kernel(masks, info, h0, h1, dv0, dv1, gm, keep, send, full):
    h0, h1 = h0.get(), h1.get()
    wide = h0.shape[1]
    full[:wide] = (mm_left(h0[...], dv0[...]) + mm_left(h1[...], dv1[...])).astype(BF16)
    full[wide:] = gm[...]
    spread_rows(info, masks, full, keep, send)


def first_kernel(
    info, x0, x1, p_ref, w, dq, dk0, dv0, dk1, dv1, s_hidden, s_back,
    own, out_ref, shared_ref, s_ref, grads,
):
    rows, wide = x1.shape
    gain_sum = jnp.zeros((1, wide), F32)
    bias_sum = jnp.zeros((1, wide), F32)
    for slot, dk, dv in ((1, dk1, dv1), (0, dk0, dv0)):
        weights = w.get()
        kept = own.buffer if slot == 0 else grads
        x = x0.get() if slot == 0 else x1
        start = window(info, slot, rows)
        kept[...] = mm_right(dk[...], weights[1]) + mm_right(dv[...], weights[2])
        kept[pl.ds(start, WIN)] += mm_right(dq[slot], weights[0])
        for at in range(0, rows, 256):
            part = slice(at, at + 256)
            grad = kept[part]
            normed, _ = norm(x[part].astype(F32))
            gain_sum = gain_sum + jnp.sum(grad * normed, axis=0, keepdims=True)
            bias_sum = bias_sum + jnp.sum(grad, axis=0, keepdims=True)
            if slot == 1:
                out_ref[part] = grad.astype(BF16)
    width = shared_ref.shape[1]
    shared_ref[...] = jnp.zeros_like(shared_ref)
    s_ref[...] = jnp.zeros_like(s_ref)
    for half in range(wide // width):
        cols = slice(half * width, (half + 1) * width)
        shared_ref[half : half + 1] = gain_sum[:, cols]
        shared_ref[2 + half : 3 + half] = bias_sum[:, cols]
        for at in range(5):
            s_ref[2 * at + half : 2 * at + half + 1] = s_back[at : at + 1, cols]
    for at in range(s_hidden.shape[1] // width):
        s_ref[10 + at : 11 + at] = s_hidden[:, at * width : (at + 1) * width]


def input_kernel(info, x, p_ref, own, there, gr, out):
    gain = p_ref[GAIN1 : GAIN1 + 1]
    x = x.get()
    rows = x.shape[0]
    for at in range(0, rows, 256):
        part = slice(at, at + 256)
        normed, inverse = norm(x[part].astype(F32))
        grad = own.get()[part] + there[part].astype(F32)
        out.buffer[part] = norm_back(grad * gain, normed, inverse)
    out.buffer[pl.ds(window(info, 0, rows), WIN)] += gr.get()[...]


def forward_kernel(slot, x, c_here, c_there, mix_here, mix_there, p_ref, we, wc, out):
    rows = x.get() if slot == 0 else x
    wide, hidden = we.buffer.shape
    for at in range(0, rows.shape[0], 256):
        part = slice(at, at + 256)
        branch = mm(c_here.get()[slot, part], mix_here.get()[...])
        branch = branch + mm(c_there[1 - slot, part], mix_there.get()[...])
        resid = rows[part].astype(F32) + branch + p_ref[MIXB : MIXB + 1]
        normed, _ = norm(resid)
        h = (normed * p_ref[GAIN2 : GAIN2 + 1] + p_ref[BIAS2 : BIAS2 + 1]).astype(BF16)
        total = jnp.zeros(resid.shape, F32)
        for row in range(hidden // wide):
            cols = slice(row * wide, (row + 1) * wide)
            act, _ = gelu_parts(mm(h, we.get()[:, cols]) + p_ref[EXPB + row : EXPB + row + 1])
            total = total + mm(act.astype(BF16), wc.get()[cols])
        if slot == 0:
            out.buffer[part] = resid + total + p_ref[OUTB : OUTB + 1]
        else:
            out[part] = total.astype(BF16)


def finish_kernel(base, there, out):
    out.buffer[...] = (base.get()[...] + there[...].astype(F32)).astype(BF16)


def pick(position, near, far, size, parts):
    half = parts // 2
    source, at = (near, position) if position < half else (far, position - half)
    return source[at * size : (at + 1) * size].astype(F32)


def assemble_kernel(masks, along, info, near, far, out, made, sems):
    rows, cols = near.shape
    parts = 1 << (len(masks) - 1)
    size = rows // parts
    core = info[HERE] & 1
    copies = []
    for at, (side, source) in enumerate(((core, near), (1 - core, far))):
        for position in range(parts):
            block = owner(info[HERE], position, masks) * size
            if along == 0:
                spot = pl.ds(pl.multiple_of(side * rows + block, ALIGN), size)
            else:
                spot = (
                    pl.ds(pl.multiple_of(block, ALIGN), size),
                    pl.ds(pl.multiple_of(side * cols, PAIR), cols),
                )
            index = at * parts + position
            made[index] = source[position * size : (position + 1) * size].astype(F32)
            copies.append(pltpu.make_async_copy(made.at[index], out.at[spot], sems.at[index]))
            copies[-1].start()
    for copy in copies:
        copy.wait()


def assemble_attention_kernel(
    masks_a, masks_b, info, near_a, far_a, near_b, far_b, extra, proj, mix, qvb, long, *rest
):
    *vectors, made, sems = rest
    size, width = made.shape[1:]
    parts = made.shape[0] // 2
    copies = []
    for position in range(parts):
        block = owner(info[HERE], position, masks_a) * size
        spot = pl.ds(pl.multiple_of(block, ALIGN), size)
        made[position] = pick(position, near_a, far_a, size, parts)
        copies.append(pltpu.make_async_copy(made.at[position], proj.at[spot], sems.at[position]))
        copies[-1].start()
    base = parts * size
    cut = (proj.shape[0] - base) // size
    for position in range(parts):
        index = parts + position
        block = owner(info[HERE], position, masks_b)
        made[index] = pick(position, near_b, far_b, size, parts)

        @pl.when(block < cut)
        def _():
            spot = pl.ds(pl.multiple_of(base + block * size, ALIGN), size)
            pltpu.make_async_copy(made.at[index], proj.at[spot], sems.at[index]).start()

        @pl.when(block >= cut)
        def _():
            left = (block - cut) * size
            half = left // width
            row = pl.multiple_of(left - half * width, ALIGN)
            col = pl.multiple_of(half * width, PAIR)
            spot = (pl.ds(row, size), pl.ds(col, width))
            pltpu.make_async_copy(made.at[index], mix.at[spot], sems.at[index]).start()

        copies.append(
            pltpu.make_async_copy(made.at[index], proj.at[pl.ds(0, size)], sems.at[index])
        )
    rows, more = near_b.shape[0], extra.shape[0]
    total = extra[...] + far_b[rows : rows + more].astype(F32)
    total = total + far_b[rows + more : rows + 2 * more].astype(F32)
    for vector, at in zip(vectors, (0, 2, 8, 10, 12, 14)):
        vector[:width] = total[at].reshape(width)
        vector[width:] = total[at + 1].reshape(width)
    qvb[...] = total[16:18]
    for at in range(long.shape[0] // width):
        long[at * width : (at + 1) * width] = total[18 + at].reshape(width)
    for copy in copies:
        copy.wait()


def flip(value, mask):
    count = lax.axis_size("dp")
    return lax.ppermute(value, "dp", [(at, at ^ mask) for at in range(count)])


def swap(value):
    return lax.ppermute(value, "tensor", [(0, 1), (1, 0)])


def add_low(a, b):
    return (a.astype(F32) + b.astype(F32)).astype(BF16)


class Order:
    def __init__(self):
        self.last = None

    def tie(self, value, *others):
        return lax.optimization_barrier((value,) + others)[0]

    def run(self, step, first, *rest):
        if self.last is not None:
            first = self.tie(first, self.last)
        out = step(first, *rest)
        self.last = out[0] if isinstance(out, tuple) else out
        return out


class Reduction:
    def __init__(self, order, keep, send, masks):
        self.order, self.masks, self.at = order, masks, 0
        self.keep, self.coming = keep, self.flip(send, masks[0])
        self.joins = [*masks[:-1]] if 1 in masks else [1, *masks[:-1]]
        self.extra = None

    def flip(self, value, mask):
        if mask != 1 or PIECES == 1:
            return flip(value, mask)
        size = value.shape[0] // PIECES
        parts = [flip(value[at * size : (at + 1) * size], 1) for at in range(PIECES)]
        return jnp.concatenate(parts)

    def load(self, total, extra):
        if extra is None:
            return total
        high = extra.astype(BF16)
        low = (extra - high.astype(F32)).astype(BF16)
        return jnp.concatenate([total, high, low])

    def take(self, merge):
        def both(coming, held, extra):
            if extra is None:
                total = merge(held, coming)
                return total, total, None
            size, more = held.shape[0], extra.shape[0]
            parts = [coming[size + at * more : size + (at + 1) * more] for at in range(2)]
            extra = extra + parts[0].astype(F32) + parts[1].astype(F32)
            total = merge(held, coming[:size])
            return self.load(total, extra), total, extra

        return self.order.run(both, self.coming, self.total, self.extra)

    def step(self):
        splits = len(self.masks) - 1
        self.at += 1
        if self.at < splits:
            total = self.order.run(add_low, self.coming, self.keep)
            half = total.shape[0] // 2
            self.keep, self.coming = total[:half], self.flip(total[half:], self.masks[self.at])
            return
        if self.at == splits:
            def last(coming, held, extra):
                total = add_low(coming, held)
                return self.load(total, extra), total

            load, self.total = self.order.run(last, self.coming, self.keep, self.extra)
            self.coming = self.flip(load, self.masks[-1])
            return
        if self.at == splits + 1:
            load, self.total, self.extra = self.take(add_low)
            mask = PARTS
            while mask < lax.axis_size("dp"):
                self.total = add_low(self.total, flip(self.total, mask))
                if self.extra is not None:
                    self.extra = self.extra + flip(self.extra, mask)
                load = self.load(self.total, self.extra)
                mask *= 2
        else:
            load, self.total, self.extra = self.take(lambda held, coming: jnp.concatenate([held, coming]))
        self.coming = self.flip(load, self.joins.pop())


def body(
    inputs, out_grad, span_starts, span_lengths, norm1_gain, norm1_bias, projections,
    query_value_bias, mix_weight, mix_bias, norm2_gain, norm2_bias, expand_weight, expand_bias,
    contract_weight, contract_bias,
):
    rows, wide = inputs.shape
    width = projections.shape[2]
    hidden = expand_weight.shape[1]
    side = lax.axis_index("tensor")
    here = lax.axis_index("dp") % PARTS
    info = jnp.concatenate([span_starts, span_lengths, side[None], here[None]])
    order = Order()
    run = order.run

    other = swap(inputs)
    vectors = (
        norm1_gain, norm1_bias, mix_bias, norm2_gain, norm2_bias, contract_bias,
        query_value_bias, expand_bias,
    )
    low_rows = struct((rows, wide), BF16)
    full_rows = struct((rows, wide), F32)
    low_heads = struct((rows, width), BF16)
    wins = struct((2 * WIN, wide), BF16)
    full_wins = struct((2 * WIN, wide), F32)
    win_heads = struct((2, WIN, width), BF16)
    logs = struct((2 * WIN, PAIR), F32)
    projected = [("h", low_rows), ("h", low_heads), ("h", low_heads), ("h", low_heads)]
    mix_size = width >> (len(MASKS["mix"]) - 1)
    mix_near = swap(
        lax.dynamic_slice_in_dim(mix_weight, owner(here, 0, MASKS["mix"]) * mix_size, mix_size)
    )
    packed, cot0 = run(
        lambda grad: call(
            prepare_kernel, "prepare",
            [("s", info)] + [("v", vector) for vector in vectors] + [("r", grad)],
            [("v", struct((EXPB + hidden // wide, wide), F32)), ("v", struct((WIN, wide), BF16))],
            [pltpu.VMEM((WIN, wide), BF16), pltpu.SemaphoreType.DMA], limit=PREPARE_LIMIT,
        ),
        out_grad,
    )
    h0, q0, k0, v0, ctx_own, window_own, log0 = run(
        lambda x: call(
            own_kernel, "own", [("s", info), ("v", x), ("v", packed), ("p", projections)],
            projected + [("h", low_heads), ("v", struct((1, WIN, width), BF16)), ("h", logs)],
        ),
        inputs,
    )
    for mask in MASKS["mix"][1:-1][::-1]:
        mix_near = jnp.concatenate([mix_near, flip(mix_near, mask)])
    mix_far = flip(order.tie(mix_near, window_own), MASKS["mix"][0])
    other = order.tie(other, window_own, mix_near, mix_far)
    cot1 = swap(order.tie(cot0, other))
    h1, q1, k1, v1, ctx, log1 = run(
        lambda x: call(
            other_kernel, "other",
            [("s", info), ("v", x), ("v", packed), ("p", projections), ("v", window_own)],
            projected + [("v", win_heads), ("h", logs)],
        ),
        other,
    )
    ctx_there = swap(ctx)
    cots = run(lambda there, here: jnp.concatenate([here, there]), cot1, cot0)
    cot_far = flip(cots, 1)
    half = hidden // 2
    low_half = struct((2 * WIN, half), BF16)
    resid, h_two, act, grad_pre, g_here, g_out, s_hidden, *far, mix_other = run(
        lambda there: call(
            partial(hidden_kernel, MASKS["mix"]), "hidden",
            [
                ("s", info), ("p", inputs), ("v", other), ("v", ctx), ("v", there),
                ("p", mix_weight), ("v", mix_near), ("v", mix_far), ("v", packed),
                ("p", expand_weight), ("p", contract_weight), ("v", cots),
            ],
            [
                ("v", full_wins), ("v", wins), ("v", low_half), ("v", low_half), ("v", full_wins),
                ("v", wins), ("v", struct((1, hidden), F32)), ("v", low_half), ("v", low_half),
                ("h", struct((width, wide), BF16)),
            ],
            [pltpu.VMEM((2 * WIN, hidden), BF16)] * 2,
        ),
        ctx_there,
    )
    g_there = swap(g_out)
    act_far, gp_far, h_far = (flip(factor, 1) for factor in (*far, h_two))
    values = {}
    groups = {}

    def whole():
        (values["ctx"],) = run(
            lambda q: call(
                whole_kernel, "whole", [("p", q), ("p", k1), ("p", v1), ("p", ctx_own)],
                [("h", struct((2, rows, width), BF16))],
            ),
            q1,
        )

    def outer():
        half_c, half_e = struct((half // 2, wide), BF16), struct((wide // 2, half), BF16)
        keep_c, send_c, keep_e, send_e = run(
            lambda h_far: call(
                partial(outer_kernel, MASKS["c"], MASKS["e"]), "outer",
                [("s", info)]
                + [("v", value) for value in (act, grad_pre, h_two, act_far, gp_far, h_far)]
                + [("v", value) for value in (cots, cot_far)],
                [("v", half_c), ("v", half_c), ("v", half_e), ("v", half_e)],
                [pltpu.VMEM((half, wide), BF16)],
            ),
            h_far,
        )
        groups["c"] = Reduction(order, keep_c, send_c, MASKS["c"])
        groups["e"] = Reduction(order, keep_e, send_e, MASKS["e"])

    def share():
        values["ctx_there"] = swap(order.tie(values["ctx"], g_there))

    def back():
        (
            values["grad_resid"], values["grad_mix"], values["dq"], values["dk0"], values["dv0"],
            values["dk1"], values["dv1"], values["s_back"],
        ) = run(
            lambda there: call(
                back_kernel, "back",
                [("s", info)]
                + [("v", value) for value in (g_here, there, resid, cots, packed, ctx)]
                + [("p", value) for value in (mix_weight, q0, k0, v0, q1, k1, v1, log0, log1)],
                [
                    ("h", struct((WIN, wide), F32)), ("v", struct((2 * width, width), BF16)),
                    ("v", win_heads), ("v", low_heads), ("v", low_heads), ("v", low_heads),
                    ("v", low_heads), ("v", struct((8, wide), F32)),
                ],
            ),
            g_there,
        )

    def gradients(group, kernel, name, *names):
        keep, send = run(
            lambda first: call(
                partial(kernel, MASKS[group]), name,
                [("s", info), ("p", h0), ("p", h1), ("v", first)]
                + [("v", values[name]) for name in names[1:]],
                [("v", struct((wide, width), BF16))] * 2, [pltpu.VMEM((2 * wide, width), BF16)],
            ),
            values[names[0]],
        )
        groups[group] = Reduction(order, keep, send, MASKS[group])

    def first():
        own, out, shared, values["small"] = run(
            lambda dq: call(
                first_kernel, "first",
                [("s", info), ("p", inputs), ("v", other), ("v", packed), ("p", projections)]
                + [("v", dq)] + [("v", values[name]) for name in ("dk0", "dv0", "dk1", "dv1")]
                + [("v", s_hidden), ("v", values["s_back"])],
                [
                    ("h", full_rows), ("v", low_rows), ("v", struct((8, width), F32)),
                    ("v", struct((24, width), F32)),
                ],
                [pltpu.VMEM((rows, wide), F32)],
            ),
            values["dq"],
        )
        values["own"], values["shared"] = own, shared
        values["there"], values["shared_there"] = swap(out), swap(shared)

    def sums():
        def joined(there, here, rest):
            return jnp.concatenate([there + here, rest])

        groups["b"].extra = run(joined, values["shared_there"], values["shared"], values["small"])

    def forward(slot, x):
        return run(
            lambda far: call(
                partial(forward_kernel, slot), "forward",
                [
                    ("p" if slot == 0 else "v", x), ("p", values["ctx"]), ("v", far),
                    ("p", mix_weight), ("p", mix_other), ("v", packed), ("p", expand_weight),
                    ("p", contract_weight),
                ],
                [("h", full_rows) if slot == 0 else ("v", low_rows)],
            ),
            values["ctx_there"],
        )[0]

    def forward_other():
        values["forward"] = swap(forward(1, other))

    def forward_own():
        values["base"] = forward(0, inputs)

    def finish():
        (values["layer_out"],) = run(
            lambda far: call(
                finish_kernel, "finish", [("p", values["base"]), ("v", far)], [("h", low_rows)]
            ),
            values["forward"],
        )

    def backward_end():
        (values["input_grad"],) = run(
            lambda far: call(
                input_kernel, "input",
                [
                    ("s", info), ("p", inputs), ("v", packed), ("p", values["own"]), ("v", far),
                    ("p", values["grad_resid"]),
                ],
                [("h", full_rows)],
            ),
            values["there"],
        )

    def assemble(group, shape, along):
        near, far = groups[group].total, groups[group].coming
        count = 1 << len(MASKS[group])
        size = 2 * near.shape[0] // count
        (values[group],) = run(
            lambda far: call(
                partial(assemble_kernel, MASKS[group], along), "assemble",
                [("s", info), ("v", near), ("v", far)], [("r", struct(shape, F32))],
                [
                    pltpu.VMEM((count, size, near.shape[1]), F32),
                    pltpu.SemaphoreType.DMA((count,)),
                ],
            ),
            far,
        )

    def assemble_attention():
        part_a, part_b = groups["a"], groups["b"]
        count = 1 << len(MASKS["a"])
        size = 4 * part_a.total.shape[0] // count
        values["attention"] = run(
            lambda far: call(
                partial(assemble_attention_kernel, MASKS["a"], MASKS["b"]), "assemble_attention",
                [("s", info), ("v", part_a.total), ("v", part_a.coming), ("v", part_b.total)]
                + [("v", far), ("v", part_b.extra)],
                [
                    ("r", struct((3 * wide, width), F32)), ("r", struct((width, wide), F32)),
                    ("v", struct((2, width), F32)), ("v", struct((hidden,), F32)),
                ]
                + [("v", struct((wide,), F32))] * 6,
                [pltpu.VMEM((count, size, width), F32), pltpu.SemaphoreType.DMA((count,))],
            ),
            part_b.coming,
        )

    steps = dict(
        whole=whole, outer=outer, cw=share, back=back, first=first, sm=sums, fwd1=forward_other,
        vm=lambda: gradients("b", value_mix_kernel, "value_mix", "dv0", "dv1", "grad_mix"),
        qk=lambda: gradients("a", query_key_kernel, "query_key", "dq", "dk0", "dk1"),
        fwd0=forward_own, finish=finish, input=backward_end,
        asm_c=lambda: assemble("c", (hidden, wide), 0),
        asm_e=lambda: assemble("e", (wide, hidden), 1), asm_ab=assemble_attention,
    )
    for name in STEPS:
        if name in steps:
            steps[name]()
        else:
            groups[name].step()
    (
        grad_proj, grad_mix_weight, grad_qv_bias, grad_expand_bias, grad_gain_one, grad_bias_one,
        grad_gain_two, grad_bias_two, grad_mix_bias, grad_contract_bias,
    ) = values["attention"]
    return (
        values["layer_out"], values["input_grad"], grad_gain_one, grad_bias_one,
        grad_proj.reshape(3, wide, width), grad_qv_bias, grad_mix_weight, grad_mix_bias,
        grad_gain_two, grad_bias_two, values["e"], grad_expand_bias, values["c"],
        grad_contract_bias,
    )


def solution(mesh):
    rows = P(("dp", "tensor"), None)
    return jax.shard_map(
        body,
        mesh=mesh,
        in_specs=(
            rows, rows, P("dp"), P("dp"), P(), P(), P(None, None, "tensor"), P(None, "tensor"),
            P("tensor", None), P(), P(), P(), P(None, "tensor"), P("tensor"), P("tensor", None),
            P(),
        ),
        out_specs=(
            rows, rows, P(), P(), P(None, None, "tensor"), P(None, "tensor"), P("tensor", None),
            P(), P(), P(), P(None, "tensor"), P("tensor"), P("tensor", None), P(),
        ),
        check_vma=False,
    )
```

```python
from functools import partial

import jax
import jax.numpy as jnp
from jax import lax
from jax.experimental import pallas as pl
from jax.experimental.pallas import tpu as pltpu
from jax.sharding import PartitionSpec as P

RATE = 4
HEAD = 64
PAIR = 2 * HEAD
EPS = 1e-12
WIN = 144
ALIGN = 16
PREPARE_LIMIT = 56
PARTS = 16
UP, MIDDLE, DOWN = -1, -2, -3
MASKS = dict(c=(4, 2, 8), e=(2, 4, 8), a=(1, 2, 0), b=(1, 4, 2, 8), mix=(1, 2, 0))
F32 = jnp.float32
BF16 = jnp.bfloat16
MIB = 1 << 20
ROOT_HALF = 0.7071067811865476
GAUSS = 0.3989422804014327

TIMES = dict(
    add=32, halve=5.6, join=8, choose=44.8, sums=0.01, prepare=0.05, own=4, other=0.05,
    hidden=2, whole=64, outer=0.49, back=16, value_mix=4, query_key=1.4, first=4, forward=0.49,
    finish=1, input=16, assemble=32, assemble_first=0.5, assemble_last=4,
)
STEPS = (
    "whole", "cw", "outer", "back", "vm", "e", "qk", "c", "b", "e", "a", "c", "b", "a", "fwd0",
    "first", "e", "sm", "c", "b", "a", "c", "e", "fwd1", "b", "a", "input", "b", "c", "a", "e",
    "asm_c", "b", "finish", "a", "asm_e", "asm_a", "asm_b",
)
PIECES = 1

GAIN1, BIAS1, MIXB, GAIN2, BIAS2, OUTB, QVB, EXPB = range(8)
STARTS, LENGTHS, SIDE, HERE = 0, 2, 4, 5


def mm(a, b):
    return lax.dot_general(a, b, (((1,), (0,)), ((), ())), preferred_element_type=F32)


def mm_right(a, b):
    return lax.dot_general(a, b, (((1,), (1,)), ((), ())), preferred_element_type=F32)


def mm_left(a, b):
    return lax.dot_general(a, b, (((0,), (0,)), ((), ())), preferred_element_type=F32)


def norm(values):
    mean = jnp.mean(values, axis=-1, keepdims=True)
    centred = values - mean
    var = jnp.mean(centred * centred, axis=-1, keepdims=True)
    inverse = lax.rsqrt(var + EPS)
    return centred * inverse, inverse


def norm_back(scaled, normed, inverse):
    inner = jnp.mean(scaled, axis=-1, keepdims=True)
    cross = jnp.mean(scaled * normed, axis=-1, keepdims=True)
    return inverse * (scaled - inner - normed * cross)


class Fetched:
    def __init__(self, source, buffer, sem):
        self.buffer = buffer
        self.copy = pltpu.make_async_copy(source, buffer, sem)
        self.copy.start()

    def get(self):
        if self.copy is not None:
            self.copy.wait()
            self.copy = None
        return self.buffer


class Present:
    def __init__(self, ref):
        self.buffer = ref

    def get(self):
        return self.buffer


class Kept:
    def __init__(self, ref):
        self.buffer = ref

    def send(self):
        pass


class Sent:
    def __init__(self, target, buffer, sem):
        self.buffer = buffer
        self.copy = pltpu.make_async_copy(buffer, target, sem)
        self.started = False

    def send(self):
        if not self.started:
            self.copy.start()
            self.started = True

    def finish(self):
        self.send()
        self.copy.wait()


def call(kernel, name, args, outs, scratch=(), limit=18, aliases=()):
    places = {
        "s": pl.BlockSpec(memory_space=pltpu.SMEM), "v": pl.BlockSpec(memory_space=pltpu.VMEM),
        "p": pl.BlockSpec(memory_space=pltpu.VMEM), "h": pl.BlockSpec(memory_space=pltpu.HBM),
        "r": pl.BlockSpec(memory_space=pltpu.HBM),
    }
    buffers = []
    for place, value in [*args, *outs]:
        if place == "h":
            buffers += [pltpu.VMEM(value.shape, value.dtype), pltpu.SemaphoreType.DMA]

    def whole(*refs):
        moving = list(refs[len(args) + len(outs) : len(args) + len(outs) + len(buffers)])
        given, results = [], []
        for at, (place, _) in enumerate(args):
            ref = refs[at]
            if place == "h":
                ref = Fetched(ref, moving.pop(0), moving.pop(0))
            elif place == "p":
                ref = Present(ref)
            given.append(ref)
        for at, (place, _) in enumerate(outs):
            ref = refs[len(args) + at]
            if place == "h":
                ref = Sent(ref, moving.pop(0), moving.pop(0))
            elif place == "p":
                ref = Kept(ref)
            results.append(ref)
        kernel(*given, *results, *refs[len(args) + len(outs) + len(buffers) :])
        for value in given:
            if isinstance(value, Fetched):
                value.get()
        for value in results:
            if isinstance(value, Sent):
                value.send()
        for value in results:
            if isinstance(value, Sent):
                value.finish()

    return pl.pallas_call(
        whole,
        out_shape=tuple(value for _, value in outs),
        in_specs=[places[place] for place, _ in args],
        out_specs=tuple(places[place] for place, _ in outs),
        scratch_shapes=buffers + list(scratch),
        input_output_aliases=dict(aliases),
        compiler_params=pltpu.CompilerParams(vmem_limit_bytes=limit * MIB),
        cost_estimate=pl.CostEstimate(
            flops=int(TIMES[name] * 5e8), bytes_accessed=int(TIMES[name] * 5e5), transcendentals=0
        ),
        name=name,
    )(*(value for _, value in args))


def struct(shape, kind):
    return jax.ShapeDtypeStruct(shape, kind)


def window(info, slot, rows):
    side = info[SIDE]
    first = info[STARTS + (side if slot == 0 else 1 - side)]
    return pl.multiple_of(jnp.minimum(first // (RATE * ALIGN) * ALIGN, rows - WIN), ALIGN)


def project_rows(x, p_ref, w, h, q, k, v):
    rows = x.shape[0]
    width = q.buffer.shape[1]
    gain, bias = p_ref[GAIN1 : GAIN1 + 1], p_ref[BIAS1 : BIAS1 + 1]
    q_bias, v_bias = p_ref[QVB : QVB + 1, :width], p_ref[QVB : QVB + 1, width : 2 * width]
    for at in range(0, rows, 256):
        part = slice(at, at + 256)
        normed, _ = norm(x[part].astype(F32))
        low = (normed * gain + bias).astype(BF16)
        h.buffer[part] = low
        weights = w.get()
        q.buffer[part] = (mm(low, weights[0]) + q_bias).astype(BF16) * BF16(HEAD**-0.5)
        k.buffer[part] = mm(low, weights[1]).astype(BF16)
        v.buffer[part] = (mm(low, weights[2]) + v_bias).astype(BF16)
    for sent in (h, q, k, v):
        sent.send()


def split_heads(values):
    low = lax.broadcasted_iota(jnp.int32, values.shape, 1) < HEAD
    zero = jnp.zeros_like(values)
    return jnp.concatenate([jnp.where(low, values, zero), jnp.where(low, zero, values)], axis=0)


def join_heads(values):
    half = values.shape[0] // 2
    low = lax.broadcasted_iota(jnp.int32, (half, PAIR), 1) < HEAD
    return jnp.where(low, values[:half], values[half:])


def softmax(scores):
    expo = jnp.exp(scores - jnp.max(scores, axis=-1, keepdims=True))
    return expo / jnp.sum(expo, axis=-1, keepdims=True)


def attend(query, key, value):
    probs = softmax(mm_right(split_heads(query), key))
    return join_heads(mm(probs.astype(BF16), value)).astype(BF16)


def attend_window(start, q, k, v, c_ref, slot, log_ref):
    for at in range(0, q.shape[1], PAIR):
        cols = slice(at, at + PAIR)
        scores = mm_right(split_heads(q[pl.ds(start, WIN), cols]), k[:, cols])
        top = jnp.max(scores, axis=-1, keepdims=True)
        expo = jnp.exp(scores - top)
        total = jnp.sum(expo, axis=-1, keepdims=True)
        lane = lax.broadcasted_iota(jnp.int32, log_ref.shape, 1)
        log_ref[...] = jnp.where(lane == at // PAIR, top + jnp.log(total), log_ref[...])
        probs = (expo / total).astype(BF16)
        c_ref[slot, :, cols] = join_heads(mm(probs, v[:, cols])).astype(BF16)


def attend_rows(q, k, v, store):
    for at in range(0, q.shape[1], PAIR):
        cols = slice(at, at + PAIR)
        for row in range(0, q.shape[0], 256):
            part = slice(row, row + 256)
            store(part, cols, attend(q[part, cols], k[:, cols], v[:, cols]))


def prepare_kernel(info, g1, b1, mb, g2, b2, ob, qv, eb, grad, p_ref, cot_ref, piece, sem):
    wide, width = grad.shape[1], qv.shape[1]
    start = window(info, 0, grad.shape[0])
    copy = pltpu.make_async_copy(grad.at[pl.ds(start, WIN)], piece, sem)
    copy.start()
    for at, vector in enumerate((g1, b1, mb, g2, b2, ob)):
        p_ref[at : at + 1] = vector[...].astype(F32).reshape(1, wide)
    p_ref[QVB : QVB + 1, :width] = qv[0:1].astype(F32)
    p_ref[QVB : QVB + 1, width : 2 * width] = qv[1:2].astype(F32)
    long = eb[...].astype(F32)
    for at in range(eb.shape[0] // wide):
        p_ref[EXPB + at : EXPB + at + 1] = long[at * wide : (at + 1) * wide].reshape(1, wide)
    copy.wait()
    side = info[SIDE]
    first = info[STARTS + side]
    last = first + info[LENGTHS + side]
    spot = (start + lax.broadcasted_iota(jnp.int32, piece.shape, 0)) * RATE
    kept = jnp.where((spot < last) & (spot + RATE > first), piece[...].astype(F32), 0.0)
    cot_ref[:WIN] = kept.astype(BF16)
    cot_ref[WIN:] = jnp.zeros((ALIGN, wide), BF16)


def own_kernel(info, x, p_ref, w, h, q, k, v, c, win_ref, log_ref):
    project_rows(x, p_ref, w, h, q, k, v)

    def store(part, cols, value):
        c.buffer[part, cols] = value

    start = window(info, 0, x.shape[0])
    attend_window(start, q.buffer, k.buffer, v.buffer, win_ref, 0, log_ref.buffer)
    attend_rows(q.buffer, k.buffer, v.buffer, store)


def other_kernel(info, x_ref, p_ref, w, win_ref, h, q, k, v, c_ref, log_ref):
    project_rows(x_ref, p_ref, w, h, q, k, v)
    start = window(info, 1, x_ref.shape[0])
    c_ref[0] = win_ref[0]
    attend_window(start, q.buffer, k.buffer, v.buffer, c_ref, 1, log_ref.buffer)


def whole_kernel(q, k, v, own, c):
    def store(part, cols, value):
        c.buffer[1, part, cols] = value

    c.buffer[0] = own.get()[...]
    attend_rows(q.get(), k.get(), v.get(), store)


def gelu_parts(pre):
    cdf = 0.5 + 0.5 * lax.erf(pre * ROOT_HALF)
    return pre * cdf, cdf


def hidden_kernel(
    masks, info, x0, x1, c_here, c_there, mix_here, mix_near, mix_far, p_ref, we, wc, cots,
    r_ref, h_ref, act_ref, gp_ref, g_ref, gout_ref, gb_ref, far_ref, mix_there,
    act_full, gp_full,
):
    gain, bias = p_ref[GAIN2 : GAIN2 + 1], p_ref[BIAS2 : BIAS2 + 1]
    wide, hidden = we.buffer.shape
    parts = 1 << (len(masks) - 1)
    size = 2 * mix_near.shape[0] // parts
    for position in range(parts):
        spot = pl.multiple_of(owner(info[HERE], position, masks) * size, ALIGN)
        source, at = (mix_near, position) if position < parts // 2 else (mix_far, position - parts // 2)
        mix_there.buffer[pl.ds(spot, size)] = source[at * size : (at + 1) * size]
    mix_there.send()
    for slot, x in enumerate((x0, x1)):
        rows = x.get() if slot == 0 else x
        start = window(info, slot, rows.shape[0])
        branch = mm(c_here[slot], mix_here.get()[...])
        branch = branch + mm(c_there[1 - slot], mix_there.buffer[...])
        resid = rows[pl.ds(start, WIN)].astype(F32) + branch + p_ref[MIXB : MIXB + 1]
        normed, _ = norm(resid)
        part = slice(slot * WIN, (slot + 1) * WIN)
        r_ref[part] = resid
        h_ref[part] = (normed * gain + bias).astype(BF16)
    h = h_ref[...]
    cot = cots[...]
    total = jnp.zeros(g_ref.shape, F32)
    for at in range(hidden // wide):
        cols = slice(at * wide, (at + 1) * wide)
        up = we.get()[:, cols]
        pre = mm(h, up) + p_ref[EXPB + at : EXPB + at + 1]
        act, cdf = gelu_parts(pre)
        act_full[:, cols] = act.astype(BF16)
        slope = cdf + pre * (jnp.exp(-0.5 * pre * pre) * GAUSS)
        grad_pre = (mm_right(cot, wc.get()[cols]) * slope).astype(BF16)
        gp_full[:, cols] = grad_pre
        gb_ref[:, cols] = jnp.sum(grad_pre.astype(F32), axis=0, keepdims=True)
        total = total + mm_right(grad_pre, up)
    g_ref[...] = total
    gout_ref[...] = total.astype(BF16)
    half = hidden // 2
    core = info[HERE] & 1
    own = pl.ds(pl.multiple_of(core * half, PAIR), half)
    their = pl.ds(pl.multiple_of((1 - core) * half, PAIR), half)
    act_ref[...] = act_full[:, own]
    gp_ref[...] = gp_full[:, own]
    far_ref[:, :half] = act_full[:, their]
    far_ref[:, half:] = gp_full[:, their]


def owner(device, position, masks):
    splits = masks[:-1]
    bits = 0
    for mask in splits:
        bits = bits * 2 + (device // mask) % 2
    return bits ^ position


def spread(device, masks, full, keep, send):
    parts = 1 << (len(masks) - 1)
    size = full.shape[0] // parts
    for position in range(parts):
        block = pl.multiple_of(owner(device, position, masks) * size, ALIGN)
        out, at = (keep, position) if position < parts // 2 else (send, position - parts // 2)
        out[at * size : (at + 1) * size] = full[pl.ds(block, size)]


def outer_kernel(
    masks_c, masks_e, info, act, gp, h, far, h_far, cots, cots_far,
    keep_c, send_c, keep_e, send_e, full,
):
    step = 256
    half = act.shape[1]

    def product(left, right):
        right = jnp.concatenate(right, axis=0)
        for at in range(0, full.shape[0], step):
            part = slice(at, at + step)
            both = jnp.concatenate([rows(part) for rows in left], axis=0)
            full[part] = mm_left(both, right).astype(BF16)

    product(
        (lambda cols: act[:, cols], lambda cols: far[:, cols]), (cots[...], cots_far[...])
    )
    spread(info[HERE], masks_c, full, keep_c, send_c)
    product(
        (lambda cols: h[:, cols], lambda cols: h_far[:, cols]), (gp[...], far[:, half:])
    )
    spread(info[HERE], masks_e, full, keep_e, send_e)


def back_kernel(
    info, g_here, g_there, r_ref, cots, p_ref, c_here, mix, q0, k0, v0, q1, k1, v1, log0, log1,
    gr, gm_ref, dq_ref, dk0, dv0, dk1, dv1, s_ref,
):
    gain = p_ref[GAIN2 : GAIN2 + 1]
    width = mix.buffer.shape[0]
    sums = [jnp.zeros((1, gain.shape[1]), F32) for _ in range(4)]
    low_parts = []
    for slot in range(2):
        part = slice(slot * WIN, (slot + 1) * WIN)
        other = slice((1 - slot) * WIN, (2 - slot) * WIN)
        grad = g_here[part] + g_there[other].astype(F32)
        normed, inverse = norm(r_ref[part])
        cot = cots[part].astype(F32)
        resid = cot + norm_back(grad * gain, normed, inverse)
        if slot == 0:
            gr.buffer[...] = resid
            gr.send()
        low_parts.append(resid.astype(BF16))
        for at, value in enumerate((grad * normed, grad, resid, cot)):
            sums[at] = sums[at] + jnp.sum(value, axis=0, keepdims=True)
    for at in range(4):
        s_ref[at : at + 1] = sums[at]
    s_ref[4:] = jnp.zeros((s_ref.shape[0] - 4, s_ref.shape[1]), F32)
    low = jnp.concatenate(low_parts, axis=0)
    ctx = jnp.concatenate([c_here[0], c_here[1]], axis=0)
    for half in range(2):
        cols = slice(half * width, (half + 1) * width)
        gm_ref[half * width : (half + 1) * width] = mm_left(ctx, low[:, cols]).astype(BF16)
    grad_ctx = mm_right(low, mix.get()[...]).astype(BF16)
    refs = ((q0, k0, v0, log0, dk0, dv0), (q1, k1, v1, log1, dk1, dv1))
    for at in range(0, width, PAIR):
        cols = slice(at, at + PAIR)
        q_sum = jnp.zeros((1, PAIR), F32)
        v_sum = jnp.zeros((1, PAIR), F32)
        for slot, (q, k, v, log, dk, dv) in enumerate(refs):
            q, k, v = q.get(), k.get(), v.get()
            start = window(info, slot, q.shape[0])
            query = split_heads(q[pl.ds(start, WIN), cols])
            grads = split_heads(grad_ctx[slot * WIN : (slot + 1) * WIN, cols])
            key, value = k[:, cols], v[:, cols]
            scores = mm_right(query, key)
            shift = log.get()[:, at // PAIR : at // PAIR + 1]
            probs = jnp.exp(scores - shift)
            slopes = mm_right(grads, value)
            inner = jnp.sum(probs * slopes, axis=-1, keepdims=True)
            grad_scores = (probs * (slopes - inner)).astype(BF16)
            grad_value = mm_left(grads, probs.astype(BF16)).T.astype(BF16)
            dv[:, cols] = grad_value
            dk[:, cols] = mm_left(query, grad_scores).T.astype(BF16)
            grad_query = (join_heads(mm(grad_scores, key)) * HEAD**-0.5).astype(BF16)
            dq_ref[slot, :, cols] = grad_query
            q_sum = q_sum + jnp.sum(grad_query.astype(F32), axis=0, keepdims=True)
            v_sum = v_sum + jnp.sum(grad_value.astype(F32), axis=0, keepdims=True)
        s_ref[4:5, cols] = q_sum
        s_ref[4:5, at + width : at + width + PAIR] = v_sum


def spread_rows(info, masks, full, keep, send):
    spread(info[HERE], masks, full, keep, send)


def query_key_kernel(masks, info, h0, h1, dq, dk0, dk1, keep, send, full):
    h0, h1 = h0.get(), h1.get()
    wide = h0.shape[1]
    starts = [window(info, slot, h0.shape[0]) for slot in range(2)]
    rows = jnp.concatenate([h0[pl.ds(starts[0], WIN)], h1[pl.ds(starts[1], WIN)]], axis=0)
    full[:wide] = mm_left(rows, jnp.concatenate([dq[0], dq[1]], axis=0)).astype(BF16)
    full[wide:] = (mm_left(h0[...], dk0[...]) + mm_left(h1[...], dk1[...])).astype(BF16)
    spread_rows(info, masks, full, keep, send)


def value_mix_kernel(masks, info, h0, h1, dv0, dv1, gm, keep, send, full):
    h0, h1 = h0.get(), h1.get()
    wide = h0.shape[1]
    full[:wide] = (mm_left(h0[...], dv0[...]) + mm_left(h1[...], dv1[...])).astype(BF16)
    full[wide:] = gm[...]
    spread_rows(info, masks, full, keep, send)


def first_kernel(
    info, x0, x1, p_ref, w, dq, dk0, dv0, dk1, dv1, s_hidden, s_back,
    own, out_ref, shared_ref, s_ref, grads,
):
    rows, wide = x1.shape
    gain_sum = jnp.zeros((1, wide), F32)
    bias_sum = jnp.zeros((1, wide), F32)
    for slot, dk, dv in ((1, dk1, dv1), (0, dk0, dv0)):
        weights = w.get()
        kept = own.buffer if slot == 0 else grads
        x = x0.get() if slot == 0 else x1
        start = window(info, slot, rows)
        kept[...] = mm_right(dk[...], weights[1]) + mm_right(dv[...], weights[2])
        kept[pl.ds(start, WIN)] += mm_right(dq[slot], weights[0])
        for at in range(0, rows, 256):
            part = slice(at, at + 256)
            grad = kept[part]
            normed, _ = norm(x[part].astype(F32))
            gain_sum = gain_sum + jnp.sum(grad * normed, axis=0, keepdims=True)
            bias_sum = bias_sum + jnp.sum(grad, axis=0, keepdims=True)
            if slot == 1:
                out_ref[part] = grad.astype(BF16)
    width = shared_ref.shape[1]
    shared_ref[...] = jnp.zeros_like(shared_ref)
    s_ref[...] = jnp.zeros_like(s_ref)
    for half in range(wide // width):
        cols = slice(half * width, (half + 1) * width)
        shared_ref[half : half + 1] = gain_sum[:, cols]
        shared_ref[2 + half : 3 + half] = bias_sum[:, cols]
        for at in range(5):
            s_ref[2 * at + half : 2 * at + half + 1] = s_back[at : at + 1, cols]
    for at in range(s_hidden.shape[1] // width):
        s_ref[10 + at : 11 + at] = s_hidden[:, at * width : (at + 1) * width]


def input_kernel(info, x, p_ref, own, there, gr, out):
    gain = p_ref[GAIN1 : GAIN1 + 1]
    x = x.get()
    rows = x.shape[0]
    for at in range(0, rows, 256):
        part = slice(at, at + 256)
        normed, inverse = norm(x[part].astype(F32))
        grad = own.get()[part] + there[part].astype(F32)
        out.buffer[part] = norm_back(grad * gain, normed, inverse)
    out.buffer[pl.ds(window(info, 0, rows), WIN)] += gr.get()[...]


def forward_kernel(slot, x, c_here, c_there, mix_here, mix_there, p_ref, we, wc, out):
    rows = x.get() if slot == 0 else x
    wide, hidden = we.buffer.shape
    for at in range(0, rows.shape[0], 256):
        part = slice(at, at + 256)
        branch = mm(c_here.get()[slot, part], mix_here.get()[...])
        branch = branch + mm(c_there[1 - slot, part], mix_there.get()[...])
        resid = rows[part].astype(F32) + branch + p_ref[MIXB : MIXB + 1]
        normed, _ = norm(resid)
        h = (normed * p_ref[GAIN2 : GAIN2 + 1] + p_ref[BIAS2 : BIAS2 + 1]).astype(BF16)
        total = jnp.zeros(resid.shape, F32)
        for row in range(hidden // wide):
            cols = slice(row * wide, (row + 1) * wide)
            act, _ = gelu_parts(mm(h, we.get()[:, cols]) + p_ref[EXPB + row : EXPB + row + 1])
            total = total + mm(act.astype(BF16), wc.get()[cols])
        if slot == 0:
            out.buffer[part] = resid + total + p_ref[OUTB : OUTB + 1]
        else:
            out[part] = total.astype(BF16)


def finish_kernel(base, there, out):
    out.buffer[...] = (base.get()[...] + there[...].astype(F32)).astype(BF16)


def pick(position, near, far, size, parts):
    half = parts // 2
    source, at = (near, position) if position < half else (far, position - half)
    return source[at * size : (at + 1) * size].astype(F32)


def assemble_kernel(masks, along, info, near, far, out, made, sems):
    rows, cols = near.shape
    parts = 1 << (len(masks) - 1)
    size = rows // parts
    core = info[HERE] & 1
    copies = []
    for at, (side, source) in enumerate(((core, near), (1 - core, far))):
        for position in range(parts):
            block = owner(info[HERE], position, masks) * size
            if along == 0:
                spot = pl.ds(pl.multiple_of(side * rows + block, ALIGN), size)
            else:
                spot = (
                    pl.ds(pl.multiple_of(block, ALIGN), size),
                    pl.ds(pl.multiple_of(side * cols, PAIR), cols),
                )
            index = at * parts + position
            made[index] = source[position * size : (position + 1) * size].astype(F32)
            copies.append(pltpu.make_async_copy(made.at[index], out.at[spot], sems.at[index]))
            copies[-1].start()
    for copy in copies:
        copy.wait()


def assemble_first_kernel(masks, info, near, far, proj, made, sems):
    size = made.shape[1]
    copies = []
    for position in range(made.shape[0]):
        spot = pl.ds(pl.multiple_of(owner(info[HERE], position, masks) * size, ALIGN), size)
        made[position] = pick(position, near, far, size, made.shape[0])
        copies.append(pltpu.make_async_copy(made.at[position], proj.at[spot], sems.at[position]))
        copies[-1].start()
    for copy in copies:
        copy.wait()


def assemble_last_kernel(masks, info, near, far, extra, _, proj, mix, qvb, long, *rest):
    *vectors, made, sems = rest
    parts, size, width = made.shape
    base = parts * size
    cut = (proj.shape[0] - base) // size
    copies = []
    for position in range(parts):
        block = owner(info[HERE], position, masks)
        made[position] = pick(position, near, far, size, parts)

        @pl.when(block < cut)
        def _():
            spot = pl.ds(pl.multiple_of(base + block * size, ALIGN), size)
            pltpu.make_async_copy(made.at[position], proj.at[spot], sems.at[position]).start()

        @pl.when(block >= cut)
        def _():
            left = (block - cut) * size
            half = left // width
            row = pl.multiple_of(left - half * width, ALIGN)
            col = pl.multiple_of(half * width, PAIR)
            spot = (pl.ds(row, size), pl.ds(col, width))
            pltpu.make_async_copy(made.at[position], mix.at[spot], sems.at[position]).start()

        copies.append(
            pltpu.make_async_copy(made.at[position], proj.at[pl.ds(0, size)], sems.at[position])
        )
    rows, more = parts * size // 2, extra.shape[0]
    total = extra[...] + far[rows : rows + more].astype(F32)
    total = total + far[rows + more : rows + 2 * more].astype(F32)
    for vector, at in zip(vectors, (0, 2, 8, 10, 12, 14)):
        vector[:width] = total[at].reshape(width)
        vector[width:] = total[at + 1].reshape(width)
    qvb[...] = total[16:18]
    for at in range(long.shape[0] // width):
        long[at * width : (at + 1) * width] = total[18 + at].reshape(width)
    for copy in copies:
        copy.wait()


def halve_kernel(coming, held, keep, send):
    half = keep.shape[0]
    keep[...] = (coming[:half].astype(F32) + held[:half].astype(F32)).astype(BF16)
    send[...] = (coming[half:].astype(F32) + held[half:].astype(F32)).astype(BF16)


def merge_kernel(kind, rows, info, coming, held, *rest):
    load = rest[-2] if len(rest) > 1 else rest[-1]
    if kind == "add":
        load[:rows] = (coming[:rows].astype(F32) + held[:rows].astype(F32)).astype(BF16)
    ends = None
    if kind == "choose":
        spot = info[HERE] // 4
        ends = (spot == 0) | (spot == 3)
        load[:rows] = jnp.where(ends, coming[:rows].astype(F32), held[:rows].astype(F32)).astype(BF16)
    if kind == "join":
        load[:rows] = held[:rows]
        load[rows : 2 * rows] = coming[:rows]
    if len(rest) > 1:
        extra, out = rest[0], rest[-1]
        more = extra.shape[0]
        base = rows * (2 if kind == "join" else 1)
        total = extra[...]
        if coming.shape[0] > rows:
            there = coming[rows : rows + more].astype(F32) + coming[rows + more :].astype(F32)
            total = jnp.where(ends, there, total) if kind == "choose" else total + there
        high = total.astype(BF16)
        load[base : base + more] = high
        load[base + more :] = (total - high.astype(F32)).astype(BF16)
        out[...] = total


def sums_kernel(there, here, small, out):
    size = here.shape[0]
    out[:size] = there[...] + here[...]
    out[size:] = small[...]


def flip(value, mask):
    count = lax.axis_size("dp")
    ends, inner = (0, 3), (1, 2)
    differ, senders = {UP: (4, ends), MIDDLE: (12, inner), DOWN: (4, inner)}.get(
        mask, (mask, (0, 1, 2, 3))
    )
    pairs = [(at, at ^ differ) for at in range(count) if at // 4 % 4 in senders]
    return lax.ppermute(value, "dp", pairs)


def swap(value):
    return lax.ppermute(value, "tensor", [(0, 1), (1, 0)])


def add_low(a, b):
    return (a.astype(F32) + b.astype(F32)).astype(BF16)


def load_extra(total, extra):
    high = extra.astype(BF16)
    return jnp.concatenate([total, high, (extra - high.astype(F32)).astype(BF16)])


class Order:
    def __init__(self):
        self.last = None

    def tie(self, value, *others):
        return lax.optimization_barrier((value,) + others)[0]

    def run(self, step, first, *rest):
        if self.last is not None:
            first = self.tie(first, self.last)
        out = step(first, *rest)
        self.last = out[0] if isinstance(out, tuple) else out
        return out


class Reduction:
    def __init__(self, order, info, keep, send, masks):
        self.order, self.info, self.masks, self.at = order, info, masks, 0
        self.held, self.coming = keep, self.flip(send, masks[0])
        self.rows = keep.shape[0]
        self.joins = [*masks[:-1]] if 1 in masks else [1, *masks[:-1]]
        self.extra = None
        self.line = [UP, MIDDLE, DOWN] if masks[-1] == 0 else [masks[-1]]

    def flip(self, value, mask):
        if mask != 1 or PIECES == 1:
            return flip(value, mask)
        size = value.shape[0] // PIECES
        parts = [flip(value[at * size : (at + 1) * size], 1) for at in range(PIECES)]
        return jnp.concatenate(parts)

    def merge(self, kind):
        rows, width = self.rows * (2 if kind == "join" else 1), self.held.shape[1]
        more = 0 if self.extra is None else 2 * self.extra.shape[0]
        outs = [("v", struct((rows + more, width), BF16))]
        extra = []
        if self.extra is not None:
            extra = [("v", self.extra)]
            outs.append(("v", struct(self.extra.shape, F32)))
        result = self.order.run(
            lambda coming: call(
                partial(merge_kernel, kind, self.rows), kind,
                [("s", self.info), ("v", coming), ("v", self.held)] + extra, outs,
            ),
            self.coming,
        )
        self.rows, self.held = rows, result[0]
        if extra:
            self.extra = result[1]

    def step(self):
        splits = len(self.masks) - 1
        self.at += 1
        if self.at < splits:
            self.rows //= 2
            half = ("v", struct((self.rows, self.held.shape[1]), BF16))
            self.held, send = self.order.run(
                lambda coming: call(
                    halve_kernel, "halve", [("v", coming), ("v", self.held)], [half, half]
                ),
                self.coming,
            )
            self.coming = self.flip(send, self.masks[self.at])
            return
        if self.at == splits:
            self.merge("add")
            self.coming = self.flip(self.held, self.line.pop(0))
            return
        if self.at <= splits + 3 and self.masks[-1] == 0:
            if self.line:
                self.merge("add")
                if self.line == [DOWN]:
                    self.outer()
                self.coming = self.flip(self.held, self.line.pop(0))
                return
            self.merge("choose")
        elif self.at == splits + 1:
            self.merge("add")
            self.outer()
        else:
            self.merge("join")
        self.coming = self.flip(self.held, self.joins.pop())

    def outer(self):
        mask = PARTS
        while mask < lax.axis_size("dp"):
            total = self.held[: self.rows]
            self.held = add_low(total, flip(total, mask))
            if self.extra is not None:
                self.extra = self.extra + flip(self.extra, mask)
                self.held = load_extra(self.held, self.extra)
            mask *= 2


def body(
    inputs, out_grad, span_starts, span_lengths, norm1_gain, norm1_bias, projections,
    query_value_bias, mix_weight, mix_bias, norm2_gain, norm2_bias, expand_weight, expand_bias,
    contract_weight, contract_bias,
):
    rows, wide = inputs.shape
    width = projections.shape[2]
    hidden = expand_weight.shape[1]
    side = lax.axis_index("tensor")
    here = lax.axis_index("dp") % PARTS
    info = jnp.concatenate([span_starts, span_lengths, side[None], here[None]])
    order = Order()
    run = order.run

    other = swap(inputs)
    vectors = (
        norm1_gain, norm1_bias, mix_bias, norm2_gain, norm2_bias, contract_bias,
        query_value_bias, expand_bias,
    )
    low_rows = struct((rows, wide), BF16)
    full_rows = struct((rows, wide), F32)
    low_heads = struct((rows, width), BF16)
    wins = struct((2 * WIN, wide), BF16)
    full_wins = struct((2 * WIN, wide), F32)
    win_heads = struct((2, WIN, width), BF16)
    logs = struct((2 * WIN, PAIR), F32)
    projected = [("h", low_rows), ("h", low_heads), ("h", low_heads), ("h", low_heads)]
    mix_size = width >> (len(MASKS["mix"]) - 1)
    mix_near = swap(
        lax.dynamic_slice_in_dim(mix_weight, owner(here, 0, MASKS["mix"]) * mix_size, mix_size)
    )
    packed, cot0 = run(
        lambda grad: call(
            prepare_kernel, "prepare",
            [("s", info)] + [("v", vector) for vector in vectors] + [("r", grad)],
            [("v", struct((EXPB + hidden // wide, wide), F32)), ("v", struct((WIN + ALIGN, wide), BF16))],
            [pltpu.VMEM((WIN, wide), BF16), pltpu.SemaphoreType.DMA], limit=PREPARE_LIMIT,
        ),
        out_grad,
    )
    h0, q0, k0, v0, ctx_own, window_own, log0 = run(
        lambda x: call(
            own_kernel, "own", [("s", info), ("v", x), ("v", packed), ("p", projections)],
            projected + [("h", low_heads), ("v", struct((1, WIN, width), BF16)), ("h", logs)],
        ),
        inputs,
    )
    for mask in MASKS["mix"][1:-1][::-1]:
        mix_near = jnp.concatenate([mix_near, flip(mix_near, mask)])
    mix_far = flip(order.tie(mix_near, window_own), MASKS["mix"][0])
    other = order.tie(other, window_own, mix_near, mix_far)
    cot1 = swap(order.tie(cot0, window_own))
    h1, q1, k1, v1, ctx, log1 = run(
        lambda x: call(
            other_kernel, "other",
            [("s", info), ("v", x), ("v", packed), ("p", projections), ("v", window_own)],
            [("p", value) for _, value in projected] + [("v", win_heads), ("h", logs)],
        ),
        other,
    )
    ctx_there = swap(ctx)
    cots = run(lambda there, here: jnp.concatenate([here[:WIN], there[:WIN]]), cot1, cot0)
    cot_far = flip(cots, 1)
    half = hidden // 2
    low_half = struct((2 * WIN, half), BF16)
    resid, h_two, act, grad_pre, g_here, g_out, s_hidden, factors, mix_other = run(
        lambda there: call(
            partial(hidden_kernel, MASKS["mix"]), "hidden",
            [
                ("s", info), ("p", inputs), ("v", other), ("v", ctx), ("v", there),
                ("p", mix_weight), ("v", mix_near), ("v", mix_far), ("v", packed),
                ("p", expand_weight), ("p", contract_weight), ("v", cots),
            ],
            [
                ("v", full_wins), ("v", wins), ("v", low_half), ("v", low_half), ("v", full_wins),
                ("v", wins), ("v", struct((1, hidden), F32)), ("v", struct((2 * WIN, hidden), BF16)),
                ("h", struct((width, wide), BF16)),
            ],
            [pltpu.VMEM((2 * WIN, hidden), BF16)] * 2,
        ),
        ctx_there,
    )
    g_there = swap(g_out)
    far, h_far = flip(factors, 1), flip(h_two, 1)
    values = {}
    groups = {}

    def whole():
        (values["ctx"],) = run(
            lambda q: call(
                whole_kernel, "whole", [("p", q), ("p", k1), ("p", v1), ("p", ctx_own)],
                [("h", struct((2, rows, width), BF16))],
            ),
            q1,
        )

    def outer():
        half_c, half_e = struct((half // 2, wide), BF16), struct((wide // 2, half), BF16)
        keep_c, send_c, keep_e, send_e = run(
            lambda h_far: call(
                partial(outer_kernel, MASKS["c"], MASKS["e"]), "outer",
                [("s", info)]
                + [("v", value) for value in (act, grad_pre, h_two, far, h_far)]
                + [("v", value) for value in (cots, cot_far)],
                [("v", half_c), ("v", half_c), ("v", half_e), ("v", half_e)],
                [pltpu.VMEM((half, wide), BF16)],
            ),
            h_far,
        )
        groups["c"] = Reduction(order, info, keep_c, send_c, MASKS["c"])
        groups["e"] = Reduction(order, info, keep_e, send_e, MASKS["e"])

    def share():
        values["ctx_there"] = swap(order.tie(values["ctx"], order.last))

    def back():
        (
            values["grad_resid"], values["grad_mix"], values["dq"], values["dk0"], values["dv0"],
            values["dk1"], values["dv1"], values["s_back"],
        ) = run(
            lambda there: call(
                back_kernel, "back",
                [("s", info)]
                + [("v", value) for value in (g_here, there, resid, cots, packed, ctx)]
                + [("p", value) for value in (mix_weight, q0, k0, v0, q1, k1, v1, log0, log1)],
                [
                    ("h", struct((WIN, wide), F32)), ("v", struct((2 * width, width), BF16)),
                    ("v", win_heads), ("v", low_heads), ("v", low_heads), ("v", low_heads),
                    ("v", low_heads), ("v", struct((8, wide), F32)),
                ],
            ),
            g_there,
        )

    def gradients(group, kernel, name, *names):
        keep, send = run(
            lambda first: call(
                partial(kernel, MASKS[group]), name,
                [("s", info), ("p", h0), ("p", h1), ("v", first)]
                + [("v", values[name]) for name in names[1:]],
                [("v", struct((wide, width), BF16))] * 2, [pltpu.VMEM((2 * wide, width), BF16)],
            ),
            values[names[0]],
        )
        groups[group] = Reduction(order, info, keep, send, MASKS[group])

    def first():
        own, out, shared, values["small"] = run(
            lambda dq: call(
                first_kernel, "first",
                [("s", info), ("p", inputs), ("v", other), ("v", packed), ("p", projections)]
                + [("v", dq)] + [("v", values[name]) for name in ("dk0", "dv0", "dk1", "dv1")]
                + [("v", s_hidden), ("v", values["s_back"])],
                [
                    ("h", full_rows), ("v", low_rows), ("v", struct((8, width), F32)),
                    ("v", struct((24, width), F32)),
                ],
                [pltpu.VMEM((rows, wide), F32)],
            ),
            values["dq"],
        )
        values["own"], values["shared"] = own, shared
        values["there"], values["shared_there"] = swap(out), swap(shared)

    def sums():
        here, small = values["shared"], values["small"]
        (groups["b"].extra,) = run(
            lambda there: call(
                sums_kernel, "sums", [("v", there), ("v", here), ("v", small)],
                [("v", struct((here.shape[0] + small.shape[0], width), F32))],
            ),
            values["shared_there"],
        )

    def forward(slot, x):
        return run(
            lambda far: call(
                partial(forward_kernel, slot), "forward",
                [
                    ("p" if slot == 0 else "v", x), ("p", values["ctx"]), ("v", far),
                    ("p", mix_weight), ("p", mix_other), ("v", packed), ("p", expand_weight),
                    ("p", contract_weight),
                ],
                [("h", full_rows) if slot == 0 else ("v", low_rows)],
            ),
            values["ctx_there"],
        )[0]

    def forward_other():
        values["forward"] = swap(forward(1, other))

    def forward_own():
        values["base"] = forward(0, inputs)

    def finish():
        (values["layer_out"],) = run(
            lambda far: call(
                finish_kernel, "finish", [("p", values["base"]), ("v", far)], [("h", low_rows)]
            ),
            values["forward"],
        )

    def backward_end():
        (values["input_grad"],) = run(
            lambda far: call(
                input_kernel, "input",
                [
                    ("s", info), ("p", inputs), ("v", packed), ("p", values["own"]), ("v", far),
                    ("p", values["grad_resid"]),
                ],
                [("h", full_rows)],
            ),
            values["there"],
        )

    def assemble(group, shape, along):
        near, far = groups[group].held, groups[group].coming
        count = 1 << len(MASKS[group])
        size = 2 * near.shape[0] // count
        (values[group],) = run(
            lambda far: call(
                partial(assemble_kernel, MASKS[group], along), "assemble",
                [("s", info), ("v", near), ("v", far)], [("r", struct(shape, F32))],
                [
                    pltpu.VMEM((count, size, near.shape[1]), F32),
                    pltpu.SemaphoreType.DMA((count,)),
                ],
            ),
            far,
        )

    def made(group):
        count = 1 << len(MASKS[group][:-1])
        size = 2 * groups[group].rows // count
        return [pltpu.VMEM((count, size, width), F32), pltpu.SemaphoreType.DMA((count,))]

    def assemble_first():
        part = groups["a"]
        (values["proj"],) = run(
            lambda far: call(
                partial(assemble_first_kernel, MASKS["a"]), "assemble_first",
                [("s", info), ("v", part.held), ("v", far)],
                [("r", struct((3 * wide, width), F32))], made("a"),
            ),
            part.coming,
        )

    def assemble_last():
        part = groups["b"]
        values["attention"] = run(
            lambda far: call(
                partial(assemble_last_kernel, MASKS["b"]), "assemble_last",
                [("s", info), ("v", part.held), ("v", far), ("v", part.extra), ("r", values["proj"])],
                [
                    ("r", struct((3 * wide, width), F32)), ("r", struct((width, wide), F32)),
                    ("v", struct((2, width), F32)), ("v", struct((hidden,), F32)),
                ]
                + [("v", struct((wide,), F32))] * 6,
                made("b"), aliases={4: 0},
            ),
            part.coming,
        )

    steps = dict(
        whole=whole, outer=outer, cw=share, back=back, first=first, sm=sums, fwd1=forward_other,
        vm=lambda: gradients("b", value_mix_kernel, "value_mix", "dv0", "dv1", "grad_mix"),
        qk=lambda: gradients("a", query_key_kernel, "query_key", "dq", "dk0", "dk1"),
        fwd0=forward_own, finish=finish, input=backward_end,
        asm_c=lambda: assemble("c", (hidden, wide), 0),
        asm_e=lambda: assemble("e", (wide, hidden), 1), asm_a=assemble_first,
        asm_b=assemble_last,
    )
    for name in STEPS:
        if name in steps:
            steps[name]()
        else:
            groups[name].step()
    (
        grad_proj, grad_mix_weight, grad_qv_bias, grad_expand_bias, grad_gain_one, grad_bias_one,
        grad_gain_two, grad_bias_two, grad_mix_bias, grad_contract_bias,
    ) = values["attention"]
    return (
        values["layer_out"], values["input_grad"], grad_gain_one, grad_bias_one,
        grad_proj.reshape(3, wide, width), grad_qv_bias, grad_mix_weight, grad_mix_bias,
        grad_gain_two, grad_bias_two, values["e"], grad_expand_bias, values["c"],
        grad_contract_bias,
    )


def solution(mesh):
    rows = P(("dp", "tensor"), None)
    return jax.shard_map(
        body,
        mesh=mesh,
        in_specs=(
            rows, rows, P("dp"), P("dp"), P(), P(), P(None, None, "tensor"), P(None, "tensor"),
            P("tensor", None), P(), P(), P(), P(None, "tensor"), P("tensor"), P("tensor", None),
            P(),
        ),
        out_specs=(
            rows, rows, P(), P(), P(None, None, "tensor"), P(None, "tensor"), P("tensor", None),
            P(), P(), P(), P(None, "tensor"), P("tensor"), P("tensor", None), P(),
        ),
        check_vma=False,
    )
```

```python
from functools import partial

import jax
import jax.numpy as jnp
from jax import lax
from jax.experimental import pallas as pl
from jax.experimental.pallas import tpu as pltpu
from jax.sharding import PartitionSpec as P

RATE = 4
HEAD = 64
PAIR = 2 * HEAD
EPS = 1e-12
WIN = 144
ALIGN = 16
PREPARE_LIMIT = 56
PARTS = 16
UP, MIDDLE, DOWN = -1, -2, -3
MASKS = dict(c=(4, 2, 8), e=(2, 4, 8), a=(1, 2, 0), b=(1, 4, 2, 8), mix=(1, 2, 0))
F32 = jnp.float32
BF16 = jnp.bfloat16
MIB = 1 << 20
ROOT_HALF = 0.7071067811865476
GAUSS = 0.3989422804014327

TIMES = dict(
    add=3.92, halve=0.49, join=22.4, choose=44.8, sums=2.8, prepare=0.05, own=4, other=0.05,
    hidden=16, whole=57.85, outer=5.6, back=22.4, value_mix=0.014, query_key=0.112, first=32,
    forward=8, finish=32, input=7.84, assemble=44.8, assemble_first=8, assemble_last=5.6,
)
STEPS = (
    "whole", "outer", "back", "qk", "vm", "cw", "e", "c", "a", "b", "e", "a", "first", "c",
    "sm", "b", "e", "fwd0", "a", "c", "b", "a", "e", "c", "fwd1", "b", "input", "e", "a", "b",
    "c", "asm_e", "a", "asm_c", "b", "asm_a", "finish", "asm_b",
)
PIECES = 1

GAIN1, BIAS1, MIXB, GAIN2, BIAS2, OUTB, QVB, EXPB = range(8)
STARTS, LENGTHS, SIDE = 0, 2, 4


def mm(a, b):
    return lax.dot_general(a, b, (((1,), (0,)), ((), ())), preferred_element_type=F32)


def mm_right(a, b):
    return lax.dot_general(a, b, (((1,), (1,)), ((), ())), preferred_element_type=F32)


def mm_left(a, b):
    return lax.dot_general(a, b, (((0,), (0,)), ((), ())), preferred_element_type=F32)


def norm(values):
    mean = jnp.mean(values, axis=-1, keepdims=True)
    centred = values - mean
    var = jnp.mean(centred * centred, axis=-1, keepdims=True)
    inverse = lax.rsqrt(var + EPS)
    return centred * inverse, inverse


def norm_back(scaled, normed, inverse):
    inner = jnp.mean(scaled, axis=-1, keepdims=True)
    cross = jnp.mean(scaled * normed, axis=-1, keepdims=True)
    return inverse * (scaled - inner - normed * cross)


class Fetched:
    def __init__(self, source, buffer, sem):
        self.buffer = buffer
        self.copy = pltpu.make_async_copy(source, buffer, sem)
        self.copy.start()

    def get(self):
        if self.copy is not None:
            self.copy.wait()
            self.copy = None
        return self.buffer


class Present:
    def __init__(self, ref):
        self.buffer = ref

    def get(self):
        return self.buffer


class Kept:
    def __init__(self, ref):
        self.buffer = ref

    def send(self):
        pass


class Sent:
    def __init__(self, target, buffer, sem):
        self.buffer = buffer
        self.copy = pltpu.make_async_copy(buffer, target, sem)
        self.started = False

    def send(self):
        if not self.started:
            self.copy.start()
            self.started = True

    def finish(self):
        self.send()
        self.copy.wait()


def call(kernel, name, args, outs, scratch=(), limit=18, aliases=()):
    places = {
        "s": pl.BlockSpec(memory_space=pltpu.SMEM), "v": pl.BlockSpec(memory_space=pltpu.VMEM),
        "p": pl.BlockSpec(memory_space=pltpu.VMEM), "h": pl.BlockSpec(memory_space=pltpu.HBM),
        "r": pl.BlockSpec(memory_space=pltpu.HBM),
    }
    buffers = []
    for place, value in [*args, *outs]:
        if place == "h":
            buffers += [pltpu.VMEM(value.shape, value.dtype), pltpu.SemaphoreType.DMA]

    def whole(*refs):
        moving = list(refs[len(args) + len(outs) : len(args) + len(outs) + len(buffers)])
        given, results = [], []
        for at, (place, _) in enumerate(args):
            ref = refs[at]
            if place == "h":
                ref = Fetched(ref, moving.pop(0), moving.pop(0))
            elif place == "p":
                ref = Present(ref)
            given.append(ref)
        for at, (place, _) in enumerate(outs):
            ref = refs[len(args) + at]
            if place == "h":
                ref = Sent(ref, moving.pop(0), moving.pop(0))
            elif place == "p":
                ref = Kept(ref)
            results.append(ref)
        kernel(*given, *results, *refs[len(args) + len(outs) + len(buffers) :])
        for value in given:
            if isinstance(value, Fetched):
                value.get()
        for value in results:
            if isinstance(value, Sent):
                value.send()
        for value in results:
            if isinstance(value, Sent):
                value.finish()

    return pl.pallas_call(
        whole,
        out_shape=tuple(value for _, value in outs),
        in_specs=[places[place] for place, _ in args],
        out_specs=tuple(places[place] for place, _ in outs),
        scratch_shapes=buffers + list(scratch),
        input_output_aliases=dict(aliases),
        compiler_params=pltpu.CompilerParams(vmem_limit_bytes=limit * MIB),
        cost_estimate=pl.CostEstimate(
            flops=int(TIMES[name] * 5e8), bytes_accessed=int(TIMES[name] * 5e5), transcendentals=0
        ),
        name=name,
    )(*(value for _, value in args))


def struct(shape, kind):
    return jax.ShapeDtypeStruct(shape, kind)


def position_here():
    return lax.rem(lax.axis_index("dp"), PARTS)


def window(spots, slot):
    return pl.multiple_of(spots[slot, 0], ALIGN)


def project_rows(x, p_ref, w, h, q, k, v):
    rows = x.shape[0]
    width = q.buffer.shape[1]
    gain, bias = p_ref[GAIN1 : GAIN1 + 1], p_ref[BIAS1 : BIAS1 + 1]
    q_bias, v_bias = p_ref[QVB : QVB + 1, :width], p_ref[QVB : QVB + 1, width : 2 * width]
    for at in range(0, rows, 256):
        part = slice(at, at + 256)
        normed, _ = norm(x[part].astype(F32))
        low = (normed * gain + bias).astype(BF16)
        h.buffer[part] = low
        weights = w.get()
        q.buffer[part] = (mm(low, weights[0]) + q_bias).astype(BF16) * BF16(HEAD**-0.5)
        k.buffer[part] = mm(low, weights[1]).astype(BF16)
        v.buffer[part] = (mm(low, weights[2]) + v_bias).astype(BF16)
    for sent in (h, q, k, v):
        sent.send()


def split_heads(values):
    low = lax.broadcasted_iota(jnp.int32, values.shape, 1) < HEAD
    zero = jnp.zeros_like(values)
    return jnp.concatenate([jnp.where(low, values, zero), jnp.where(low, zero, values)], axis=0)


def join_heads(values):
    half = values.shape[0] // 2
    low = lax.broadcasted_iota(jnp.int32, (half, PAIR), 1) < HEAD
    return jnp.where(low, values[:half], values[half:])


def softmax(scores):
    expo = jnp.exp(scores - jnp.max(scores, axis=-1, keepdims=True))
    return expo / jnp.sum(expo, axis=-1, keepdims=True)


def attend(query, key, value):
    probs = softmax(mm_right(split_heads(query), key))
    return join_heads(mm(probs.astype(BF16), value)).astype(BF16)


def attend_window(start, q, k, v, c_ref, slot, log_ref):
    for at in range(0, q.shape[1], PAIR):
        cols = slice(at, at + PAIR)
        scores = mm_right(split_heads(q[pl.ds(start, WIN), cols]), k[:, cols])
        top = jnp.max(scores, axis=-1, keepdims=True)
        expo = jnp.exp(scores - top)
        total = jnp.sum(expo, axis=-1, keepdims=True)
        lane = lax.broadcasted_iota(jnp.int32, log_ref.shape, 1)
        log_ref[...] = jnp.where(lane == at // PAIR, top + jnp.log(total), log_ref[...])
        probs = (expo / total).astype(BF16)
        c_ref[slot, :, cols] = join_heads(mm(probs, v[:, cols])).astype(BF16)


def attend_rows(q, k, v, store):
    for at in range(0, q.shape[1], PAIR):
        cols = slice(at, at + PAIR)
        for row in range(0, q.shape[0], 256):
            part = slice(row, row + 256)
            store(part, cols, attend(q[part, cols], k[:, cols], v[:, cols]))


def prepare_kernel(info, g1, b1, mb, g2, b2, ob, qv, eb, grad, p_ref, cot_ref, spots, piece, sem):
    wide, width = grad.shape[1], qv.shape[1]
    side = info[SIDE]
    starts = []
    for first in (info[STARTS + side], info[STARTS + 1 - side]):
        start = first // (RATE * ALIGN) * ALIGN
        starts.append(pl.multiple_of(jnp.minimum(start, grad.shape[0] - WIN), ALIGN))
    row = lax.broadcasted_iota(jnp.int32, spots.shape, 0)
    spots[...] = jnp.where(row == 0, starts[0], starts[1])
    start = starts[0]
    copy = pltpu.make_async_copy(grad.at[pl.ds(start, WIN)], piece, sem)
    copy.start()
    for at, vector in enumerate((g1, b1, mb, g2, b2, ob)):
        p_ref[at : at + 1] = vector[...].astype(F32).reshape(1, wide)
    p_ref[QVB : QVB + 1, :width] = qv[0:1].astype(F32)
    p_ref[QVB : QVB + 1, width : 2 * width] = qv[1:2].astype(F32)
    long = eb[...].astype(F32)
    for at in range(eb.shape[0] // wide):
        p_ref[EXPB + at : EXPB + at + 1] = long[at * wide : (at + 1) * wide].reshape(1, wide)
    copy.wait()
    first = info[STARTS + side]
    last = first + info[LENGTHS + side]
    spot = (start + lax.broadcasted_iota(jnp.int32, piece.shape, 0)) * RATE
    kept = jnp.where((spot < last) & (spot + RATE > first), piece[...].astype(F32), 0.0)
    cot_ref[:WIN] = kept.astype(BF16)
    cot_ref[WIN:] = jnp.zeros((ALIGN, wide), BF16)


def own_kernel(spots, x, p_ref, w, h, q, k, v, c, win_ref, log_ref):
    project_rows(x, p_ref, w, h, q, k, v)

    def store(part, cols, value):
        c.buffer[part, cols] = value

    start = window(spots, 0)
    attend_window(start, q.buffer, k.buffer, v.buffer, win_ref, 0, log_ref.buffer)
    attend_rows(q.buffer, k.buffer, v.buffer, store)


def other_kernel(spots, x_ref, p_ref, w, win_ref, h, q, k, v, c_ref, log_ref):
    project_rows(x_ref, p_ref, w, h, q, k, v)
    start = window(spots, 1)
    c_ref[0] = win_ref[0]
    attend_window(start, q.buffer, k.buffer, v.buffer, c_ref, 1, log_ref.buffer)


def whole_kernel(q, k, v, own, c):
    def store(part, cols, value):
        c.buffer[1, part, cols] = value

    c.buffer[0] = own.get()[...]
    attend_rows(q.get(), k.get(), v.get(), store)


def gelu_parts(pre):
    cdf = 0.5 + 0.5 * lax.erf(pre * ROOT_HALF)
    return pre * cdf, cdf


def hidden_kernel(
    masks, spots, x0, x1, c_here, c_there, mix_here, mix_near, mix_far, p_ref, we, wc, cots,
    r_ref, h_ref, act_ref, gp_ref, g_ref, gout_ref, gb_ref, far_ref, mix_there,
    act_full, gp_full,
):
    gain, bias = p_ref[GAIN2 : GAIN2 + 1], p_ref[BIAS2 : BIAS2 + 1]
    wide, hidden = we.buffer.shape
    parts = 1 << (len(masks) - 1)
    size = 2 * mix_near.shape[0] // parts
    for position in range(parts):
        spot = pl.multiple_of(owner(position_here(), position, masks) * size, ALIGN)
        source, at = (mix_near, position) if position < parts // 2 else (mix_far, position - parts // 2)
        mix_there.buffer[pl.ds(spot, size)] = source[at * size : (at + 1) * size]
    mix_there.send()
    for slot, x in enumerate((x0, x1)):
        rows = x.get() if slot == 0 else x
        start = window(spots, slot)
        branch = mm(c_here[slot], mix_here.get()[...])
        branch = branch + mm(c_there[1 - slot], mix_there.buffer[...])
        resid = rows[pl.ds(start, WIN)].astype(F32) + branch + p_ref[MIXB : MIXB + 1]
        normed, _ = norm(resid)
        part = slice(slot * WIN, (slot + 1) * WIN)
        r_ref[part] = resid
        h_ref[part] = (normed * gain + bias).astype(BF16)
    h = h_ref[...]
    cot = cots[...]
    total = jnp.zeros(g_ref.shape, F32)
    for at in range(hidden // wide):
        cols = slice(at * wide, (at + 1) * wide)
        up = we.get()[:, cols]
        pre = mm(h, up) + p_ref[EXPB + at : EXPB + at + 1]
        act, cdf = gelu_parts(pre)
        act_full[:, cols] = act.astype(BF16)
        slope = cdf + pre * (jnp.exp(-0.5 * pre * pre) * GAUSS)
        grad_pre = (mm_right(cot, wc.get()[cols]) * slope).astype(BF16)
        gp_full[:, cols] = grad_pre
        gb_ref[:, cols] = jnp.sum(grad_pre.astype(F32), axis=0, keepdims=True)
        total = total + mm_right(grad_pre, up)
    g_ref[...] = total
    gout_ref[...] = total.astype(BF16)
    half = hidden // 2
    core = lax.rem(position_here(), 2)
    own = pl.ds(pl.multiple_of(core * half, PAIR), half)
    their = pl.ds(pl.multiple_of((1 - core) * half, PAIR), half)
    act_ref[...] = act_full[:, own]
    gp_ref[...] = gp_full[:, own]
    far_ref[:, :half] = act_full[:, their]
    far_ref[:, half:] = gp_full[:, their]


def owner(device, position, masks):
    splits = masks[:-1]
    bits = 0
    for mask in splits:
        bits = bits * 2 + (device // mask) % 2
    return bits ^ position


def spread(masks, full, keep, send):
    device = position_here()
    parts = 1 << (len(masks) - 1)
    size = full.shape[0] // parts
    for position in range(parts):
        block = pl.multiple_of(owner(device, position, masks) * size, ALIGN)
        out, at = (keep, position) if position < parts // 2 else (send, position - parts // 2)
        out[at * size : (at + 1) * size] = full[pl.ds(block, size)]


def outer_kernel(
    masks_c, masks_e, act, gp, h, far, h_far, cots, cots_far,
    keep_c, send_c, keep_e, send_e, full,
):
    step = 256
    half = act.shape[1]

    def product(left, right):
        right = jnp.concatenate(right, axis=0)
        for at in range(0, full.shape[0], step):
            part = slice(at, at + step)
            both = jnp.concatenate([rows(part) for rows in left], axis=0)
            full[part] = mm_left(both, right).astype(BF16)

    product(
        (lambda cols: act[:, cols], lambda cols: far[:, cols]), (cots[...], cots_far[...])
    )
    spread(masks_c, full, keep_c, send_c)
    product(
        (lambda cols: h[:, cols], lambda cols: h_far[:, cols]), (gp[...], far[:, half:])
    )
    spread(masks_e, full, keep_e, send_e)


def back_kernel(
    spots, g_here, g_there, r_ref, cots, p_ref, c_here, mix, q0, k0, v0, q1, k1, v1, log0, log1,
    gr, gm_ref, dq_ref, dk0, dv0, dk1, dv1, s_ref,
):
    gain = p_ref[GAIN2 : GAIN2 + 1]
    width = mix.buffer.shape[0]
    sums = [jnp.zeros((1, gain.shape[1]), F32) for _ in range(4)]
    low_parts = []
    for slot in range(2):
        part = slice(slot * WIN, (slot + 1) * WIN)
        other = slice((1 - slot) * WIN, (2 - slot) * WIN)
        grad = g_here[part] + g_there[other].astype(F32)
        normed, inverse = norm(r_ref[part])
        cot = cots[part].astype(F32)
        resid = cot + norm_back(grad * gain, normed, inverse)
        if slot == 0:
            gr.buffer[...] = resid
            gr.send()
        low_parts.append(resid.astype(BF16))
        for at, value in enumerate((grad * normed, grad, resid, cot)):
            sums[at] = sums[at] + jnp.sum(value, axis=0, keepdims=True)
    for at in range(4):
        s_ref[at : at + 1] = sums[at]
    s_ref[4:] = jnp.zeros((s_ref.shape[0] - 4, s_ref.shape[1]), F32)
    low = jnp.concatenate(low_parts, axis=0)
    ctx = jnp.concatenate([c_here[0], c_here[1]], axis=0)
    for half in range(2):
        cols = slice(half * width, (half + 1) * width)
        gm_ref[half * width : (half + 1) * width] = mm_left(ctx, low[:, cols]).astype(BF16)
    grad_ctx = mm_right(low, mix.get()[...]).astype(BF16)
    refs = ((q0, k0, v0, log0, dk0, dv0), (q1, k1, v1, log1, dk1, dv1))
    for at in range(0, width, PAIR):
        cols = slice(at, at + PAIR)
        q_sum = jnp.zeros((1, PAIR), F32)
        v_sum = jnp.zeros((1, PAIR), F32)
        for slot, (q, k, v, log, dk, dv) in enumerate(refs):
            q, k, v = q.get(), k.get(), v.get()
            start = window(spots, slot)
            query = split_heads(q[pl.ds(start, WIN), cols])
            grads = split_heads(grad_ctx[slot * WIN : (slot + 1) * WIN, cols])
            key, value = k[:, cols], v[:, cols]
            scores = mm_right(query, key)
            shift = log.get()[:, at // PAIR : at // PAIR + 1]
            probs = jnp.exp(scores - shift)
            slopes = mm_right(grads, value)
            inner = jnp.sum(probs * slopes, axis=-1, keepdims=True)
            grad_scores = (probs * (slopes - inner)).astype(BF16)
            grad_value = mm_left(grads, probs.astype(BF16)).T.astype(BF16)
            dv[:, cols] = grad_value
            dk[:, cols] = mm_left(query, grad_scores).T.astype(BF16)
            grad_query = (join_heads(mm(grad_scores, key)) * HEAD**-0.5).astype(BF16)
            dq_ref[slot, :, cols] = grad_query
            q_sum = q_sum + jnp.sum(grad_query.astype(F32), axis=0, keepdims=True)
            v_sum = v_sum + jnp.sum(grad_value.astype(F32), axis=0, keepdims=True)
        s_ref[4:5, cols] = q_sum
        s_ref[4:5, at + width : at + width + PAIR] = v_sum


def query_key_kernel(masks, spots, h0, h1, dq, dk0, dk1, keep, send, full):
    h0, h1 = h0.get(), h1.get()
    wide = h0.shape[1]
    starts = [window(spots, slot) for slot in range(2)]
    rows = jnp.concatenate([h0[pl.ds(starts[0], WIN)], h1[pl.ds(starts[1], WIN)]], axis=0)
    full[:wide] = mm_left(rows, jnp.concatenate([dq[0], dq[1]], axis=0)).astype(BF16)
    full[wide:] = (mm_left(h0[...], dk0[...]) + mm_left(h1[...], dk1[...])).astype(BF16)
    spread(masks, full, keep, send)


def value_mix_kernel(masks, h0, h1, dv0, dv1, gm, keep, send, full):
    h0, h1 = h0.get(), h1.get()
    wide = h0.shape[1]
    full[:wide] = (mm_left(h0[...], dv0[...]) + mm_left(h1[...], dv1[...])).astype(BF16)
    full[wide:] = gm[...]
    spread(masks, full, keep, send)


def first_kernel(
    spots, x0, x1, p_ref, w, dq, dk0, dv0, dk1, dv1, s_hidden, s_back,
    own, out_ref, shared_ref, s_ref, grads,
):
    rows, wide = x1.shape
    gain_sum = jnp.zeros((1, wide), F32)
    bias_sum = jnp.zeros((1, wide), F32)
    for slot, dk, dv in ((1, dk1, dv1), (0, dk0, dv0)):
        weights = w.get()
        kept = own.buffer if slot == 0 else grads
        x = x0.get() if slot == 0 else x1
        start = window(spots, slot)
        kept[...] = mm_right(dk[...], weights[1]) + mm_right(dv[...], weights[2])
        kept[pl.ds(start, WIN)] += mm_right(dq[slot], weights[0])
        for at in range(0, rows, 256):
            part = slice(at, at + 256)
            grad = kept[part]
            normed, _ = norm(x[part].astype(F32))
            gain_sum = gain_sum + jnp.sum(grad * normed, axis=0, keepdims=True)
            bias_sum = bias_sum + jnp.sum(grad, axis=0, keepdims=True)
            if slot == 1:
                out_ref[part] = grad.astype(BF16)
    width = shared_ref.shape[1]
    shared_ref[...] = jnp.zeros_like(shared_ref)
    s_ref[...] = jnp.zeros_like(s_ref)
    for half in range(wide // width):
        cols = slice(half * width, (half + 1) * width)
        shared_ref[half : half + 1] = gain_sum[:, cols]
        shared_ref[2 + half : 3 + half] = bias_sum[:, cols]
        for at in range(5):
            s_ref[2 * at + half : 2 * at + half + 1] = s_back[at : at + 1, cols]
    for at in range(s_hidden.shape[1] // width):
        s_ref[10 + at : 11 + at] = s_hidden[:, at * width : (at + 1) * width]


def input_kernel(spots, x, p_ref, own, there, gr, out):
    gain = p_ref[GAIN1 : GAIN1 + 1]
    x = x.get()
    rows = x.shape[0]
    for at in range(0, rows, 256):
        part = slice(at, at + 256)
        normed, inverse = norm(x[part].astype(F32))
        grad = own.get()[part] + there[part].astype(F32)
        out.buffer[part] = norm_back(grad * gain, normed, inverse)
    out.buffer[pl.ds(window(spots, 0), WIN)] += gr.get()[...]


def forward_kernel(slot, x, c_here, c_there, mix_here, mix_there, p_ref, we, wc, out):
    rows = x.get() if slot == 0 else x
    wide, hidden = we.buffer.shape
    for at in range(0, rows.shape[0], 256):
        part = slice(at, at + 256)
        branch = mm(c_here.get()[slot, part], mix_here.get()[...])
        branch = branch + mm(c_there[1 - slot, part], mix_there.get()[...])
        resid = rows[part].astype(F32) + branch + p_ref[MIXB : MIXB + 1]
        normed, _ = norm(resid)
        h = (normed * p_ref[GAIN2 : GAIN2 + 1] + p_ref[BIAS2 : BIAS2 + 1]).astype(BF16)
        total = jnp.zeros(resid.shape, F32)
        for row in range(hidden // wide):
            cols = slice(row * wide, (row + 1) * wide)
            act, _ = gelu_parts(mm(h, we.get()[:, cols]) + p_ref[EXPB + row : EXPB + row + 1])
            total = total + mm(act.astype(BF16), wc.get()[cols])
        if slot == 0:
            out.buffer[part] = resid + total + p_ref[OUTB : OUTB + 1]
        else:
            out[part] = total.astype(BF16)


def finish_kernel(base, there, out):
    out.buffer[...] = (base.get()[...] + there[...].astype(F32)).astype(BF16)


def pick(position, near, far, size, parts):
    half = parts // 2
    source, at = (near, position) if position < half else (far, position - half)
    return source[at * size : (at + 1) * size].astype(F32)


def assemble_kernel(masks, along, near, far, out, made, sems):
    rows, cols = near.shape
    parts = 1 << (len(masks) - 1)
    size = rows // parts
    here = position_here()
    core = lax.rem(here, 2)
    copies = []
    for at, (side, source) in enumerate(((core, near), (1 - core, far))):
        for position in range(parts):
            block = owner(here, position, masks) * size
            if along == 0:
                spot = pl.ds(pl.multiple_of(side * rows + block, ALIGN), size)
            else:
                spot = (
                    pl.ds(pl.multiple_of(block, ALIGN), size),
                    pl.ds(pl.multiple_of(side * cols, PAIR), cols),
                )
            index = at * parts + position
            made[index] = source[position * size : (position + 1) * size].astype(F32)
            copies.append(pltpu.make_async_copy(made.at[index], out.at[spot], sems.at[index]))
            copies[-1].start()
    for copy in copies:
        copy.wait()


def assemble_first_kernel(masks, near, far, proj, made, sems):
    size = made.shape[1]
    copies = []
    for position in range(made.shape[0]):
        spot = pl.ds(pl.multiple_of(owner(position_here(), position, masks) * size, ALIGN), size)
        made[position] = pick(position, near, far, size, made.shape[0])
        copies.append(pltpu.make_async_copy(made.at[position], proj.at[spot], sems.at[position]))
        copies[-1].start()
    for copy in copies:
        copy.wait()


def assemble_last_kernel(masks, near, far, extra, _, proj, mix, qvb, long, *rest):
    *vectors, made, sems = rest
    parts, size, width = made.shape
    base = parts * size
    cut = (proj.shape[0] - base) // size
    copies = []
    for position in range(parts):
        block = owner(position_here(), position, masks)
        made[position] = pick(position, near, far, size, parts)

        @pl.when(block < cut)
        def _():
            spot = pl.ds(pl.multiple_of(base + block * size, ALIGN), size)
            pltpu.make_async_copy(made.at[position], proj.at[spot], sems.at[position]).start()

        @pl.when(block >= cut)
        def _():
            left = (block - cut) * size
            half = left // width
            row = pl.multiple_of(left - half * width, ALIGN)
            col = pl.multiple_of(half * width, PAIR)
            spot = (pl.ds(row, size), pl.ds(col, width))
            pltpu.make_async_copy(made.at[position], mix.at[spot], sems.at[position]).start()

        copies.append(
            pltpu.make_async_copy(made.at[position], proj.at[pl.ds(0, size)], sems.at[position])
        )
    rows, more = parts * size // 2, extra.shape[0]
    total = extra[...] + far[rows : rows + more].astype(F32)
    total = total + far[rows + more : rows + 2 * more].astype(F32)
    for vector, at in zip(vectors, (0, 2, 8, 10, 12, 14)):
        vector[:width] = total[at].reshape(width)
        vector[width:] = total[at + 1].reshape(width)
    qvb[...] = total[16:18]
    for at in range(long.shape[0] // width):
        long[at * width : (at + 1) * width] = total[18 + at].reshape(width)
    for copy in copies:
        copy.wait()


def halve_kernel(coming, held, keep, send):
    half = keep.shape[0]
    keep[...] = (coming[:half].astype(F32) + held[:half].astype(F32)).astype(BF16)
    send[...] = (coming[half:].astype(F32) + held[half:].astype(F32)).astype(BF16)


def merge_kernel(kind, rows, coming, held, *rest):
    load = rest[-2] if len(rest) > 1 else rest[-1]
    if kind == "add":
        load[:rows] = (coming[:rows].astype(F32) + held[:rows].astype(F32)).astype(BF16)
    ends = None
    if kind == "choose":
        spot = position_here() // 4
        ends = (spot == 0) | (spot == 3)
        load[:rows] = jnp.where(ends, coming[:rows].astype(F32), held[:rows].astype(F32)).astype(BF16)
    if kind == "join":
        load[:rows] = held[:rows]
        load[rows : 2 * rows] = coming[:rows]
    if len(rest) > 1:
        extra, out = rest[0], rest[-1]
        more = extra.shape[0]
        base = rows * (2 if kind == "join" else 1)
        total = extra[...]
        if coming.shape[0] > rows:
            there = coming[rows : rows + more].astype(F32) + coming[rows + more :].astype(F32)
            total = jnp.where(ends, there, total) if kind == "choose" else total + there
        high = total.astype(BF16)
        load[base : base + more] = high
        load[base + more :] = (total - high.astype(F32)).astype(BF16)
        out[...] = total


def sums_kernel(there, here, small, out):
    size = here.shape[0]
    out[:size] = there[...] + here[...]
    out[size:] = small[...]


def flip(value, mask):
    count = lax.axis_size("dp")
    ends, inner = (0, 3), (1, 2)
    differ, senders = {UP: (4, ends), MIDDLE: (12, inner), DOWN: (4, inner)}.get(
        mask, (mask, (0, 1, 2, 3))
    )
    pairs = [(at, at ^ differ) for at in range(count) if at // 4 % 4 in senders]
    return lax.ppermute(value, "dp", pairs)


def swap(value):
    return lax.ppermute(value, "tensor", [(0, 1), (1, 0)])


def add_low(a, b):
    return (a.astype(F32) + b.astype(F32)).astype(BF16)


def load_extra(total, extra):
    high = extra.astype(BF16)
    return jnp.concatenate([total, high, (extra - high.astype(F32)).astype(BF16)])


class Order:
    def __init__(self):
        self.last = None

    def tie(self, value, *others):
        return lax.optimization_barrier((value,) + others)[0]

    def run(self, step, first, *rest):
        if self.last is not None:
            first = self.tie(first, self.last)
        out = step(first, *rest)
        self.last = out[0] if isinstance(out, tuple) else out
        return out


class Reduction:
    def __init__(self, order, keep, send, masks):
        self.order, self.masks, self.at = order, masks, 0
        self.held, self.coming = keep, self.flip(send, masks[0])
        self.rows = keep.shape[0]
        self.joins = [*masks[:-1]] if 1 in masks else [1, *masks[:-1]]
        self.extra = None
        self.line = [UP, MIDDLE, DOWN] if masks[-1] == 0 else [masks[-1]]

    def flip(self, value, mask):
        if mask != 1 or PIECES == 1:
            return flip(value, mask)
        size = value.shape[0] // PIECES
        parts = [flip(value[at * size : (at + 1) * size], 1) for at in range(PIECES)]
        return jnp.concatenate(parts)

    def merge(self, kind):
        rows, width = self.rows * (2 if kind == "join" else 1), self.held.shape[1]
        more = 0 if self.extra is None else 2 * self.extra.shape[0]
        outs = [("v", struct((rows + more, width), BF16))]
        extra = []
        if self.extra is not None:
            extra = [("v", self.extra)]
            outs.append(("v", struct(self.extra.shape, F32)))
        result = self.order.run(
            lambda coming: call(
                partial(merge_kernel, kind, self.rows), kind,
                [("v", coming), ("v", self.held)] + extra, outs,
            ),
            self.coming,
        )
        self.rows, self.held = rows, result[0]
        if extra:
            self.extra = result[1]

    def step(self):
        splits = len(self.masks) - 1
        self.at += 1
        if self.at < splits:
            self.rows //= 2
            half = ("v", struct((self.rows, self.held.shape[1]), BF16))
            self.held, send = self.order.run(
                lambda coming: call(
                    halve_kernel, "halve", [("v", coming), ("v", self.held)], [half, half]
                ),
                self.coming,
            )
            self.coming = self.flip(send, self.masks[self.at])
            return
        if self.at == splits:
            self.merge("add")
            self.coming = self.flip(self.held, self.line.pop(0))
            return
        if self.at <= splits + 3 and self.masks[-1] == 0:
            if self.line:
                self.merge("add")
                if self.line == [DOWN]:
                    self.outer()
                self.coming = self.flip(self.held, self.line.pop(0))
                return
            self.merge("choose")
        elif self.at == splits + 1:
            self.merge("add")
            self.outer()
        else:
            self.merge("join")
        self.coming = self.flip(self.held, self.joins.pop())

    def outer(self):
        mask = PARTS
        while mask < lax.axis_size("dp"):
            total = self.held[: self.rows]
            self.held = add_low(total, flip(total, mask))
            if self.extra is not None:
                self.extra = self.extra + flip(self.extra, mask)
                self.held = load_extra(self.held, self.extra)
            mask *= 2


def body(
    inputs, out_grad, span_starts, span_lengths, norm1_gain, norm1_bias, projections,
    query_value_bias, mix_weight, mix_bias, norm2_gain, norm2_bias, expand_weight, expand_bias,
    contract_weight, contract_bias,
):
    rows, wide = inputs.shape
    width = projections.shape[2]
    hidden = expand_weight.shape[1]
    side = lax.axis_index("tensor")
    here = lax.axis_index("dp") % PARTS
    info = jnp.concatenate([span_starts, span_lengths, side[None]])
    order = Order()
    run = order.run

    other = swap(inputs)
    vectors = (
        norm1_gain, norm1_bias, mix_bias, norm2_gain, norm2_bias, contract_bias,
        query_value_bias, expand_bias,
    )
    low_rows = struct((rows, wide), BF16)
    full_rows = struct((rows, wide), F32)
    low_heads = struct((rows, width), BF16)
    wins = struct((2 * WIN, wide), BF16)
    full_wins = struct((2 * WIN, wide), F32)
    win_heads = struct((2, WIN, width), BF16)
    logs = struct((2 * WIN, PAIR), F32)
    projected = [("h", low_rows), ("h", low_heads), ("h", low_heads), ("h", low_heads)]
    mix_size = width >> (len(MASKS["mix"]) - 1)
    mix_near = swap(
        lax.dynamic_slice_in_dim(mix_weight, owner(here, 0, MASKS["mix"]) * mix_size, mix_size)
    )
    packed, cot0, spots = run(
        lambda grad: call(
            prepare_kernel, "prepare",
            [("s", info)] + [("v", vector) for vector in vectors] + [("r", grad)],
            [("v", struct((EXPB + hidden // wide, wide), F32)), ("v", struct((WIN + ALIGN, wide), BF16)), ("v", struct((8, PAIR), jnp.int32))],
            [pltpu.VMEM((WIN, wide), BF16), pltpu.SemaphoreType.DMA], limit=PREPARE_LIMIT,
        ),
        out_grad,
    )
    h0, q0, k0, v0, ctx_own, window_own, log0 = run(
        lambda x: call(
            own_kernel, "own", [("v", spots), ("v", x), ("v", packed), ("p", projections)],
            projected + [("h", low_heads), ("v", struct((1, WIN, width), BF16)), ("h", logs)],
        ),
        inputs,
    )
    for mask in MASKS["mix"][1:-1][::-1]:
        mix_near = jnp.concatenate([mix_near, flip(mix_near, mask)])
    mix_far = flip(order.tie(mix_near, window_own), MASKS["mix"][0])
    other = order.tie(other, window_own, mix_near, mix_far)
    cot1 = swap(order.tie(cot0, window_own))
    h1, q1, k1, v1, ctx, log1 = run(
        lambda x: call(
            other_kernel, "other",
            [("v", spots), ("v", x), ("v", packed), ("p", projections), ("v", window_own)],
            [("p", value) for _, value in projected] + [("v", win_heads), ("h", logs)],
        ),
        other,
    )
    ctx_there = swap(ctx)
    cots = run(lambda there, here: jnp.concatenate([here[:WIN], there[:WIN]]), cot1, cot0)
    cot_far = flip(cots, 1)
    half = hidden // 2
    low_half = struct((2 * WIN, half), BF16)
    resid, h_two, act, grad_pre, g_here, g_out, s_hidden, factors, mix_other = run(
        lambda there: call(
            partial(hidden_kernel, MASKS["mix"]), "hidden",
            [
                ("v", spots), ("p", inputs), ("v", other), ("v", ctx), ("v", there),
                ("p", mix_weight), ("v", mix_near), ("v", mix_far), ("v", packed),
                ("p", expand_weight), ("p", contract_weight), ("v", cots),
            ],
            [
                ("v", full_wins), ("v", wins), ("v", low_half), ("v", low_half), ("v", full_wins),
                ("v", wins), ("v", struct((1, hidden), F32)), ("v", struct((2 * WIN, hidden), BF16)),
                ("h", struct((width, wide), BF16)),
            ],
            [pltpu.VMEM((2 * WIN, hidden), BF16)] * 2,
        ),
        ctx_there,
    )
    g_there = swap(g_out)
    far, h_far = flip(factors, 1), flip(h_two, 1)
    values = {}
    groups = {}

    def whole():
        (values["ctx"],) = run(
            lambda q: call(
                whole_kernel, "whole", [("p", q), ("p", k1), ("p", v1), ("p", ctx_own)],
                [("h", struct((2, rows, width), BF16))],
            ),
            q1,
        )

    def outer():
        half_c, half_e = struct((half // 2, wide), BF16), struct((wide // 2, half), BF16)
        keep_c, send_c, keep_e, send_e = run(
            lambda h_far: call(
                partial(outer_kernel, MASKS["c"], MASKS["e"]), "outer",
                [("v", value) for value in (act, grad_pre, h_two, far, h_far)]
                + [("v", value) for value in (cots, cot_far)],
                [("v", half_c), ("v", half_c), ("v", half_e), ("v", half_e)],
                [pltpu.VMEM((half, wide), BF16)],
            ),
            h_far,
        )
        groups["c"] = Reduction(order, keep_c, send_c, MASKS["c"])
        groups["e"] = Reduction(order, keep_e, send_e, MASKS["e"])

    def share():
        values["ctx_there"] = swap(order.tie(values["ctx"], order.last))

    def back():
        (
            values["grad_resid"], values["grad_mix"], values["dq"], values["dk0"], values["dv0"],
            values["dk1"], values["dv1"], values["s_back"],
        ) = run(
            lambda there: call(
                back_kernel, "back",
                [("v", spots)]
                + [("v", value) for value in (g_here, there, resid, cots, packed, ctx)]
                + [("p", value) for value in (mix_weight, q0, k0, v0, q1, k1, v1, log0, log1)],
                [
                    ("h", struct((WIN, wide), F32)), ("v", struct((2 * width, width), BF16)),
                    ("v", win_heads), ("v", low_heads), ("v", low_heads), ("v", low_heads),
                    ("v", low_heads), ("v", struct((8, wide), F32)),
                ],
            ),
            g_there,
        )

    def gradients(group, scalars, kernel, name, *names):
        keep, send = run(
            lambda first: call(
                partial(kernel, MASKS[group]), name,
                scalars + [("p", h0), ("p", h1), ("v", first)]
                + [("v", values[name]) for name in names[1:]],
                [("v", struct((wide, width), BF16))] * 2, [pltpu.VMEM((2 * wide, width), BF16)],
            ),
            values[names[0]],
        )
        groups[group] = Reduction(order, keep, send, MASKS[group])

    def first():
        own, out, shared, values["small"] = run(
            lambda dq: call(
                first_kernel, "first",
                [("v", spots), ("p", inputs), ("v", other), ("v", packed), ("p", projections)]
                + [("v", dq)] + [("v", values[name]) for name in ("dk0", "dv0", "dk1", "dv1")]
                + [("v", s_hidden), ("v", values["s_back"])],
                [
                    ("h", full_rows), ("v", low_rows), ("v", struct((8, width), F32)),
                    ("v", struct((24, width), F32)),
                ],
                [pltpu.VMEM((rows, wide), F32)],
            ),
            values["dq"],
        )
        values["own"], values["shared"] = own, shared
        values["there"], values["shared_there"] = swap(out), swap(shared)

    def sums():
        here, small = values["shared"], values["small"]
        (groups["b"].extra,) = run(
            lambda there: call(
                sums_kernel, "sums", [("v", there), ("v", here), ("v", small)],
                [("v", struct((here.shape[0] + small.shape[0], width), F32))],
            ),
            values["shared_there"],
        )

    def forward(slot, x):
        return run(
            lambda far: call(
                partial(forward_kernel, slot), "forward",
                [
                    ("p" if slot == 0 else "v", x), ("p", values["ctx"]), ("v", far),
                    ("p", mix_weight), ("p", mix_other), ("v", packed), ("p", expand_weight),
                    ("p", contract_weight),
                ],
                [("h", full_rows) if slot == 0 else ("v", low_rows)],
            ),
            values["ctx_there"],
        )[0]

    def forward_other():
        values["forward"] = swap(forward(1, other))

    def forward_own():
        values["base"] = forward(0, inputs)

    def finish():
        (values["layer_out"],) = run(
            lambda far: call(
                finish_kernel, "finish", [("p", values["base"]), ("v", far)], [("h", low_rows)]
            ),
            values["forward"],
        )

    def backward_end():
        (values["input_grad"],) = run(
            lambda far: call(
                input_kernel, "input",
                [
                    ("v", spots), ("p", inputs), ("v", packed), ("p", values["own"]), ("v", far),
                    ("p", values["grad_resid"]),
                ],
                [("h", full_rows)],
            ),
            values["there"],
        )

    def assemble(group, shape, along):
        near, far = groups[group].held, groups[group].coming
        count = 1 << len(MASKS[group])
        size = 2 * near.shape[0] // count
        (values[group],) = run(
            lambda far: call(
                partial(assemble_kernel, MASKS[group], along), "assemble",
                [("v", near), ("v", far)], [("r", struct(shape, F32))],
                [
                    pltpu.VMEM((count, size, near.shape[1]), F32),
                    pltpu.SemaphoreType.DMA((count,)),
                ],
            ),
            far,
        )

    def made(group):
        count = 1 << len(MASKS[group][:-1])
        size = 2 * groups[group].rows // count
        return [pltpu.VMEM((count, size, width), F32), pltpu.SemaphoreType.DMA((count,))]

    def assemble_first():
        part = groups["a"]
        (values["proj"],) = run(
            lambda far: call(
                partial(assemble_first_kernel, MASKS["a"]), "assemble_first",
                [("v", part.held), ("v", far)],
                [("r", struct((3 * wide, width), F32))], made("a"),
            ),
            part.coming,
        )

    def assemble_last():
        part = groups["b"]
        values["attention"] = run(
            lambda far: call(
                partial(assemble_last_kernel, MASKS["b"]), "assemble_last",
                [("v", part.held), ("v", far), ("v", part.extra), ("r", values["proj"])],
                [
                    ("r", struct((3 * wide, width), F32)), ("r", struct((width, wide), F32)),
                    ("v", struct((2, width), F32)), ("v", struct((hidden,), F32)),
                ]
                + [("v", struct((wide,), F32))] * 6,
                made("b"), aliases={3: 0},
            ),
            part.coming,
        )

    steps = dict(
        whole=whole, outer=outer, cw=share, back=back, first=first, sm=sums, fwd1=forward_other,
        vm=lambda: gradients("b", [], value_mix_kernel, "value_mix", "dv0", "dv1", "grad_mix"),
        qk=lambda: gradients("a", [("v", spots)], query_key_kernel, "query_key", "dq", "dk0", "dk1"),
        fwd0=forward_own, finish=finish, input=backward_end,
        asm_c=lambda: assemble("c", (hidden, wide), 0),
        asm_e=lambda: assemble("e", (wide, hidden), 1), asm_a=assemble_first,
        asm_b=assemble_last,
    )
    for name in STEPS:
        if name in steps:
            steps[name]()
        else:
            groups[name].step()
    (
        grad_proj, grad_mix_weight, grad_qv_bias, grad_expand_bias, grad_gain_one, grad_bias_one,
        grad_gain_two, grad_bias_two, grad_mix_bias, grad_contract_bias,
    ) = values["attention"]
    return (
        values["layer_out"], values["input_grad"], grad_gain_one, grad_bias_one,
        grad_proj.reshape(3, wide, width), grad_qv_bias, grad_mix_weight, grad_mix_bias,
        grad_gain_two, grad_bias_two, values["e"], grad_expand_bias, values["c"],
        grad_contract_bias,
    )


def solution(mesh):
    rows = P(("dp", "tensor"), None)
    return jax.shard_map(
        body,
        mesh=mesh,
        in_specs=(
            rows, rows, P("dp"), P("dp"), P(), P(), P(None, None, "tensor"), P(None, "tensor"),
            P("tensor", None), P(), P(), P(), P(None, "tensor"), P("tensor"), P("tensor", None),
            P(),
        ),
        out_specs=(
            rows, rows, P(), P(), P(None, None, "tensor"), P(None, "tensor"), P("tensor", None),
            P(), P(), P(), P(None, "tensor"), P("tensor"), P("tensor", None), P(),
        ),
        check_vma=False,
    )
```

```python
from functools import partial

import jax
import jax.numpy as jnp
from jax import lax
from jax.experimental import pallas as pl
from jax.experimental.pallas import tpu as pltpu
from jax.sharding import PartitionSpec as P

RATE = 4
HEAD = 64
PAIR = 2 * HEAD
EPS = 1e-12
WIN = 144
ALIGN = 16
PREPARE_LIMIT = 56
PARTS = 16
UP, MIDDLE, DOWN = -1, -2, -3
MASKS = dict(c=(4, 2, 8), e=(2, 4, 8), a=(1, 2, 0), b=(1, 4, 2, 8), mix=(1, 2, 0))
F32 = jnp.float32
BF16 = jnp.bfloat16
MIB = 1 << 20
ROOT_HALF = 0.7071067811865476
GAUSS = 0.3989422804014327

TIMES = dict(
    add=3.92, halve=0.49, join=22.4, choose=44.8, sums=2.8, prepare=0.05, own=4, other=0.05,
    hidden=16, whole=57.85, outer=5.6, back=22.4, value_mix=0.014, query_key=0.112, first=32,
    forward=8, finish=32, input=7.84, assemble=44.8, assemble_first=8, assemble_last=5.6,
)
STEPS = (
    "whole", "outer", "back", "qk", "vm", "cw", "e", "c", "a", "b", "e", "a", "first", "c",
    "sm", "b", "e", "fwd0", "a", "c", "b", "a", "e", "c", "fwd1", "b", "input", "e", "a", "b",
    "c", "asm_e", "a", "asm_c", "b", "asm_a", "finish", "asm_b",
)
PIECES = 1

GAIN1, BIAS1, MIXB, GAIN2, BIAS2, OUTB, QVB, EXPB = range(8)
STARTS, LENGTHS, SIDE = 0, 2, 4


def mm(a, b):
    return lax.dot_general(a, b, (((1,), (0,)), ((), ())), preferred_element_type=F32)


def mm_right(a, b):
    return lax.dot_general(a, b, (((1,), (1,)), ((), ())), preferred_element_type=F32)


def mm_left(a, b):
    return lax.dot_general(a, b, (((0,), (0,)), ((), ())), preferred_element_type=F32)


def norm(values):
    mean = jnp.mean(values, axis=-1, keepdims=True)
    centred = values - mean
    var = jnp.mean(centred * centred, axis=-1, keepdims=True)
    inverse = lax.rsqrt(var + EPS)
    return centred * inverse, inverse


def norm_back(scaled, normed, inverse):
    inner = jnp.mean(scaled, axis=-1, keepdims=True)
    cross = jnp.mean(scaled * normed, axis=-1, keepdims=True)
    return inverse * (scaled - inner - normed * cross)


class Fetched:
    def __init__(self, source, buffer, sem):
        self.buffer = buffer
        self.copy = pltpu.make_async_copy(source, buffer, sem)
        self.copy.start()

    def get(self):
        if self.copy is not None:
            self.copy.wait()
            self.copy = None
        return self.buffer


class Present:
    def __init__(self, ref):
        self.buffer = ref

    def get(self):
        return self.buffer


class Kept:
    def __init__(self, ref):
        self.buffer = ref

    def send(self):
        pass


class Sent:
    def __init__(self, target, buffer, sem):
        self.buffer = buffer
        self.copy = pltpu.make_async_copy(buffer, target, sem)
        self.started = False

    def send(self):
        if not self.started:
            self.copy.start()
            self.started = True

    def finish(self):
        self.send()
        self.copy.wait()


def call(kernel, name, args, outs, scratch=(), limit=18, aliases=()):
    places = {
        "s": pl.BlockSpec(memory_space=pltpu.SMEM), "v": pl.BlockSpec(memory_space=pltpu.VMEM),
        "p": pl.BlockSpec(memory_space=pltpu.VMEM), "h": pl.BlockSpec(memory_space=pltpu.HBM),
        "r": pl.BlockSpec(memory_space=pltpu.HBM),
    }
    buffers = []
    for place, value in [*args, *outs]:
        if place == "h":
            buffers += [pltpu.VMEM(value.shape, value.dtype), pltpu.SemaphoreType.DMA]

    def whole(*refs):
        moving = list(refs[len(args) + len(outs) : len(args) + len(outs) + len(buffers)])
        given, results = [], []
        for at, (place, _) in enumerate(args):
            ref = refs[at]
            if place == "h":
                ref = Fetched(ref, moving.pop(0), moving.pop(0))
            elif place == "p":
                ref = Present(ref)
            given.append(ref)
        for at, (place, _) in enumerate(outs):
            ref = refs[len(args) + at]
            if place == "h":
                ref = Sent(ref, moving.pop(0), moving.pop(0))
            elif place == "p":
                ref = Kept(ref)
            results.append(ref)
        kernel(*given, *results, *refs[len(args) + len(outs) + len(buffers) :])
        for value in given:
            if isinstance(value, Fetched):
                value.get()
        for value in results:
            if isinstance(value, Sent):
                value.send()
        for value in results:
            if isinstance(value, Sent):
                value.finish()

    return pl.pallas_call(
        whole,
        out_shape=tuple(value for _, value in outs),
        in_specs=[places[place] for place, _ in args],
        out_specs=tuple(places[place] for place, _ in outs),
        scratch_shapes=buffers + list(scratch),
        input_output_aliases=dict(aliases),
        compiler_params=pltpu.CompilerParams(vmem_limit_bytes=limit * MIB),
        cost_estimate=pl.CostEstimate(
            flops=int(TIMES[name] * 5e8), bytes_accessed=int(TIMES[name] * 5e5), transcendentals=0
        ),
        name=name,
    )(*(value for _, value in args))


def struct(shape, kind):
    return jax.ShapeDtypeStruct(shape, kind)


def position_here():
    return lax.rem(lax.axis_index("dp"), PARTS)


def window(spots, slot):
    return pl.multiple_of(spots[slot, 0], ALIGN)


def project_rows(x, p_ref, w, h, q, k, v):
    rows = x.shape[0]
    width = q.buffer.shape[1]
    gain, bias = p_ref[GAIN1 : GAIN1 + 1], p_ref[BIAS1 : BIAS1 + 1]
    q_bias, v_bias = p_ref[QVB : QVB + 1, :width], p_ref[QVB : QVB + 1, width : 2 * width]
    for at in range(0, rows, 256):
        part = slice(at, at + 256)
        normed, _ = norm(x[part].astype(F32))
        low = (normed * gain + bias).astype(BF16)
        h.buffer[part] = low
        weights = w.get()
        q.buffer[part] = (mm(low, weights[0]) + q_bias).astype(BF16) * BF16(HEAD**-0.5)
        k.buffer[part] = mm(low, weights[1]).astype(BF16)
        v.buffer[part] = (mm(low, weights[2]) + v_bias).astype(BF16)
    for sent in (h, q, k, v):
        sent.send()


def split_heads(values):
    low = lax.broadcasted_iota(jnp.int32, values.shape, 1) < HEAD
    zero = jnp.zeros_like(values)
    return jnp.concatenate([jnp.where(low, values, zero), jnp.where(low, zero, values)], axis=0)


def join_heads(values):
    half = values.shape[0] // 2
    low = lax.broadcasted_iota(jnp.int32, (half, PAIR), 1) < HEAD
    return jnp.where(low, values[:half], values[half:])


def softmax(scores):
    expo = jnp.exp(scores - jnp.max(scores, axis=-1, keepdims=True))
    return expo / jnp.sum(expo, axis=-1, keepdims=True)


def attend(query, key, value):
    probs = softmax(mm_right(split_heads(query), key))
    return join_heads(mm(probs.astype(BF16), value)).astype(BF16)


def attend_window(start, q, k, v, c_ref, slot, log_ref):
    for at in range(0, q.shape[1], PAIR):
        cols = slice(at, at + PAIR)
        scores = mm_right(split_heads(q[pl.ds(start, WIN), cols]), k[:, cols])
        top = jnp.max(scores, axis=-1, keepdims=True)
        expo = jnp.exp(scores - top)
        total = jnp.sum(expo, axis=-1, keepdims=True)
        lane = lax.broadcasted_iota(jnp.int32, log_ref.shape, 1)
        log_ref[...] = jnp.where(lane == at // PAIR, top + jnp.log(total), log_ref[...])
        probs = (expo / total).astype(BF16)
        c_ref[slot, :, cols] = join_heads(mm(probs, v[:, cols])).astype(BF16)


def attend_rows(q, k, v, store):
    for at in range(0, q.shape[1], PAIR):
        cols = slice(at, at + PAIR)
        for row in range(0, q.shape[0], 256):
            part = slice(row, row + 256)
            store(part, cols, attend(q[part, cols], k[:, cols], v[:, cols]))


def prepare_kernel(info, g1, b1, mb, g2, b2, ob, qv, eb, grad, p_ref, cot_ref, spots, piece, sem):
    wide, width = grad.shape[1], qv.shape[1]
    side = info[SIDE]
    starts = []
    for first in (info[STARTS + side], info[STARTS + 1 - side]):
        start = first // (RATE * ALIGN) * ALIGN
        starts.append(pl.multiple_of(jnp.minimum(start, grad.shape[0] - WIN), ALIGN))
    row = lax.broadcasted_iota(jnp.int32, spots.shape, 0)
    spots[...] = jnp.where(row == 0, starts[0], starts[1])
    start = starts[0]
    copy = pltpu.make_async_copy(grad.at[pl.ds(start, WIN)], piece, sem)
    copy.start()
    for at, vector in enumerate((g1, b1, mb, g2, b2, ob)):
        p_ref[at : at + 1] = vector[...].astype(F32).reshape(1, wide)
    p_ref[QVB : QVB + 1, :width] = qv[0:1].astype(F32)
    p_ref[QVB : QVB + 1, width : 2 * width] = qv[1:2].astype(F32)
    long = eb[...].astype(F32)
    for at in range(eb.shape[0] // wide):
        p_ref[EXPB + at : EXPB + at + 1] = long[at * wide : (at + 1) * wide].reshape(1, wide)
    copy.wait()
    first = info[STARTS + side]
    last = first + info[LENGTHS + side]
    spot = (start + lax.broadcasted_iota(jnp.int32, piece.shape, 0)) * RATE
    kept = jnp.where((spot < last) & (spot + RATE > first), piece[...].astype(F32), 0.0)
    cot_ref[:WIN] = kept.astype(BF16)
    cot_ref[WIN:] = jnp.zeros((ALIGN, wide), BF16)


def own_kernel(spots, x, p_ref, w, h, q, k, v, c, win_ref, log_ref):
    project_rows(x, p_ref, w, h, q, k, v)

    def store(part, cols, value):
        c.buffer[part, cols] = value

    start = window(spots, 0)
    attend_window(start, q.buffer, k.buffer, v.buffer, win_ref, 0, log_ref.buffer)
    attend_rows(q.buffer, k.buffer, v.buffer, store)


def other_kernel(spots, x_ref, p_ref, w, win_ref, h, q, k, v, c_ref, log_ref):
    project_rows(x_ref, p_ref, w, h, q, k, v)
    start = window(spots, 1)
    c_ref[0] = win_ref[0]
    attend_window(start, q.buffer, k.buffer, v.buffer, c_ref, 1, log_ref.buffer)


def whole_kernel(q, k, v, own, c):
    def store(part, cols, value):
        c.buffer[1, part, cols] = value

    c.buffer[0] = own.get()[...]
    attend_rows(q.get(), k.get(), v.get(), store)


def gelu_parts(pre):
    cdf = 0.5 + 0.5 * lax.erf(pre * ROOT_HALF)
    return pre * cdf, cdf


def hidden_kernel(
    masks, spots, x0, x1, c_here, c_there, mix_here, mix_near, mix_far, p_ref, we, wc, cots,
    r_ref, h_ref, act_ref, gp_ref, g_ref, gout_ref, gb_ref, far_ref, mix_there,
    act_full, gp_full,
):
    gain, bias = p_ref[GAIN2 : GAIN2 + 1], p_ref[BIAS2 : BIAS2 + 1]
    wide, hidden = we.buffer.shape
    parts = 1 << (len(masks) - 1)
    size = 2 * mix_near.shape[0] // parts
    for position in range(parts):
        spot = pl.multiple_of(owner(position_here(), position, masks) * size, ALIGN)
        source, at = (mix_near, position) if position < parts // 2 else (mix_far, position - parts // 2)
        mix_there.buffer[pl.ds(spot, size)] = source[at * size : (at + 1) * size]
    mix_there.send()
    for slot, x in enumerate((x0, x1)):
        rows = x.get() if slot == 0 else x
        start = window(spots, slot)
        branch = mm(c_here[slot], mix_here.get()[...])
        branch = branch + mm(c_there[1 - slot], mix_there.buffer[...])
        resid = rows[pl.ds(start, WIN)].astype(F32) + branch + p_ref[MIXB : MIXB + 1]
        normed, _ = norm(resid)
        part = slice(slot * WIN, (slot + 1) * WIN)
        r_ref[part] = resid
        h_ref[part] = (normed * gain + bias).astype(BF16)
    h = h_ref[...]
    cot = cots[...]
    total = jnp.zeros(g_ref.shape, F32)
    for at in range(hidden // wide):
        cols = slice(at * wide, (at + 1) * wide)
        up = we.get()[:, cols]
        pre = mm(h, up) + p_ref[EXPB + at : EXPB + at + 1]
        act, cdf = gelu_parts(pre)
        act_full[:, cols] = act.astype(BF16)
        slope = cdf + pre * (jnp.exp(-0.5 * pre * pre) * GAUSS)
        grad_pre = (mm_right(cot, wc.get()[cols]) * slope).astype(BF16)
        gp_full[:, cols] = grad_pre
        gb_ref[:, cols] = jnp.sum(grad_pre.astype(F32), axis=0, keepdims=True)
        total = total + mm_right(grad_pre, up)
    g_ref[...] = total
    gout_ref[...] = total.astype(BF16)
    half = hidden // 2
    core = lax.rem(position_here(), 2)
    own = pl.ds(pl.multiple_of(core * half, PAIR), half)
    their = pl.ds(pl.multiple_of((1 - core) * half, PAIR), half)
    act_ref[...] = act_full[:, own]
    gp_ref[...] = gp_full[:, own]
    far_ref[:, :half] = act_full[:, their]
    far_ref[:, half:] = gp_full[:, their]


def owner(device, position, masks):
    splits = masks[:-1]
    bits = 0
    for mask in splits:
        bits = bits * 2 + (device // mask) % 2
    return bits ^ position


def spread(masks, full, keep, send):
    device = position_here()
    parts = 1 << (len(masks) - 1)
    size = full.shape[0] // parts
    for position in range(parts):
        block = pl.multiple_of(owner(device, position, masks) * size, ALIGN)
        out, at = (keep, position) if position < parts // 2 else (send, position - parts // 2)
        out[at * size : (at + 1) * size] = full[pl.ds(block, size)]


def outer_kernel(
    masks_c, masks_e, act, gp, h, far, h_far, cots, cots_far,
    keep_c, send_c, keep_e, send_e, full,
):
    step = 256
    half = act.shape[1]

    def product(left, right):
        right = jnp.concatenate(right, axis=0)
        for at in range(0, full.shape[0], step):
            part = slice(at, at + step)
            both = jnp.concatenate([rows(part) for rows in left], axis=0)
            full[part] = mm_left(both, right).astype(BF16)

    product(
        (lambda cols: act[:, cols], lambda cols: far[:, cols]), (cots[...], cots_far[...])
    )
    spread(masks_c, full, keep_c, send_c)
    product(
        (lambda cols: h[:, cols], lambda cols: h_far[:, cols]), (gp[...], far[:, half:])
    )
    spread(masks_e, full, keep_e, send_e)


def back_kernel(
    spots, g_here, g_there, r_ref, cots, p_ref, c_here, mix, q0, k0, v0, q1, k1, v1, log0, log1,
    gr, gm_ref, dq_ref, dk0, dv0, dk1, dv1, s_ref,
):
    gain = p_ref[GAIN2 : GAIN2 + 1]
    width = mix.buffer.shape[0]
    sums = [jnp.zeros((1, gain.shape[1]), F32) for _ in range(4)]
    low_parts = []
    for slot in range(2):
        part = slice(slot * WIN, (slot + 1) * WIN)
        other = slice((1 - slot) * WIN, (2 - slot) * WIN)
        grad = g_here[part] + g_there[other].astype(F32)
        normed, inverse = norm(r_ref[part])
        cot = cots[part].astype(F32)
        resid = cot + norm_back(grad * gain, normed, inverse)
        if slot == 0:
            gr.buffer[...] = resid
            gr.send()
        low_parts.append(resid.astype(BF16))
        for at, value in enumerate((grad * normed, grad, resid, cot)):
            sums[at] = sums[at] + jnp.sum(value, axis=0, keepdims=True)
    for at in range(4):
        s_ref[at : at + 1] = sums[at]
    s_ref[4:] = jnp.zeros((s_ref.shape[0] - 4, s_ref.shape[1]), F32)
    low = jnp.concatenate(low_parts, axis=0)
    ctx = jnp.concatenate([c_here[0], c_here[1]], axis=0)
    for half in range(2):
        cols = slice(half * width, (half + 1) * width)
        gm_ref[half * width : (half + 1) * width] = mm_left(ctx, low[:, cols]).astype(BF16)
    grad_ctx = mm_right(low, mix.get()[...]).astype(BF16)
    refs = ((q0, k0, v0, log0, dk0, dv0), (q1, k1, v1, log1, dk1, dv1))
    for at in range(0, width, PAIR):
        cols = slice(at, at + PAIR)
        q_sum = jnp.zeros((1, PAIR), F32)
        v_sum = jnp.zeros((1, PAIR), F32)
        for slot, (q, k, v, log, dk, dv) in enumerate(refs):
            q, k, v = q.get(), k.get(), v.get()
            start = window(spots, slot)
            query = split_heads(q[pl.ds(start, WIN), cols])
            grads = split_heads(grad_ctx[slot * WIN : (slot + 1) * WIN, cols])
            key, value = k[:, cols], v[:, cols]
            scores = mm_right(query, key)
            shift = log.get()[:, at // PAIR : at // PAIR + 1]
            probs = jnp.exp(scores - shift)
            slopes = mm_right(grads, value)
            inner = jnp.sum(probs * slopes, axis=-1, keepdims=True)
            grad_scores = (probs * (slopes - inner)).astype(BF16)
            grad_value = mm_left(grads, probs.astype(BF16)).T.astype(BF16)
            dv[:, cols] = grad_value
            dk[:, cols] = mm_left(query, grad_scores).T.astype(BF16)
            grad_query = (join_heads(mm(grad_scores, key)) * HEAD**-0.5).astype(BF16)
            dq_ref[slot, :, cols] = grad_query
            q_sum = q_sum + jnp.sum(grad_query.astype(F32), axis=0, keepdims=True)
            v_sum = v_sum + jnp.sum(grad_value.astype(F32), axis=0, keepdims=True)
        s_ref[4:5, cols] = q_sum
        s_ref[4:5, at + width : at + width + PAIR] = v_sum


def query_key_kernel(masks, spots, h0, h1, dq, dk0, dk1, keep, send, full):
    h0, h1 = h0.get(), h1.get()
    wide = h0.shape[1]
    starts = [window(spots, slot) for slot in range(2)]
    rows = jnp.concatenate([h0[pl.ds(starts[0], WIN)], h1[pl.ds(starts[1], WIN)]], axis=0)
    full[:wide] = mm_left(rows, jnp.concatenate([dq[0], dq[1]], axis=0)).astype(BF16)
    both = jnp.concatenate([h0[...], h1[...]], axis=0)
    full[wide:] = mm_left(both, jnp.concatenate([dk0[...], dk1[...]], axis=0)).astype(BF16)
    spread(masks, full, keep, send)


def value_mix_kernel(masks, h0, h1, dv0, dv1, gm, keep, send, full):
    h0, h1 = h0.get(), h1.get()
    wide = h0.shape[1]
    both = jnp.concatenate([h0[...], h1[...]], axis=0)
    full[:wide] = mm_left(both, jnp.concatenate([dv0[...], dv1[...]], axis=0)).astype(BF16)
    full[wide:] = gm[...]
    spread(masks, full, keep, send)


def first_kernel(
    spots, x0, x1, p_ref, w, dq, dk0, dv0, dk1, dv1, s_hidden, s_back,
    own, out_ref, shared_ref, s_ref, grads,
):
    rows, wide = x1.shape
    gain_sum = jnp.zeros((1, wide), F32)
    bias_sum = jnp.zeros((1, wide), F32)
    for slot, dk, dv in ((1, dk1, dv1), (0, dk0, dv0)):
        weights = w.get()
        kept = own.buffer if slot == 0 else grads
        x = x0.get() if slot == 0 else x1
        start = window(spots, slot)
        both = jnp.concatenate([weights[1], weights[2]], axis=1)
        kept[...] = mm_right(jnp.concatenate([dk[...], dv[...]], axis=1), both)
        kept[pl.ds(start, WIN)] += mm_right(dq[slot], weights[0])
        for at in range(0, rows, 256):
            part = slice(at, at + 256)
            grad = kept[part]
            normed, _ = norm(x[part].astype(F32))
            gain_sum = gain_sum + jnp.sum(grad * normed, axis=0, keepdims=True)
            bias_sum = bias_sum + jnp.sum(grad, axis=0, keepdims=True)
            if slot == 1:
                out_ref[part] = grad.astype(BF16)
    width = shared_ref.shape[1]
    shared_ref[...] = jnp.zeros_like(shared_ref)
    s_ref[...] = jnp.zeros_like(s_ref)
    for half in range(wide // width):
        cols = slice(half * width, (half + 1) * width)
        shared_ref[half : half + 1] = gain_sum[:, cols]
        shared_ref[2 + half : 3 + half] = bias_sum[:, cols]
        for at in range(5):
            s_ref[2 * at + half : 2 * at + half + 1] = s_back[at : at + 1, cols]
    for at in range(s_hidden.shape[1] // width):
        s_ref[10 + at : 11 + at] = s_hidden[:, at * width : (at + 1) * width]


def input_kernel(spots, x, p_ref, own, there, gr, out):
    gain = p_ref[GAIN1 : GAIN1 + 1]
    x = x.get()
    rows = x.shape[0]
    for at in range(0, rows, 256):
        part = slice(at, at + 256)
        normed, inverse = norm(x[part].astype(F32))
        grad = own.get()[part] + there[part].astype(F32)
        out.buffer[part] = norm_back(grad * gain, normed, inverse)
    out.buffer[pl.ds(window(spots, 0), WIN)] += gr.get()[...]


def forward_kernel(slot, x, c_here, c_there, mix_here, mix_there, p_ref, we, wc, out):
    rows = x.get() if slot == 0 else x
    wide, hidden = we.buffer.shape
    for at in range(0, rows.shape[0], 256):
        part = slice(at, at + 256)
        heads = jnp.concatenate([c_here.get()[slot, part], c_there[1 - slot, part]], axis=1)
        branch = mm(heads, jnp.concatenate([mix_here.get()[...], mix_there.get()[...]], axis=0))
        resid = rows[part].astype(F32) + branch + p_ref[MIXB : MIXB + 1]
        normed, _ = norm(resid)
        h = (normed * p_ref[GAIN2 : GAIN2 + 1] + p_ref[BIAS2 : BIAS2 + 1]).astype(BF16)
        total = jnp.zeros(resid.shape, F32)
        for row in range(hidden // wide):
            cols = slice(row * wide, (row + 1) * wide)
            act, _ = gelu_parts(mm(h, we.get()[:, cols]) + p_ref[EXPB + row : EXPB + row + 1])
            total = total + mm(act.astype(BF16), wc.get()[cols])
        if slot == 0:
            out.buffer[part] = resid + total + p_ref[OUTB : OUTB + 1]
        else:
            out[part] = total.astype(BF16)


def finish_kernel(base, there, out):
    out.buffer[...] = (base.get()[...] + there[...].astype(F32)).astype(BF16)


def pick(position, near, far, size, parts):
    half = parts // 2
    source, at = (near, position) if position < half else (far, position - half)
    return source[at * size : (at + 1) * size].astype(F32)


def assemble_kernel(masks, along, near, far, out, made, sems):
    rows, cols = near.shape
    parts = 1 << (len(masks) - 1)
    size = rows // parts
    here = position_here()
    core = lax.rem(here, 2)
    copies = []
    for at, (side, source) in enumerate(((core, near), (1 - core, far))):
        for position in range(parts):
            block = owner(here, position, masks) * size
            if along == 0:
                spot = pl.ds(pl.multiple_of(side * rows + block, ALIGN), size)
            else:
                spot = (
                    pl.ds(pl.multiple_of(block, ALIGN), size),
                    pl.ds(pl.multiple_of(side * cols, PAIR), cols),
                )
            index = at * parts + position
            made[index] = source[position * size : (position + 1) * size].astype(F32)
            copies.append(pltpu.make_async_copy(made.at[index], out.at[spot], sems.at[index]))
            copies[-1].start()
    for copy in copies:
        copy.wait()


def assemble_first_kernel(masks, near, far, proj, made, sems):
    size = made.shape[1]
    copies = []
    for position in range(made.shape[0]):
        spot = pl.ds(pl.multiple_of(owner(position_here(), position, masks) * size, ALIGN), size)
        made[position] = pick(position, near, far, size, made.shape[0])
        copies.append(pltpu.make_async_copy(made.at[position], proj.at[spot], sems.at[position]))
        copies[-1].start()
    for copy in copies:
        copy.wait()


def assemble_last_kernel(masks, near, far, extra, _, proj, mix, qvb, long, *rest):
    *vectors, made, sems = rest
    parts, size, width = made.shape
    base = parts * size
    cut = (proj.shape[0] - base) // size
    copies = []
    for position in range(parts):
        block = owner(position_here(), position, masks)
        made[position] = pick(position, near, far, size, parts)

        @pl.when(block < cut)
        def _():
            spot = pl.ds(pl.multiple_of(base + block * size, ALIGN), size)
            pltpu.make_async_copy(made.at[position], proj.at[spot], sems.at[position]).start()

        @pl.when(block >= cut)
        def _():
            left = (block - cut) * size
            half = left // width
            row = pl.multiple_of(left - half * width, ALIGN)
            col = pl.multiple_of(half * width, PAIR)
            spot = (pl.ds(row, size), pl.ds(col, width))
            pltpu.make_async_copy(made.at[position], mix.at[spot], sems.at[position]).start()

        copies.append(
            pltpu.make_async_copy(made.at[position], proj.at[pl.ds(0, size)], sems.at[position])
        )
    rows, more = parts * size // 2, extra.shape[0]
    total = extra[...] + far[rows : rows + more].astype(F32)
    total = total + far[rows + more : rows + 2 * more].astype(F32)
    for vector, at in zip(vectors, (0, 2, 8, 10, 12, 14)):
        vector[:width] = total[at].reshape(width)
        vector[width:] = total[at + 1].reshape(width)
    qvb[...] = total[16:18]
    for at in range(long.shape[0] // width):
        long[at * width : (at + 1) * width] = total[18 + at].reshape(width)
    for copy in copies:
        copy.wait()


def halve_kernel(coming, held, keep, send):
    half = keep.shape[0]
    keep[...] = (coming[:half].astype(F32) + held[:half].astype(F32)).astype(BF16)
    send[...] = (coming[half:].astype(F32) + held[half:].astype(F32)).astype(BF16)


def merge_kernel(kind, rows, coming, held, *rest):
    load = rest[-2] if len(rest) > 1 else rest[-1]
    if kind == "add":
        load[:rows] = (coming[:rows].astype(F32) + held[:rows].astype(F32)).astype(BF16)
    ends = None
    if kind == "choose":
        spot = position_here() // 4
        ends = (spot == 0) | (spot == 3)
        load[:rows] = jnp.where(ends, coming[:rows].astype(F32), held[:rows].astype(F32)).astype(BF16)
    if kind == "join":
        load[:rows] = held[:rows]
        load[rows : 2 * rows] = coming[:rows]
    if len(rest) > 1:
        extra, out = rest[0], rest[-1]
        more = extra.shape[0]
        base = rows * (2 if kind == "join" else 1)
        total = extra[...]
        if coming.shape[0] > rows:
            there = coming[rows : rows + more].astype(F32) + coming[rows + more :].astype(F32)
            total = jnp.where(ends, there, total) if kind == "choose" else total + there
        high = total.astype(BF16)
        load[base : base + more] = high
        load[base + more :] = (total - high.astype(F32)).astype(BF16)
        out[...] = total


def sums_kernel(there, here, small, out):
    size = here.shape[0]
    out[:size] = there[...] + here[...]
    out[size:] = small[...]


def flip(value, mask):
    count = lax.axis_size("dp")
    ends, inner = (0, 3), (1, 2)
    differ, senders = {UP: (4, ends), MIDDLE: (12, inner), DOWN: (4, inner)}.get(
        mask, (mask, (0, 1, 2, 3))
    )
    pairs = [(at, at ^ differ) for at in range(count) if at // 4 % 4 in senders]
    return lax.ppermute(value, "dp", pairs)


def swap(value):
    return lax.ppermute(value, "tensor", [(0, 1), (1, 0)])


def add_low(a, b):
    return (a.astype(F32) + b.astype(F32)).astype(BF16)


def load_extra(total, extra):
    high = extra.astype(BF16)
    return jnp.concatenate([total, high, (extra - high.astype(F32)).astype(BF16)])


class Order:
    def __init__(self):
        self.last = None

    def tie(self, value, *others):
        return lax.optimization_barrier((value,) + others)[0]

    def run(self, step, first, *rest):
        if self.last is not None:
            first = self.tie(first, self.last)
        out = step(first, *rest)
        self.last = out[0] if isinstance(out, tuple) else out
        return out


class Reduction:
    def __init__(self, order, keep, send, masks):
        self.order, self.masks, self.at = order, masks, 0
        self.held, self.coming = keep, self.flip(send, masks[0])
        self.rows = keep.shape[0]
        self.joins = [*masks[:-1]] if 1 in masks else [1, *masks[:-1]]
        self.extra = None
        self.line = [UP, MIDDLE, DOWN] if masks[-1] == 0 else [masks[-1]]

    def flip(self, value, mask):
        if mask != 1 or PIECES == 1:
            return flip(value, mask)
        size = value.shape[0] // PIECES
        parts = [flip(value[at * size : (at + 1) * size], 1) for at in range(PIECES)]
        return jnp.concatenate(parts)

    def merge(self, kind):
        rows, width = self.rows * (2 if kind == "join" else 1), self.held.shape[1]
        more = 0 if self.extra is None else 2 * self.extra.shape[0]
        outs = [("v", struct((rows + more, width), BF16))]
        extra = []
        if self.extra is not None:
            extra = [("v", self.extra)]
            outs.append(("v", struct(self.extra.shape, F32)))
        result = self.order.run(
            lambda coming: call(
                partial(merge_kernel, kind, self.rows), kind,
                [("v", coming), ("v", self.held)] + extra, outs,
            ),
            self.coming,
        )
        self.rows, self.held = rows, result[0]
        if extra:
            self.extra = result[1]

    def step(self):
        splits = len(self.masks) - 1
        self.at += 1
        if self.at < splits:
            self.rows //= 2
            half = ("v", struct((self.rows, self.held.shape[1]), BF16))
            self.held, send = self.order.run(
                lambda coming: call(
                    halve_kernel, "halve", [("v", coming), ("v", self.held)], [half, half]
                ),
                self.coming,
            )
            self.coming = self.flip(send, self.masks[self.at])
            return
        if self.at == splits:
            self.merge("add")
            self.coming = self.flip(self.held, self.line.pop(0))
            return
        if self.at <= splits + 3 and self.masks[-1] == 0:
            if self.line:
                self.merge("add")
                if self.line == [DOWN]:
                    self.outer()
                self.coming = self.flip(self.held, self.line.pop(0))
                return
            self.merge("choose")
        elif self.at == splits + 1:
            self.merge("add")
            self.outer()
        else:
            self.merge("join")
        self.coming = self.flip(self.held, self.joins.pop())

    def outer(self):
        mask = PARTS
        while mask < lax.axis_size("dp"):
            total = self.held[: self.rows]
            self.held = add_low(total, flip(total, mask))
            if self.extra is not None:
                self.extra = self.extra + flip(self.extra, mask)
                self.held = load_extra(self.held, self.extra)
            mask *= 2


def body(
    inputs, out_grad, span_starts, span_lengths, norm1_gain, norm1_bias, projections,
    query_value_bias, mix_weight, mix_bias, norm2_gain, norm2_bias, expand_weight, expand_bias,
    contract_weight, contract_bias,
):
    rows, wide = inputs.shape
    width = projections.shape[2]
    hidden = expand_weight.shape[1]
    side = lax.axis_index("tensor")
    here = lax.axis_index("dp") % PARTS
    info = jnp.concatenate([span_starts, span_lengths, side[None]])
    order = Order()
    run = order.run

    other = swap(inputs)
    vectors = (
        norm1_gain, norm1_bias, mix_bias, norm2_gain, norm2_bias, contract_bias,
        query_value_bias, expand_bias,
    )
    low_rows = struct((rows, wide), BF16)
    full_rows = struct((rows, wide), F32)
    low_heads = struct((rows, width), BF16)
    wins = struct((2 * WIN, wide), BF16)
    full_wins = struct((2 * WIN, wide), F32)
    win_heads = struct((2, WIN, width), BF16)
    logs = struct((2 * WIN, PAIR), F32)
    projected = [("h", low_rows), ("h", low_heads), ("h", low_heads), ("h", low_heads)]
    mix_size = width >> (len(MASKS["mix"]) - 1)
    mix_near = swap(
        lax.dynamic_slice_in_dim(mix_weight, owner(here, 0, MASKS["mix"]) * mix_size, mix_size)
    )
    packed, cot0, spots = run(
        lambda grad: call(
            prepare_kernel, "prepare",
            [("s", info)] + [("v", vector) for vector in vectors] + [("r", grad)],
            [("v", struct((EXPB + hidden // wide, wide), F32)), ("v", struct((WIN + ALIGN, wide), BF16)), ("v", struct((8, PAIR), jnp.int32))],
            [pltpu.VMEM((WIN, wide), BF16), pltpu.SemaphoreType.DMA], limit=PREPARE_LIMIT,
        ),
        out_grad,
    )
    h0, q0, k0, v0, ctx_own, window_own, log0 = run(
        lambda x: call(
            own_kernel, "own", [("v", spots), ("v", x), ("v", packed), ("p", projections)],
            projected + [("h", low_heads), ("v", struct((1, WIN, width), BF16)), ("h", logs)],
        ),
        inputs,
    )
    for mask in MASKS["mix"][1:-1][::-1]:
        mix_near = jnp.concatenate([mix_near, flip(mix_near, mask)])
    mix_far = flip(order.tie(mix_near, window_own), MASKS["mix"][0])
    other = order.tie(other, window_own, mix_near, mix_far)
    cot1 = swap(order.tie(cot0, window_own))
    h1, q1, k1, v1, ctx, log1 = run(
        lambda x: call(
            other_kernel, "other",
            [("v", spots), ("v", x), ("v", packed), ("p", projections), ("v", window_own)],
            [("p", value) for _, value in projected] + [("v", win_heads), ("h", logs)],
        ),
        other,
    )
    ctx_there = swap(ctx)
    cots = run(lambda there, here: jnp.concatenate([here[:WIN], there[:WIN]]), cot1, cot0)
    cot_far = flip(cots, 1)
    half = hidden // 2
    low_half = struct((2 * WIN, half), BF16)
    resid, h_two, act, grad_pre, g_here, g_out, s_hidden, factors, mix_other = run(
        lambda there: call(
            partial(hidden_kernel, MASKS["mix"]), "hidden",
            [
                ("v", spots), ("p", inputs), ("v", other), ("v", ctx), ("v", there),
                ("p", mix_weight), ("v", mix_near), ("v", mix_far), ("v", packed),
                ("p", expand_weight), ("p", contract_weight), ("v", cots),
            ],
            [
                ("v", full_wins), ("v", wins), ("v", low_half), ("v", low_half), ("v", full_wins),
                ("v", wins), ("v", struct((1, hidden), F32)), ("v", struct((2 * WIN, hidden), BF16)),
                ("h", struct((width, wide), BF16)),
            ],
            [pltpu.VMEM((2 * WIN, hidden), BF16)] * 2,
        ),
        ctx_there,
    )
    g_there = swap(g_out)
    far, h_far = flip(factors, 1), flip(h_two, 1)
    values = {}
    groups = {}

    def whole():
        (values["ctx"],) = run(
            lambda q: call(
                whole_kernel, "whole", [("p", q), ("p", k1), ("p", v1), ("p", ctx_own)],
                [("h", struct((2, rows, width), BF16))],
            ),
            q1,
        )

    def outer():
        half_c, half_e = struct((half // 2, wide), BF16), struct((wide // 2, half), BF16)
        keep_c, send_c, keep_e, send_e = run(
            lambda h_far: call(
                partial(outer_kernel, MASKS["c"], MASKS["e"]), "outer",
                [("v", value) for value in (act, grad_pre, h_two, far, h_far)]
                + [("v", value) for value in (cots, cot_far)],
                [("v", half_c), ("v", half_c), ("v", half_e), ("v", half_e)],
                [pltpu.VMEM((half, wide), BF16)],
            ),
            h_far,
        )
        groups["c"] = Reduction(order, keep_c, send_c, MASKS["c"])
        groups["e"] = Reduction(order, keep_e, send_e, MASKS["e"])

    def share():
        values["ctx_there"] = swap(order.tie(values["ctx"], order.last))

    def back():
        (
            values["grad_resid"], values["grad_mix"], values["dq"], values["dk0"], values["dv0"],
            values["dk1"], values["dv1"], values["s_back"],
        ) = run(
            lambda there: call(
                back_kernel, "back",
                [("v", spots)]
                + [("v", value) for value in (g_here, there, resid, cots, packed, ctx)]
                + [("p", value) for value in (mix_weight, q0, k0, v0, q1, k1, v1, log0, log1)],
                [
                    ("h", struct((WIN, wide), F32)), ("v", struct((2 * width, width), BF16)),
                    ("v", win_heads), ("v", low_heads), ("v", low_heads), ("v", low_heads),
                    ("v", low_heads), ("v", struct((8, wide), F32)),
                ],
            ),
            g_there,
        )

    def gradients(group, scalars, kernel, name, *names):
        keep, send = run(
            lambda first: call(
                partial(kernel, MASKS[group]), name,
                scalars + [("p", h0), ("p", h1), ("v", first)]
                + [("v", values[name]) for name in names[1:]],
                [("v", struct((wide, width), BF16))] * 2, [pltpu.VMEM((2 * wide, width), BF16)],
            ),
            values[names[0]],
        )
        groups[group] = Reduction(order, keep, send, MASKS[group])

    def first():
        own, out, shared, values["small"] = run(
            lambda dq: call(
                first_kernel, "first",
                [("v", spots), ("p", inputs), ("v", other), ("v", packed), ("p", projections)]
                + [("v", dq)] + [("v", values[name]) for name in ("dk0", "dv0", "dk1", "dv1")]
                + [("v", s_hidden), ("v", values["s_back"])],
                [
                    ("h", full_rows), ("v", low_rows), ("v", struct((8, width), F32)),
                    ("v", struct((24, width), F32)),
                ],
                [pltpu.VMEM((rows, wide), F32)],
            ),
            values["dq"],
        )
        values["own"], values["shared"] = own, shared
        values["there"], values["shared_there"] = swap(out), swap(shared)

    def sums():
        here, small = values["shared"], values["small"]
        (groups["b"].extra,) = run(
            lambda there: call(
                sums_kernel, "sums", [("v", there), ("v", here), ("v", small)],
                [("v", struct((here.shape[0] + small.shape[0], width), F32))],
            ),
            values["shared_there"],
        )

    def forward(slot, x):
        return run(
            lambda far: call(
                partial(forward_kernel, slot), "forward",
                [
                    ("p" if slot == 0 else "v", x), ("p", values["ctx"]), ("v", far),
                    ("p", mix_weight), ("p", mix_other), ("v", packed), ("p", expand_weight),
                    ("p", contract_weight),
                ],
                [("h", full_rows) if slot == 0 else ("v", low_rows)],
            ),
            values["ctx_there"],
        )[0]

    def forward_other():
        values["forward"] = swap(forward(1, other))

    def forward_own():
        values["base"] = forward(0, inputs)

    def finish():
        (values["layer_out"],) = run(
            lambda far: call(
                finish_kernel, "finish", [("p", values["base"]), ("v", far)], [("h", low_rows)]
            ),
            values["forward"],
        )

    def backward_end():
        (values["input_grad"],) = run(
            lambda far: call(
                input_kernel, "input",
                [
                    ("v", spots), ("p", inputs), ("v", packed), ("p", values["own"]), ("v", far),
                    ("p", values["grad_resid"]),
                ],
                [("h", full_rows)],
            ),
            values["there"],
        )

    def assemble(group, shape, along):
        near, far = groups[group].held, groups[group].coming
        count = 1 << len(MASKS[group])
        size = 2 * near.shape[0] // count
        (values[group],) = run(
            lambda far: call(
                partial(assemble_kernel, MASKS[group], along), "assemble",
                [("v", near), ("v", far)], [("r", struct(shape, F32))],
                [
                    pltpu.VMEM((count, size, near.shape[1]), F32),
                    pltpu.SemaphoreType.DMA((count,)),
                ],
            ),
            far,
        )

    def made(group):
        count = 1 << len(MASKS[group][:-1])
        size = 2 * groups[group].rows // count
        return [pltpu.VMEM((count, size, width), F32), pltpu.SemaphoreType.DMA((count,))]

    def assemble_first():
        part = groups["a"]
        (values["proj"],) = run(
            lambda far: call(
                partial(assemble_first_kernel, MASKS["a"]), "assemble_first",
                [("v", part.held), ("v", far)],
                [("r", struct((3 * wide, width), F32))], made("a"),
            ),
            part.coming,
        )

    def assemble_last():
        part = groups["b"]
        values["attention"] = run(
            lambda far: call(
                partial(assemble_last_kernel, MASKS["b"]), "assemble_last",
                [("v", part.held), ("v", far), ("v", part.extra), ("r", values["proj"])],
                [
                    ("r", struct((3 * wide, width), F32)), ("r", struct((width, wide), F32)),
                    ("v", struct((2, width), F32)), ("v", struct((hidden,), F32)),
                ]
                + [("v", struct((wide,), F32))] * 6,
                made("b"), aliases={3: 0},
            ),
            part.coming,
        )

    steps = dict(
        whole=whole, outer=outer, cw=share, back=back, first=first, sm=sums, fwd1=forward_other,
        vm=lambda: gradients("b", [], value_mix_kernel, "value_mix", "dv0", "dv1", "grad_mix"),
        qk=lambda: gradients("a", [("v", spots)], query_key_kernel, "query_key", "dq", "dk0", "dk1"),
        fwd0=forward_own, finish=finish, input=backward_end,
        asm_c=lambda: assemble("c", (hidden, wide), 0),
        asm_e=lambda: assemble("e", (wide, hidden), 1), asm_a=assemble_first,
        asm_b=assemble_last,
    )
    for name in STEPS:
        if name in steps:
            steps[name]()
        else:
            groups[name].step()
    (
        grad_proj, grad_mix_weight, grad_qv_bias, grad_expand_bias, grad_gain_one, grad_bias_one,
        grad_gain_two, grad_bias_two, grad_mix_bias, grad_contract_bias,
    ) = values["attention"]
    return (
        values["layer_out"], values["input_grad"], grad_gain_one, grad_bias_one,
        grad_proj.reshape(3, wide, width), grad_qv_bias, grad_mix_weight, grad_mix_bias,
        grad_gain_two, grad_bias_two, values["e"], grad_expand_bias, values["c"],
        grad_contract_bias,
    )


def solution(mesh):
    rows = P(("dp", "tensor"), None)
    return jax.shard_map(
        body,
        mesh=mesh,
        in_specs=(
            rows, rows, P("dp"), P("dp"), P(), P(), P(None, None, "tensor"), P(None, "tensor"),
            P("tensor", None), P(), P(), P(), P(None, "tensor"), P("tensor"), P("tensor", None),
            P(),
        ),
        out_specs=(
            rows, rows, P(), P(), P(None, None, "tensor"), P(None, "tensor"), P("tensor", None),
            P(), P(), P(), P(None, "tensor"), P("tensor"), P("tensor", None), P(),
        ),
        check_vma=False,
    )
```
